32 devices in a mesh: clip: 16 (over z, y, core), frame: 2 (over x).
Axes of the slice: x: 2, y: 2, z: 4, core: 2. Of those that a mesh axis runs over, the one named last changes fastest.
Arguments:
- frames_in: bfloat16 [16, 8, 16, 16, 1024], P('clip', 'frame'), may hold values from -6 to 6
- size_group: int32 [16], P('clip'), may hold values from 0 to 2
- modulation: float32 [16, 12, 1024], P('clip'), may hold values from -3 to 3
- w_qkv: bfloat16 [1024, 2, 3072], P('clip'), may hold values from -0.1875 to 0.1875
- w_proj: bfloat16 [1024, 2, 1024], P('clip'), may hold values from -0.75 to 0.75
- w_up: bfloat16 [1024, 2, 4096], P('clip'), may hold values from -0.1875 to 0.1875
- w_down: bfloat16 [4096, 2, 1024], P('clip'), may hold values from -0.09375 to 0.09375
- table_sp: float32 [16, 961], replicated, may hold values from -3 to 3
- table_st: float32 [16, 3375], replicated, may hold values from -3 to 3
- cotangent: bfloat16 [16, 8, 16, 16, 1024], P('clip', 'frame'), may hold values from -6 to 6
Outputs:
- mixed: bfloat16 [16, 8, 16, 16, 1024], P('clip', 'frame')
- grad_in: bfloat16 [16, 8, 16, 16, 1024], P('clip', 'frame')
- grad_modulation: float32 [16, 12, 1024], P('clip')
- grad_qkv: float32 [1024, 2, 3072], P('clip')
- grad_proj: float32 [1024, 2, 1024], P('clip')
- grad_up: float32 [1024, 2, 4096], P('clip')
- grad_down: float32 [4096, 2, 1024], P('clip')
- grad_table_sp: float32 [16, 961], replicated
- grad_table_st: float32 [16, 3375], replicated
The draws below stay inside these ranges and needn't reach their ends.
All inputs are finite; a program needn't handle non-finite values.
Results may differ from the reference program's by a relative error of at most 0.028.
Values may be sent and summed in bfloat16 or wider, within the bound.
A program may use at most 512 MiB of HBM per device.

```python
import jax
import jax.numpy as jnp
from jax import lax

D = 1024
HEADS = 16
HD = 64
FF = 4096
SWIN = 16
TWIN = 8
FRAMES = 8
FILLED = 5
HT = 16
WD = 16
CLIPS = 16
NREL_SP = 961
NREL_ST = 3375


def place_ends(values, rng, least, largest):
    extent = values.shape
    place = [jax.random.randint(jax.random.fold_in(rng, axis), (), 0, extent[axis]) for axis in range(len(extent))]
    values = values.at[tuple(place)].set(least)
    longest = extent.index(max(extent))
    place[longest] = (place[longest] + 1) % extent[longest]
    return values.at[tuple(place)].set(largest)


def block_scale(key, extent, cuts, low, high):
    def one(dim, parts):
        draws = jax.random.uniform(jax.random.fold_in(jax.random.fold_in(key, 6), dim), (parts,), jnp.float32, low / len(cuts), high / len(cuts))
        return jnp.repeat(jnp.exp(draws), extent[dim] // parts).reshape((-1,) + (1,) * (len(extent) - dim - 1))

    gain = one(*cuts[0])
    for cut in cuts[1:]:
        gain = gain * one(*cut)
    return gain


def noise(rng, shape, scale, most, pieces=(), kind=jnp.bfloat16):
    level = block_scale(rng, shape, pieces, -0.22, 0.18) if pieces else 1.0
    array = jax.random.normal(rng, shape, jnp.float32) * scale * level
    return jnp.minimum(jnp.maximum(array, -most), most).astype(kind)


def setup_inputs(seed: int = 0) -> dict:
    seeds = jax.random.split(jax.random.key(seed), 11)
    frames_in = noise(seeds[0], (CLIPS, FRAMES, HT, WD, D), 1.0, 6.0, ((0, 16), (1, 2)))
    size_group = place_ends(jax.random.randint(seeds[1], (CLIPS,), 0, 3), jax.random.fold_in(seeds[1], 1), 0, 2).astype(jnp.int32)
    modulation = noise(seeds[2], (CLIPS, 12, D), 0.6, 3.0, ((0, 16),), jnp.float32)
    w_qkv = noise(seeds[3], (D, 2, 3 * D), D ** -0.5, 0.1875, ((0, 16),))
    w_proj = noise(seeds[4], (D, 2, D), (D // 16) ** -0.5, 0.75, ((0, 16),))
    w_up = noise(seeds[5], (D, 2, FF), D ** -0.5, 0.1875, ((0, 16),))
    w_down = noise(seeds[6], (FF, 2, D), FF ** -0.5, 0.09375, ((0, 16),))
    table_sp = noise(seeds[7], (HEADS, NREL_SP), 0.5, 3.0, (), jnp.float32)
    table_st = noise(seeds[8], (HEADS, NREL_ST), 0.5, 3.0, (), jnp.float32)
    cotangent = noise(seeds[9], (CLIPS, FRAMES, HT, WD, D), 1.0, 6.0, ((0, 16), (1, 2)))
    return {"frames_in": frames_in, "size_group": size_group, "modulation": modulation, "w_qkv": w_qkv, "w_proj": w_proj, "w_up": w_up, "w_down": w_down, "table_sp": table_sp, "table_st": table_st, "cotangent": cotangent}


@jax.custom_vjp
def low(v):
    return lax.optimization_barrier(v.astype(jnp.bfloat16)).astype(jnp.float32)

@jax.custom_vjp
def low_back(v):
    return v

def low_keep(v):
    return (low(v), None)

def low_pass(kept, grad):
    return (grad,)

def back_keep(v):
    return (v, None)

def back_low(kept, grad):
    return (low(grad),)
low.defvjp(low_keep, low_pass)
low_back.defvjp(back_keep, back_low)
NEG_FILL = -1000000000.0
NORM_EPS = 1e-06

def layer_norm(values):
    centered = values - lax.optimization_barrier(jnp.mean(values, axis=-1, keepdims=True))
    spread = lax.optimization_barrier(jnp.mean(centered * centered, axis=-1, keepdims=True))
    return centered * lax.rsqrt(spread + NORM_EPS)

def project(values, weight):
    return jnp.dot(values, weight, precision=lax.Precision.HIGHEST)

def square_index(side_len):
    position = jnp.arange(side_len * side_len, dtype=jnp.int32)
    row_index = position // side_len
    column_index = position % side_len
    span_size = 2 * side_len - 1
    row_part = (row_index[:, None] - row_index[None, :] + side_len - 1) * span_size
    return row_part + column_index[:, None] - column_index[None, :] + side_len - 1

def cube_index():
    inner_index = square_index(TWIN)
    frame_ids = jnp.arange(FRAMES, dtype=jnp.int32)
    frame_offset = frame_ids[:, None] - frame_ids[None, :] + FRAMES - 1
    span_size = (2 * TWIN - 1) ** 2
    full_index = frame_offset[:, None, :, None] * span_size + inner_index[None, :, None, :]
    return full_index.reshape(FRAMES * TWIN * TWIN, FRAMES * TWIN * TWIN)

def spatial_windows(values):
    n_frames, n_rows, n_cols, n_depth = values.shape
    blocked = values.reshape(n_frames, n_rows // SWIN, SWIN, n_cols // SWIN, SWIN, n_depth)
    return blocked.transpose(0, 1, 3, 2, 4, 5).reshape(-1, SWIN * SWIN, n_depth)

def spatial_unwindow(values, full_shape):
    n_frames, n_rows, n_cols, n_depth = full_shape
    blocked = values.reshape(n_frames, n_rows // SWIN, n_cols // SWIN, SWIN, SWIN, n_depth)
    return blocked.transpose(0, 1, 3, 2, 4, 5).reshape(full_shape)

def cube_windows(values):
    n_frames, n_rows, n_cols, n_depth = values.shape
    blocked = values.reshape(n_frames, n_rows // TWIN, TWIN, n_cols // TWIN, TWIN, n_depth)
    return blocked.transpose(1, 3, 0, 2, 4, 5).reshape(-1, n_frames * TWIN * TWIN, n_depth)

def cube_unwindow(values, full_shape):
    n_frames, n_rows, n_cols, n_depth = full_shape
    blocked = values.reshape(n_rows // TWIN, n_cols // TWIN, n_frames, TWIN, TWIN, n_depth)
    return blocked.transpose(2, 0, 3, 1, 4, 5).reshape(full_shape)

def attend(query_win, key_win, value_win, bias, key_ok):
    n_win, length, width_d = query_win.shape
    query_h = query_win.reshape(n_win, length, HEADS, HD)
    key_h = key_win.reshape(n_win, key_win.shape[1], HEADS, HD)
    value_h = value_win.reshape(n_win, value_win.shape[1], HEADS, HD)
    scores = jnp.einsum('nqhd,nkhd->nhqk', query_h, key_h, precision=lax.Precision.HIGHEST) * HD ** (-0.5) + bias[None]
    scores = low_back(scores)
    scores = jnp.where(key_ok[:, None, None, :], scores, NEG_FILL)
    row_top = lax.optimization_barrier(jnp.max(scores, axis=-1, keepdims=True))
    expo_values = jnp.exp(scores - row_top)
    soft_probs = expo_values / lax.optimization_barrier(jnp.sum(expo_values, axis=-1, keepdims=True))
    probs = low(soft_probs)
    mixed_h = jnp.einsum('nhqk,nkhd->nqhd', probs, value_h, precision=lax.Precision.HIGHEST)
    return low_back(low(mixed_h.reshape(n_win, length, width_d)))

def block(stream, mod_rows, qkv_w, proj_w, up_w, down_w, bias, key_ok, to_windows, from_windows):
    width_d = stream.shape[-1]
    normed_a = low(layer_norm(stream) * (1.0 + mod_rows[1]) + mod_rows[0])
    qkv_values = low_back(low(project(normed_a, qkv_w)))
    query_win = to_windows(qkv_values[..., :width_d])
    key_win = to_windows(qkv_values[..., width_d:2 * width_d])
    value_win = to_windows(qkv_values[..., 2 * width_d:])
    att_win = attend(query_win, key_win, value_win, bias, key_ok)
    att_out = from_windows(att_win, stream.shape)
    proj_out = low_back(project(att_out, proj_w))
    mid_stream = stream + mod_rows[2] * proj_out
    normed_m = low(layer_norm(mid_stream) * (1.0 + mod_rows[4]) + mod_rows[3])
    up_value = low_back(project(normed_m, up_w))
    active = low(jax.nn.gelu(up_value, approximate=True))
    down_out = low_back(project(active, down_w))
    return mid_stream + mod_rows[5] * down_out

def reference(frames_in, size_group, modulation, w_qkv, w_proj, w_up, w_down, table_sp, table_st, cotangent):
    index_sp = square_index(SWIN)
    index_st = cube_index()
    weights = (w_qkv.astype(jnp.float32), w_proj.astype(jnp.float32), w_up.astype(jnp.float32), w_down.astype(jnp.float32))
    column_ids = jnp.arange(WD, dtype=jnp.int32)
    frame_ids = jnp.arange(FRAMES, dtype=jnp.int32)

    def per_clip(totals, clip_items):
        clip_in, group_id, mod_rows, clip_cot = clip_items
        column_limit = WD - 3 * (2 - group_id)
        wide_ok = jnp.broadcast_to((column_ids < column_limit)[None, None, :], (FRAMES, HT, WD))
        frame_ok = wide_ok & (frame_ids < FILLED)[:, None, None]
        valid_sp = spatial_windows(wide_ok[..., None])[..., 0]
        valid_st = cube_windows(frame_ok[..., None])[..., 0]

        def forward(stream, rows, qkv_all, proj_all, up_all, down_all, tab_sp, tab_st):
            bias_sp = tab_sp[:, index_sp]
            bias_st = tab_st[:, index_st]
            stream = block(stream, rows[0:6], qkv_all[:, 0], proj_all[:, 0], up_all[:, 0], down_all[:, 0], bias_sp, valid_sp, spatial_windows, spatial_unwindow)
            return block(stream, rows[6:12], qkv_all[:, 1], proj_all[:, 1], up_all[:, 1], down_all[:, 1], bias_st, valid_st, cube_windows, cube_unwindow)
        result, pullback = jax.vjp(forward, clip_in.astype(jnp.float32), mod_rows, weights[0], weights[1], weights[2], weights[3], table_sp, table_st)
        grad_list = pullback(clip_cot.astype(jnp.float32))
        totals = tuple((old_sum + new_term for old_sum, new_term in zip(totals, grad_list[2:])))
        return (totals, (result.astype(jnp.bfloat16), grad_list[0].astype(jnp.bfloat16), grad_list[1]))
    start_sums = (jnp.zeros(w_qkv.shape, jnp.float32), jnp.zeros(w_proj.shape, jnp.float32), jnp.zeros(w_up.shape, jnp.float32), jnp.zeros(w_down.shape, jnp.float32), jnp.zeros(table_sp.shape, jnp.float32), jnp.zeros(table_st.shape, jnp.float32))
    totals, per_out = lax.scan(per_clip, start_sums, (frames_in, size_group, modulation, cotangent))
    return (per_out[0], per_out[1], per_out[2], totals[0], totals[1], totals[2], totals[3], totals[4], totals[5])
```

```python
import functools

import jax
import jax.numpy as jnp
from jax import lax
from jax.experimental import pallas as pl
from jax.experimental.pallas import tpu as pltpu
from jax.sharding import PartitionSpec as P

SWIN = 16
TWIN = 8
FRAMES = 8
FILLED = 5
KEYF = 6
NEG_FILL = -1000000000.0
NORM_EPS = 1e-06
F32 = jnp.float32
BF16 = jnp.bfloat16
NT = (((1,), (1,)), ((), ()))
TN = (((0,), (0,)), ((), ()))


def dot_nn(a, b):
    return jnp.dot(a, b, preferred_element_type=F32)


def dot_nt(a, b):
    return lax.dot_general(a, b, NT, preferred_element_type=F32)


def dot_tn(a, b):
    return lax.dot_general(a, b, TN, preferred_element_type=F32)


def norm_stats(values):
    mean = jnp.mean(values, axis=-1, keepdims=True)
    centered = values - mean
    spread = jnp.mean(centered * centered, axis=-1, keepdims=True)
    inv = lax.rsqrt(spread + NORM_EPS)
    return centered * inv, inv


def pick_sp():
    span = 2 * SWIN - 1
    shape = (8 * span, SWIN, 128)
    source = lax.broadcasted_iota(jnp.int32, shape, 0)
    ci = lax.broadcasted_iota(jnp.int32, shape, 1)
    lane = lax.broadcasted_iota(jnp.int32, shape, 2)
    hit = (source // span == 7 - lane // SWIN) & (source % span == SWIN - 1 + ci - lane % SWIN)
    return hit.astype(F32).reshape(8 * span, SWIN * 128)


def pick_st():
    span = 2 * TWIN - 1
    shape = (span * span, TWIN, 128)
    source = lax.broadcasted_iota(jnp.int32, shape, 0)
    ci = lax.broadcasted_iota(jnp.int32, shape, 1)
    lane = lax.broadcasted_iota(jnp.int32, shape, 2)
    row = span - 1 - lane // TWIN
    hit = (source // span == row) & (source % span == TWIN - 1 + ci - lane % TWIN)
    return hit.astype(F32).reshape(span * span, TWIN * 128)


def spread_sp(table):
    n_heads = table.shape[0]
    span = 2 * SWIN - 1
    padded = jnp.pad(table, ((0, 0), (span, 0))).reshape(n_heads * 4, 8 * span)
    out = jnp.dot(padded, pick_sp(), precision=lax.Precision.HIGHEST)
    return out.reshape(n_heads, 4, SWIN, 128)


def spread_st(table):
    n_heads = table.shape[0]
    span = 2 * TWIN - 1
    fspan = 2 * FRAMES - 1
    flat = table.reshape(n_heads * fspan, span * span)
    out = jnp.dot(flat, pick_st(), precision=lax.Precision.HIGHEST)
    return out.reshape(n_heads, fspan, TWIN, 128)


def gather_sp(spread):
    n_heads = spread.shape[0]
    span = 2 * SWIN - 1
    flat = spread.reshape(n_heads * 4, SWIN * 128)
    out = lax.dot_general(flat, pick_sp(), NT, precision=lax.Precision.HIGHEST)
    return out.reshape(n_heads, 32 * span)[:, span:]


def gather_st(spread):
    n_heads = spread.shape[0]
    span = 2 * TWIN - 1
    fspan = 2 * FRAMES - 1
    flat = spread.reshape(n_heads * fspan, TWIN * 128)
    out = lax.dot_general(flat, pick_st(), NT, precision=lax.Precision.HIGHEST)
    return out.reshape(n_heads, fspan * span * span)


def fill_bias_sp(spread_ref, hh, bias_ref):
    spread = jnp.concatenate([spread_ref[hh, g] for g in (3, 2, 1, 0)], axis=1)
    width = spread.shape[1]
    win = SWIN * SWIN
    for ri in range(SWIN):
        shift = (width - (SWIN - 1 - ri) * SWIN) % width
        rolled = pltpu.roll(spread, shift, 1) if shift else spread
        bias_ref[ri * SWIN : (ri + 1) * SWIN, :] = rolled[:, :win]


def fold_bias_sp(grad_ref, out_ref, hh):
    win = SWIN * SWIN
    width = 2 * win
    total = None
    for ri in range(SWIN):
        rows = grad_ref[ri * SWIN : (ri + 1) * SWIN, :]
        rows = jnp.concatenate([rows, jnp.zeros((SWIN, width - win), F32)], axis=1)
        shift = (SWIN - 1 - ri) * SWIN
        rows = pltpu.roll(rows, shift, 1) if shift else rows
        total = rows if total is None else total + rows
    for g in range(4):
        out_ref[hh, g] = total[:, (3 - g) * 128 : (4 - g) * 128]


def fill_bias_st(spread_ref, hh, bias_ref):
    lanes = lax.broadcasted_iota(jnp.int32, (TWIN, 128), 1)
    half = TWIN * TWIN
    n_pairs = KEYF // 2
    for ri in range(TWIN):
        shift = (128 - (TWIN - 1 - ri) * TWIN) % 128
        cache = {}

        def low_of(f):
            if f not in cache:
                rows = spread_ref[hh, 2 * FRAMES - 2 - f]
                cache[f] = pltpu.roll(rows, shift, 1) if shift else rows
            return cache[f]

        pairs = {}
        for fi in range(FRAMES):
            for pair in range(n_pairs):
                f = FRAMES - 1 - fi + 2 * pair
                if f not in pairs:
                    pairs[f] = jnp.where(
                        lanes < half, low_of(f), pltpu.roll(low_of(f + 1), half, 1)
                    )
                row = fi * half + ri * TWIN
                bias_ref[row : row + TWIN, pair * 128 : (pair + 1) * 128] = pairs[f]


def fold_bias_st(grad_ref, out_ref, hh):
    lanes = lax.broadcasted_iota(jnp.int32, (TWIN, 128), 1)
    half = TWIN * TWIN
    n_pairs = KEYF // 2
    fspan = 2 * FRAMES - 1
    totals = [None] * fspan
    for ri in range(TWIN):
        sums = {}
        for fi in range(FRAMES):
            for pair in range(n_pairs):
                f = FRAMES - 1 - fi + 2 * pair
                row = fi * half + ri * TWIN
                part = grad_ref[row : row + TWIN, pair * 128 : (pair + 1) * 128]
                sums[f] = part if f not in sums else sums[f] + part
        for f in range(fspan):
            piece = None
            if f in sums:
                piece = jnp.where(lanes < half, sums[f], 0.0)
            if f - 1 in sums:
                upper = pltpu.roll(jnp.where(lanes >= half, sums[f - 1], 0.0), half, 1)
                piece = upper if piece is None else piece + upper
            if piece is None:
                continue
            shift = (TWIN - 1 - ri) * TWIN
            piece = pltpu.roll(piece, shift, 1) if shift else piece
            totals[f] = piece if totals[f] is None else totals[f] + piece
    for f in range(fspan):
        out_ref[hh, 2 * FRAMES - 2 - f] = jnp.zeros((TWIN, 128), F32) if totals[f] is None else totals[f]


def lane_mask(rows, hh):
    lanes = lax.broadcasted_iota(jnp.int32, (rows, 128), 1)
    return (lanes < 64) if hh == 0 else (lanes >= 64)


def attend_forward(spatial, n_win, n_query, n_key, chunk, q_ref, k_ref, v_ref, m_ref, ok_ref, att_ref, p_ref, bias_ref):
    for hh in range(2):
        if spatial:
            fill_bias_sp(m_ref, hh, bias_ref.at[hh])
        else:
            fill_bias_st(m_ref, hh, bias_ref.at[hh])
    own = lane_mask(chunk, 0)
    for n in range(n_win):
        key = k_ref[n * n_query : n * n_query + n_key, :]
        val = v_ref[n * n_query : n * n_query + n_key, :]
        ok = ok_ref[n] > 0.0
        for c in range(n_query // chunk):
            rows = slice(n * n_query + c * chunk, n * n_query + (c + 1) * chunk)
            query = q_ref[rows, :]
            query = query * jnp.asarray(0.125, BF16)
            outs = []
            for hh in range(2):
                mine = own if hh == 0 else jnp.logical_not(own)
                picked = jnp.where(mine, query, jnp.zeros_like(query))
                scores = dot_nt(picked, key) + bias_ref[hh, c * chunk : (c + 1) * chunk, :]
                scores = jnp.where(ok, scores, NEG_FILL)
                top = jnp.max(scores, axis=-1, keepdims=True)
                expo = jnp.exp(scores - top)
                probs = (expo * (1.0 / jnp.sum(expo, axis=-1, keepdims=True))).astype(BF16)
                p_ref[hh, n, c * chunk : (c + 1) * chunk, :] = probs
                outs.append(dot_nn(probs, val))
            att_ref[rows, :] = jnp.where(own, outs[0], outs[1]).astype(BF16)


def attend_backward(
    spatial, n_win, n_query, n_key, chunk, head, q_ref, k_ref, v_ref, do_ref, p_ref, g_ref, dm_ref, db_ref
):
    width = g_ref.shape[1] // 3
    own = lane_mask(chunk, 0)
    own_k = lane_mask(n_key, 0)

    def store(rows, which, values):
        g_ref[rows, pl.ds(pl.multiple_of(which * width + head * 128, 128), 128)] = values

    db_ref[...] = jnp.zeros_like(db_ref)
    for n in range(n_win):
        keys = slice(n * n_query, n * n_query + n_key)
        key = k_ref[keys, :]
        val = v_ref[keys, :]
        gk = [None, None]
        gv = [None, None]
        for c in range(n_query // chunk):
            rows = slice(n * n_query + c * chunk, n * n_query + (c + 1) * chunk)
            part = slice(c * chunk, (c + 1) * chunk)
            query = q_ref[rows, :]
            gout = do_ref[rows, :]
            gq = []
            for hh in range(2):
                mine = own if hh == 0 else jnp.logical_not(own)
                probs = p_ref[hh, n, part, :]
                gsel = jnp.where(mine, gout, jnp.zeros_like(gout))
                dprob = dot_nt(gsel, val)
                soft = probs.astype(F32)
                delta = jnp.sum(soft * dprob, axis=-1, keepdims=True)
                dscore = (soft * (dprob - delta)).astype(BF16)
                db_ref[hh, part, :] += dscore.astype(F32)
                gq.append(dot_nn(dscore, key))
                dk = dot_tn(dscore, query)
                dv = dot_tn(probs, gout)
                gk[hh] = dk if gk[hh] is None else gk[hh] + dk
                gv[hh] = dv if gv[hh] is None else gv[hh] + dv
            store(rows, 0, (jnp.where(own, gq[0], gq[1]) * 0.125).astype(BF16))
        store(keys, 1, (jnp.where(own_k, gk[0], gk[1]) * 0.125).astype(BF16))
        store(keys, 2, jnp.where(own_k, gv[0], gv[1]).astype(BF16))
        if n_key < n_query:
            rest = slice(n * n_query + n_key, (n + 1) * n_query)
            empty = jnp.zeros((n_query - n_key, 128), BF16)
            store(rest, 1, empty)
            store(rest, 2, empty)
    for hh in range(2):
        if spatial:
            fold_bias_sp(db_ref.at[hh], dm_ref, hh)
        else:
            fold_bias_st(db_ref.at[hh], dm_ref, hh)


def attention_shapes(spatial, tokens):
    n_query = SWIN * SWIN if spatial else FRAMES * TWIN * TWIN
    n_key = n_query if spatial else KEYF * TWIN * TWIN
    return tokens // n_query, n_query, n_key, 256


def attention_forward(spatial, qkv, spread, key_ok):
    tokens, width3 = qkv.shape
    width = width3 // 3
    pairs = width // 128
    n_win, n_query, n_key, chunk = attention_shapes(spatial, tokens)
    n_heads = 2 * pairs
    tail = spread.shape[1:]
    zeros = (0,) * len(tail)
    return pl.pallas_call(
        functools.partial(attend_forward, spatial, n_win, n_query, n_key, chunk),
        grid=(pairs,),
        in_specs=[
            pl.BlockSpec((tokens, 128), lambda i: (0, i)),
            pl.BlockSpec((tokens, 128), lambda i: (0, pairs + i)),
            pl.BlockSpec((tokens, 128), lambda i: (0, 2 * pairs + i)),
            pl.BlockSpec((2,) + tail, lambda i: (i,) + zeros),
            pl.BlockSpec((n_win, 1, n_key), lambda i: (0, 0, 0)),
        ],
        out_specs=[
            pl.BlockSpec((tokens, 128), lambda i: (0, i)),
            pl.BlockSpec((2, n_win, n_query, n_key), lambda i: (i, 0, 0, 0)),
        ],
        out_shape=[
            jax.ShapeDtypeStruct((tokens, width), BF16),
            jax.ShapeDtypeStruct((n_heads, n_win, n_query, n_key), BF16),
        ],
        scratch_shapes=[pltpu.VMEM((2, n_query, n_key), F32)],
        compiler_params=pltpu.CompilerParams(vmem_limit_bytes=48 * 1024 * 1024),
        name="attend_forward",
    )(qkv, qkv, qkv, spread, key_ok)


ROWS = 64
COLS = 1024
MESH = pl.DeviceIdType.MESH


def place(n_clip):
    clip = lax.axis_index("clip")
    x = lax.axis_index("frame")
    z = clip // 4
    y = lax.rem(clip // 2, 2)
    c = lax.rem(clip, 2)
    return clip, z, y, c, x


def remote(src, dst, send, recv, clip, frame):
    return pltpu.make_async_remote_copy(
        src_ref=src,
        dst_ref=dst,
        send_sem=send,
        recv_sem=recv,
        device_id={"clip": clip, "frame": frame},
        device_id_type=MESH,
    )


def greet(targets):
    barrier = pltpu.get_barrier_semaphore()
    count = 0
    for clip, frame, valid in targets:
        if valid is None:
            pl.semaphore_signal(barrier, inc=1, device_id={"clip": clip, "frame": frame}, device_id_type=MESH)
            count = count + 1
        else:
            @pl.when(valid)
            def _():
                pl.semaphore_signal(barrier, inc=1, device_id={"clip": clip, "frame": frame}, device_id_type=MESH)
            count = count + valid.astype(jnp.int32)
    pl.semaphore_wait(barrier, count)


GATHER_HI = 640


def gather_tick(t, n, nz, where, shard, full, local, up_s, up_r, dn_s, dn_r, y_s, y_r, x_s, x_r, c_s, c_r):
    clip, z, y, c, x = where
    hi = GATHER_HI
    lo = COLS - hi
    fetch = pl.ds(pl.multiple_of(x * lo, 128), hi)
    give = pl.ds(pl.multiple_of(x * hi, 128), lo)
    last = nz - 1

    def own(i):
        return pltpu.make_async_copy(
            shard.at[i, :, fetch], full.at[i, z, y, c, :, fetch], local.at[i]
        )

    def up(i, s, origin):
        src = shard.at[i, :, fetch] if s == 0 else full.at[i, origin, y, c, :, fetch]
        return remote(src, full.at[i, origin, y, c, :, fetch], up_s.at[s, i], up_r.at[s, i], clip + 4, x)

    def down(i, s, origin):
        src = shard.at[i, :, fetch] if s == 0 else full.at[i, origin, y, c, :, fetch]
        return remote(src, full.at[i, origin, y, c, :, fetch], dn_s.at[s, i], dn_r.at[s, i], clip - 4, x)

    def over_y(i):
        src = full.at[i, :, y, c, :, fetch]
        return remote(src, src, y_s.at[i], y_r.at[i], clip + 2 - 4 * y, x)

    def over_x(i):
        src = full.at[i, :, :, c, :, give]
        return remote(src, src, x_s.at[i], x_r.at[i], clip, 1 - x)

    def over_c(i):
        src = full.at[i, :, :, c]
        return remote(src, src, c_s.at[i], c_r.at[i], clip + 1 - 2 * c, x)

    def when_item(i):
        return jnp.logical_and(i >= 0, i < n)

    def z_wait(i, s):
        @pl.when(z - 1 - s >= 0)
        def _():
            up(i, s, z - 1 - s).wait_recv()

        @pl.when(z + 1 + s <= last)
        def _():
            down(i, s, z + 1 + s).wait_recv()

    def z_start(i, s):
        @pl.when(jnp.logical_and(z < last, z - s >= 0))
        def _():
            up(i, s, z - s).start()

        @pl.when(jnp.logical_and(z > 0, z + s <= last))
        def _():
            down(i, s, z + s).start()

    def z_sent(i, s):
        @pl.when(jnp.logical_and(z < last, z - s >= 0))
        def _():
            up(i, s, z - s).wait_send()

        @pl.when(jnp.logical_and(z > 0, z + s <= last))
        def _():
            down(i, s, z + s).wait_send()

    steps = nz - 1
    i = t

    @pl.when(when_item(i))
    def _():
        own(i).start()
        z_start(i, 0)

    for s in range(1, steps):
        i = t - s

        @pl.when(when_item(i))
        def _(i=i, s=s):
            z_wait(i, s - 1)
            z_start(i, s)

    i_y = t - steps

    @pl.when(when_item(i_y))
    def _():
        z_wait(i_y, steps - 1)
        own(i_y).wait()
        over_y(i_y).start()

    i_x = t - steps - 1

    @pl.when(when_item(i_x))
    def _():
        over_y(i_x).wait_recv()
        over_x(i_x).start()

    i_c = t - steps - 2

    @pl.when(when_item(i_c))
    def _():
        over_x(i_c).wait_recv()
        over_c(i_c).start()

    i_d = t - steps - 3

    @pl.when(when_item(i_d))
    def _():
        over_c(i_d).wait_recv()
        for s in range(steps):
            z_sent(i_d, s)
        over_y(i_d).wait_send()
        over_x(i_d).wait_send()
        over_c(i_d).wait_send()


def gather_kernel(n, nz, shard, full, *sems):
    where = place(4 * nz)
    clip, z, y, c, x = where
    greet([
        (clip + 4, x, z < nz - 1),
        (clip - 4, x, z > 0),
        (clip + 2 - 4 * y, x, None),
        (clip, 1 - x, None),
        (clip + 1 - 2 * c, x, None),
    ])

    def step(t, carry):
        gather_tick(t, n, nz, where, shard, full, *sems)
        return carry

    lax.fori_loop(0, n + nz + 2, step, 0)


def gather_sems(n, nz):
    dma = pltpu.SemaphoreType.DMA
    z = dma((nz - 1, n))
    one = dma((n,))
    return [one, z, z, z, z, one, one, one, one, one, one]


def gather_all(shard, nz, cid):
    n = shard.shape[0]
    return pl.pallas_call(
        functools.partial(gather_kernel, n, nz),
        out_shape=jax.ShapeDtypeStruct((n, nz, 2, 2, ROWS, COLS), BF16),
        in_specs=[pl.BlockSpec(memory_space=pl.ANY)],
        out_specs=pl.BlockSpec(memory_space=pl.ANY),
        scratch_shapes=gather_sems(n, nz),
        compiler_params=pltpu.CompilerParams(collective_id=cid, has_side_effects=True),
        name="gather_all",
    )(shard)


NBUF = 3
REDUCE_TAIL = 7
NACC = 4


def reduce_tick(t, n, nz, where, sources, out, acc, cbuf, ya, xa, yb, xb, tb, zb, sb, fb, ob,
                loc, c_s, c_r, ya_s, ya_r, xa_s, xa_r, yb_s, yb_r, xb_s, xb_r, z_s, z_r, f_s, f_r, o_s,
                cred_c, cred_y, cred_x, cred_z, cred_f):
    clip, z, y, c, x = where
    half = COLS // 2
    quarter = COLS // 4
    peer_c = clip + 1 - 2 * c
    peer_y = clip + 2 - 4 * y

    def lanes(base, which):
        return pl.ds(pl.multiple_of(base + which * quarter, 128), quarter)

    mine1, their1 = lanes(0, x), lanes(0, 1 - x)
    mine2, their2 = lanes(half, x), lanes(half, 1 - x)

    def slot(i):
        return lax.rem(i, NBUF)

    def aslot(i):
        return lax.rem(i, NACC)

    def load(i, source, first):
        return pltpu.make_async_copy(source.at[i - first, :, :, c], acc.at[aslot(i)], loc.at[slot(i)])

    def over_c(i, source, first):
        src = source.at[i - first, :, :, 1 - c]
        return remote(src, cbuf.at[slot(i)], c_s.at[slot(i)], c_r.at[slot(i)], peer_c, x)

    def over_ya(i):
        return remote(acc.at[aslot(i), :, 1 - y, :, pl.ds(0, half)], ya.at[slot(i)], ya_s.at[slot(i)], ya_r.at[slot(i)], peer_y, x)

    def over_xa(i):
        return remote(acc.at[aslot(i), :, :, :, their2], xa.at[slot(i)], xa_s.at[slot(i)], xa_r.at[slot(i)], clip, 1 - x)

    def over_xb(i):
        return remote(acc.at[aslot(i), :, y, :, their1], xb.at[slot(i)], xb_s.at[slot(i)], xb_r.at[slot(i)], clip, 1 - x)

    def over_yb(i):
        return remote(acc.at[aslot(i), :, 1 - y, :, mine2], yb.at[slot(i)], yb_s.at[slot(i)], yb_r.at[slot(i)], peer_y, x)

    def over_z(i, k):
        to = lax.rem(z + k, nz)
        return remote(tb.at[slot(i), to], zb.at[slot(i), k - 1], z_s.at[slot(i), k - 1], z_r.at[slot(i), k - 1],
                      clip + 4 * (to - z), x)

    def over_f(i):
        return remote(sb.at[slot(i)], fb.at[slot(i)], f_s.at[slot(i)], f_r.at[slot(i)], clip, 1 - x)

    def write(i):
        return pltpu.make_async_copy(ob.at[slot(i)], out.at[i], o_s.at[slot(i)])

    def credit(sem, who, frame, i):
        @pl.when(i + NBUF < n)
        def _():
            pl.semaphore_signal(sem, inc=1, device_id={"clip": who, "frame": frame}, device_id_type=MESH)

    def need(sem, i):
        @pl.when(i >= NBUF)
        def _():
            pl.semaphore_wait(sem, 1)

    def item(i):
        return jnp.logical_and(i >= 0, i < n)

    i = t - 6

    @pl.when(item(i))
    def _(i=i):
        write(i).wait()

    i = t

    @pl.when(item(i))
    def _(i=i):
        need(cred_c, i)
        first = 0
        for source, skip, count in sources:

            @pl.when(jnp.logical_and(i >= first, i < first + count))
            def _(source=source, offset=first - skip):
                over_c(i, source, offset).start()
                load(i, source, offset).start()

            first += count

    i = t - 1

    @pl.when(item(i))
    def _(i=i):
        over_c(i, sources[0][0], i).wait()
        load(i, sources[0][0], i).wait()
        a, b = aslot(i), slot(i)

        def body(k, carry):
            acc[a, k] = acc[a, k] + cbuf[b, k]
            return carry

        lax.fori_loop(0, nz, body, 0)
        credit(cred_c, peer_c, x, i)
        need(cred_y, i)
        need(cred_x, i)
        over_ya(i).start()
        over_xa(i).start()

    i = t - 2

    @pl.when(item(i))
    def _(i=i):
        over_ya(i).wait()
        over_xa(i).wait()
        a, b = aslot(i), slot(i)

        def body(k, carry):
            acc[a, k, y, :, pl.ds(0, half)] = acc[a, k, y, :, pl.ds(0, half)] + ya[b, k]
            acc[a, k, :, :, mine2] = acc[a, k, :, :, mine2] + xa[b, k]
            return carry

        lax.fori_loop(0, nz, body, 0)
        over_xb(i).start()
        over_yb(i).start()

    i = t - 3

    @pl.when(item(i))
    def _(i=i):
        over_xb(i).wait()
        over_yb(i).wait()
        a, b = aslot(i), slot(i)

        def body(k, carry):
            tb[b, k, :, pl.ds(0, quarter)] = acc[a, k, y, :, mine1] + xb[b, k]
            tb[b, k, :, pl.ds(quarter, quarter)] = acc[a, k, y, :, mine2] + yb[b, k]
            return carry

        lax.fori_loop(0, nz, body, 0)
        credit(cred_y, peer_y, x, i)
        credit(cred_x, clip, 1 - x, i)
        for k in range(1, nz):
            need(cred_z.at[k - 1], i)
            over_z(i, k).start()

    i = t - 4

    @pl.when(item(i))
    def _(i=i):
        for k in range(1, nz):
            over_z(i, k).wait()
        b = slot(i)
        total = tb[b, z].astype(F32)
        for k in range(1, nz):
            total = total + zb[b, k - 1].astype(F32)
        sb[b] = total.astype(BF16)
        for k in range(1, nz):
            sender = lax.rem(z + nz - k, nz)
            credit(cred_z.at[k - 1], clip + 4 * (sender - z), x, i)
        need(cred_f, i)
        over_f(i).start()

    i = t - 5

    @pl.when(item(i))
    def _(i=i):
        over_f(i).wait()
        b = slot(i)
        ob[b, :, mine1] = sb[b, :, pl.ds(0, quarter)].astype(F32)
        ob[b, :, mine2] = sb[b, :, pl.ds(quarter, quarter)].astype(F32)
        ob[b, :, their1] = fb[b, :, pl.ds(0, quarter)].astype(F32)
        ob[b, :, their2] = fb[b, :, pl.ds(quarter, quarter)].astype(F32)
        credit(cred_f, clip, 1 - x, i)
        write(i).start()


def greet_reduce(nz, where):
    clip, z, y, c, x = where
    others = [(clip + 4 * (lax.rem(z + k, nz) - z), x, None) for k in range(1, nz)]
    greet(others + [
        (clip + 2 - 4 * y, x, None),
        (clip, 1 - x, None),
        (clip + 1 - 2 * c, x, None),
    ])


def reduce_kernel(picks, nz, *refs):
    n_in = len(picks)
    sources = [(ref, skip, count) for ref, (skip, count) in zip(refs[:n_in], picks)]
    out, rest = refs[n_in], refs[n_in + 1 :]
    n = sum(count for _, count in picks)
    where = place(4 * nz)
    greet_reduce(nz, where)

    def step(t, carry):
        reduce_tick(t, n, nz, where, sources, out, *rest)
        return carry

    lax.fori_loop(0, n + REDUCE_TAIL, step, 0)


def reduce_scratch(nz):
    half, quarter = COLS // 2, COLS // 4
    dma = pltpu.SemaphoreType.DMA
    one = dma((NBUF,))
    regular = pltpu.SemaphoreType.REGULAR
    return [
        pltpu.VMEM((NACC, nz, 2, ROWS, COLS), BF16),
        pltpu.VMEM((NBUF, nz, 2, ROWS, COLS), BF16),
        pltpu.VMEM((NBUF, nz, ROWS, half), BF16),
        pltpu.VMEM((NBUF, nz, 2, ROWS, quarter), BF16),
        pltpu.VMEM((NBUF, nz, ROWS, quarter), BF16),
        pltpu.VMEM((NBUF, nz, ROWS, quarter), BF16),
        pltpu.VMEM((NBUF, nz, ROWS, half), BF16),
        pltpu.VMEM((NBUF, nz - 1, ROWS, half), BF16),
        pltpu.VMEM((NBUF, ROWS, half), BF16),
        pltpu.VMEM((NBUF, ROWS, half), BF16),
        pltpu.VMEM((NBUF, ROWS, COLS), F32),
        one, one, one, one, one, one, one, one, one, one, one,
        dma((NBUF, nz - 1)), dma((NBUF, nz - 1)),
        one, one, one,
        regular, regular, regular, pltpu.SemaphoreType.REGULAR((nz - 1,)), regular,
    ]


def reduce_all(grads, picks, nz, cid):
    n = sum(count for _, count in picks)
    return pl.pallas_call(
        functools.partial(reduce_kernel, picks, nz),
        out_shape=jax.ShapeDtypeStruct((n, ROWS, COLS), F32),
        in_specs=[pl.BlockSpec(memory_space=pl.ANY)] * len(grads),
        out_specs=pl.BlockSpec(memory_space=pl.ANY),
        scratch_shapes=reduce_scratch(nz),
        compiler_params=pltpu.CompilerParams(
            collective_id=cid, has_side_effects=True, vmem_limit_bytes=48 * 1024 * 1024
        ),
        name="reduce_all",
    )(*grads)


CHUNK = 512
STEP_ROWS = 128
MIB = 1024 * 1024
GELU_C = 0.7978845608028654
GELU_A = 0.044715


def fixed(shape, **kw):
    zeros = (0,) * len(shape)
    return pl.BlockSpec(shape, lambda i: zeros, pipeline_mode=pl.Buffered(1), **kw)


def over_rows(tokens, body):
    def step(k, carry):
        body(pl.ds(pl.multiple_of(k * STEP_ROWS, STEP_ROWS), STEP_ROWS))
        return carry

    lax.fori_loop(0, tokens // STEP_ROWS, step, 0)


def qkv_body(s_ref, m_ref, w_ref, na_ref, q_ref):
    @pl.when(pl.program_id(0) == 0)
    def _():
        def rows_of(rows):
            normed, _ = norm_stats(s_ref[rows, :])
            na_ref[rows, :] = (normed * (1.0 + m_ref[1:2, :]) + m_ref[0:1, :]).astype(BF16)

        over_rows(s_ref.shape[0], rows_of)

    q_ref[...] = dot_nn(na_ref[...], w_ref[0]).astype(BF16)


def qkv_forward(stream, mods, weights, base):
    tokens, width = stream.shape
    per = width // CHUNK
    return pl.pallas_call(
        qkv_body,
        grid=(3 * per,),
        in_specs=[
            fixed((tokens, width)),
            fixed(mods.shape),
            pl.BlockSpec((1, width, CHUNK), lambda i: (base + i // per, 0, i % per)),
        ],
        out_specs=[fixed((tokens, width)), pl.BlockSpec((tokens, CHUNK), lambda i: (0, i))],
        out_shape=[
            jax.ShapeDtypeStruct((tokens, width), BF16),
            jax.ShapeDtypeStruct((tokens, 3 * width), BF16),
        ],
        compiler_params=pltpu.CompilerParams(vmem_limit_bytes=48 * MIB),
        name="qkv_forward",
    )(stream, mods, weights)


def proj_body(att_ref, s_ref, m_ref, w_ref, proj_ref, mid_ref, nm_ref):
    proj = dot_nn(att_ref[...], w_ref[0])
    proj_ref[...] = proj.astype(BF16)
    mid = s_ref[...] + m_ref[2:3, :] * proj
    mid_ref[...] = mid
    normed, _ = norm_stats(mid)
    nm_ref[...] = (normed * (1.0 + m_ref[4:5, :]) + m_ref[3:4, :]).astype(BF16)


def proj_forward(att, stream, mods, weights, base):
    tokens, width = stream.shape
    rows = 256
    row = pl.BlockSpec((rows, width), lambda i: (i, 0))
    return pl.pallas_call(
        proj_body,
        grid=(tokens // rows,),
        in_specs=[row, row, fixed(mods.shape), pl.BlockSpec((1, width, width), lambda i: (base + 3, 0, 0))],
        out_specs=[row, row, row],
        out_shape=[
            jax.ShapeDtypeStruct((tokens, width), BF16),
            jax.ShapeDtypeStruct((tokens, width), F32),
            jax.ShapeDtypeStruct((tokens, width), BF16),
        ],
        compiler_params=pltpu.CompilerParams(vmem_limit_bytes=48 * MIB),
        name="proj_forward",
    )(att, stream, mods, weights)


def down_rows(w_ref):
    return jnp.concatenate(
        [w_ref[sub, c * 64 : (c + 1) * 64, :] for c in range(2) for sub in range(4)], axis=0
    )


def mlp_forward_body(n_steps, nm_ref, mid_ref, m_ref, up_ref, dn_ref, act_ref, dact_ref, down_ref, res_ref, acc_ref):
    step = pl.program_id(0)
    tokens = nm_ref.shape[0]
    w_down = down_rows(dn_ref)
    rows_each = 256

    def part(k, carry):
        rows = pl.ds(pl.multiple_of(k * rows_each, rows_each), rows_each)
        up = dot_nn(nm_ref[rows, :], up_ref[0])
        square = up * up
        tanh = jnp.tanh(GELU_C * up * (1.0 + GELU_A * square))
        half = 0.5 * (1.0 + tanh)
        act = (up * half).astype(BF16)
        slope = GELU_C * (1.0 + 3.0 * GELU_A * square)
        act_ref[rows, :] = act
        dact_ref[rows, :] = (half + 0.5 * up * (1.0 - tanh * tanh) * slope).astype(BF16)
        down = dot_nn(act, w_down)

        @pl.when(step == 0)
        def _():
            acc_ref[rows, :] = down

        @pl.when(step > 0)
        def _():
            acc_ref[rows, :] += down

        return carry

    lax.fori_loop(0, tokens // rows_each, part, 0)

    @pl.when(step == n_steps - 1)
    def _():
        def rows_of(rows):
            down = acc_ref[rows, :]
            down_ref[rows, :] = down.astype(BF16)
            res_ref[rows, :] = (mid_ref[rows, :] + m_ref[5:6, :] * down).astype(res_ref.dtype)

        over_rows(tokens, rows_of)


def mlp_forward(normed_m, mid, mods, weights, base, result_type):
    tokens, width = mid.shape
    n_steps = 4 * width // CHUNK
    per = width // CHUNK
    hidden = 4 * width
    return pl.pallas_call(
        functools.partial(mlp_forward_body, n_steps),
        grid=(n_steps,),
        in_specs=[
            fixed((tokens, width)),
            fixed((tokens, width)),
            fixed(mods.shape),
            pl.BlockSpec((1, width, CHUNK), lambda i: (base + 4 + i // per, 0, i % per)),
            pl.BlockSpec((4, 128, width), lambda i: (base // 4 + 2, i, 0)),
        ],
        out_specs=[
            pl.BlockSpec((tokens, CHUNK), lambda i: (0, i)),
            pl.BlockSpec((tokens, CHUNK), lambda i: (0, i)),
            fixed((tokens, width)),
            fixed((tokens, width)),
        ],
        out_shape=[
            jax.ShapeDtypeStruct((tokens, hidden), BF16),
            jax.ShapeDtypeStruct((tokens, hidden), BF16),
            jax.ShapeDtypeStruct((tokens, width), BF16),
            jax.ShapeDtypeStruct((tokens, width), result_type),
        ],
        scratch_shapes=[pltpu.VMEM((tokens, width), F32)],
        compiler_params=pltpu.CompilerParams(vmem_limit_bytes=56 * MIB),
        name="mlp_forward",
    )(normed_m, mid, mods, weights, weights)


def norm_back_rows(values, scale_row, grad):
    normed, inv = norm_stats(values)
    u = grad * (1.0 + scale_row)
    out = (
        u
        - jnp.mean(u, axis=-1, keepdims=True)
        - normed * jnp.mean(u * normed, axis=-1, keepdims=True)
    ) * inv
    return out, jnp.sum(grad, axis=0, keepdims=True), jnp.sum(grad * normed, axis=0, keepdims=True)


BLOCK_ROWS = 128


def backward_plan(tokens, width):
    rows = tokens // BLOCK_ROWS
    chunks = 4 * width // CHUNK
    halves = width // CHUNK
    pairs = width // 128
    sizes = (rows, chunks, rows, halves, pairs, 3 * halves, rows)
    starts = [0]
    for size in sizes:
        starts.append(starts[-1] + size)
    return starts


def backward_body(
    spatial, shapes, n_prev, n_own, tick_steps, nz,
    g_ref, down_ref, mid_ref, proj_ref, s_ref, m_ref, act_ref, dact_ref, w_ref, dn_ref,
    q_ref, k_ref, v_ref, p_ref, nm_hbm, att_hbm, na_hbm, prev_hbm,
    out_ref, dm_ref, rows_ref, grads_hbm, share_hbm,
    res_ref, gv_ref, e_ref, gm_ref, ga_ref, gq_ref, db_ref, gdb_ref, gub_ref,
    res_sem, gd_sem, gu_sem, *comm,
):
    n_win, n_query, n_key, chunk = shapes
    tokens, width = e_ref.shape
    starts = backward_plan(tokens, width)
    a0, a1, a2, a3, a4, a5, a6, end = starts
    halves = width // CHUNK
    step = pl.program_id(0)
    where = place(4 * nz)
    n_items = n_prev + n_own
    sources = []
    if n_prev:
        sources.append((prev_hbm, 8, n_prev))
    sources.append((grads_hbm, 0, n_own))

    @pl.when(step == 0)
    def _():
        greet_reduce(nz, where)

    def tick(t):
        reduce_tick(t, n_items, nz, where, sources, share_hbm, *comm)

    due = jnp.zeros((), jnp.bool_)
    passed = jnp.zeros((), jnp.int32)
    for s in tick_steps:
        due = jnp.logical_or(due, step == s)
        passed = passed + (step > s).astype(jnp.int32)

    def resident(source):
        return pltpu.make_async_copy(source, res_ref, res_sem)

    def put_down(i):
        slot = lax.rem(i, 2)
        target = grads_hbm.at[pl.ds(0, 4), i // 2, lax.rem(i, 2)]
        return pltpu.make_async_copy(gdb_ref.at[slot], target, gd_sem.at[slot])

    def put_cols(i, item, half):
        slot = lax.rem(i, 2)
        cols = pl.ds(pl.multiple_of(half * CHUNK, CHUNK), CHUNK)
        target = grads_hbm.at[item, :, :, :, :, cols]
        return pltpu.make_async_copy(gub_ref.at[slot], target, gu_sem.at[slot])

    def keep_cols(i, values):
        gub_ref[lax.rem(i, 2)] = values.reshape(gub_ref.shape[1:])

    def rows_at(i):
        return pl.ds(pl.multiple_of(i * BLOCK_ROWS, BLOCK_ROWS), BLOCK_ROWS)

    def add_e(first, left, right):
        part = tokens // 2
        for k in range(2):
            rows = slice(k * part, (k + 1) * part)
            value = dot_nt(left[rows], right)

            @pl.when(first)
            def _(rows=rows, value=value):
                e_ref[rows, :] = value

            @pl.when(jnp.logical_not(first))
            def _(rows=rows, value=value):
                e_ref[rows, :] += value

    @pl.when(step == 0)
    def _():
        resident(nm_hbm).start()
        rows_ref[...] = jnp.zeros_like(rows_ref)

    @pl.when(step < a1)
    def _():
        grad = g_ref[...].astype(F32)
        gv_ref[rows_at(step), :] = (m_ref[5:6, :] * grad).astype(BF16)
        rows_ref[5:6, :] += jnp.sum(grad * down_ref[...].astype(F32), axis=0, keepdims=True)

    @pl.when(step == a1)
    def _():
        resident(nm_hbm).wait()

    @pl.when(jnp.logical_and(step >= a1, step < a2))
    def _():
        i = step - a1

        @pl.when(i >= 2)
        def _():
            put_down(i).wait()
            put_cols(i, 4, 0).wait()

        gdv = gv_ref[...]
        grad_act = dot_nt(gdv, down_rows(dn_ref))
        gup = (grad_act * dact_ref[...].astype(F32)).astype(BF16)
        slot = lax.rem(i, 2)
        grad_down = dot_tn(act_ref[...], gdv).astype(BF16)
        for c in range(2):
            for sub in range(4):
                first = (c * 4 + sub) * 64
                gdb_ref[slot, sub, c] = grad_down[first : first + 64, :]
        put_down(i).start()
        keep_cols(i, dot_tn(res_ref[...], gup).astype(BF16))
        put_cols(i, 4 + i // halves, lax.rem(i, halves)).start()
        add_e(i == 0, gup, w_ref[0])

    @pl.when(step == a2)
    def _():
        resident(att_hbm).start()
        for k in range(2):
            put_down(k).wait()
            put_cols(k, 4, 0).wait()

    @pl.when(jnp.logical_and(step >= a2, step < a3))
    def _():
        rows = rows_at(step - a2)
        out, shift, scale = norm_back_rows(mid_ref[...], m_ref[4:5, :], e_ref[rows, :])
        grad_mid = out + g_ref[...].astype(F32)
        gm_ref[rows, :] = grad_mid
        gv_ref[rows, :] = (m_ref[2:3, :] * grad_mid).astype(BF16)
        rows_ref[3:4, :] += shift
        rows_ref[4:5, :] += scale
        rows_ref[2:3, :] += jnp.sum(grad_mid * proj_ref[...].astype(F32), axis=0, keepdims=True)

    @pl.when(step == a3)
    def _():
        resident(att_hbm).wait()

    @pl.when(jnp.logical_and(step >= a3, step < a4))
    def _():
        i = step - a3
        part = gv_ref[:, pl.ds(pl.multiple_of(i * CHUNK, CHUNK), CHUNK)]
        keep_cols(i, dot_tn(res_ref[...], part).astype(BF16))
        put_cols(i, 8, i).start()
        add_e(i == 0, part, w_ref[0])

    @pl.when(step == a4)
    def _():
        resident(na_hbm).start()
        ga_ref[...] = e_ref[...].astype(BF16)

    @pl.when(jnp.logical_and(step >= a4, step < a5))
    def _():
        head = step - a4
        lanes = pl.ds(pl.multiple_of(head * 128, 128), 128)
        attend_backward(
            spatial, n_win, n_query, n_key, chunk, head,
            q_ref, k_ref, v_ref, ga_ref.at[:, lanes], p_ref, gq_ref, dm_ref, db_ref,
        )

    @pl.when(step == a5)
    def _():
        resident(na_hbm).wait()

    @pl.when(jnp.logical_and(step >= a5, step < a6))
    def _():
        i = step - a5
        put_cols(i, 8, 0).wait()
        part = gq_ref[:, pl.ds(pl.multiple_of(i * CHUNK, CHUNK), CHUNK)]
        keep_cols(i, dot_tn(res_ref[...], part).astype(BF16))
        put_cols(i, 9 + i // halves, lax.rem(i, halves)).start()
        add_e(i == 0, part, w_ref[0])

    @pl.when(step >= a6)
    def _():
        rows = rows_at(step - a6)
        out, shift, scale = norm_back_rows(s_ref[...].astype(F32), m_ref[1:2, :], e_ref[rows, :])
        out_ref[...] = (out + gm_ref[rows, :]).astype(out_ref.dtype)
        rows_ref[0:1, :] += shift
        rows_ref[1:2, :] += scale

    @pl.when(due)
    def _():
        tick(passed)

    @pl.when(step == end - 1)
    def _():
        for k in range(2):
            put_cols(k, 8, 0).wait()

        def rest(t, carry):
            tick(t)
            return carry

        lax.fori_loop(len(tick_steps), n_items + REDUCE_TAIL, rest, 0)


def block_backward(grad, saved, mods, weights, base, spread_shape, spatial, out_type, prev, n_own, tick_steps, nz, cid):
    stream, normed_a, qkv, probs, att, proj, mid, normed_m, act, dact, down = saved
    tokens, width = mid.shape
    shapes = attention_shapes(spatial, tokens)
    n_win, n_query, n_key, _ = shapes
    pairs = width // 128
    halves = width // CHUNK
    a0, a1, a2, a3, a4, a5, a6, end = backward_plan(tokens, width)
    tail = spread_shape[1:]
    zeros = (0,) * len(tail)

    def at(start, stop):
        return lambda i: jnp.clip(i - start, 0, stop - start - 1)

    def row_block(place_of):
        return pl.BlockSpec((BLOCK_ROWS, width), lambda i: (place_of(i), 0))

    def g_at(i):
        return jnp.where(i < a1, i, at(a2, a3)(i))

    def weight_at(i):
        up = at(a1, a2)(i)
        proj_half = at(a3, a4)(i)
        third = at(a5, a6)(i)
        item = jnp.where(i < a3, 4 + up // halves, jnp.where(i < a5, 3, third // halves))
        half = jnp.where(i < a3, up % halves, jnp.where(i < a5, proj_half, third % halves))
        return (base + item, 0, half)

    heads = at(a4, a5)
    hidden = pl.BlockSpec((tokens, CHUNK), lambda i: (0, at(a1, a2)(i)))
    anywhere = pl.BlockSpec(memory_space=pl.ANY)
    n_prev = 0 if prev is None else 4
    n_items = n_prev + n_own
    extra = [] if prev is None else [prev]
    body = functools.partial(backward_body, spatial, shapes, n_prev, n_own, tick_steps, nz)
    if prev is None:
        whole = body

        def body(*refs):
            return whole(*refs[:17], None, *refs[17:])

    dma = pltpu.SemaphoreType.DMA
    return pl.pallas_call(
        body,
        grid=(end,),
        in_specs=[
            row_block(g_at),
            row_block(at(a0, a1)),
            row_block(at(a2, a3)),
            row_block(at(a2, a3)),
            row_block(at(a6, end)),
            fixed(mods.shape),
            hidden,
            hidden,
            pl.BlockSpec((1, width, CHUNK), weight_at),
            pl.BlockSpec((4, 128, width), lambda i: (base // 4 + 2, at(a1, a2)(i), 0)),
            pl.BlockSpec((tokens, 128), lambda i: (0, heads(i))),
            pl.BlockSpec((tokens, 128), lambda i: (0, pairs + heads(i))),
            pl.BlockSpec((tokens, 128), lambda i: (0, 2 * pairs + heads(i))),
            pl.BlockSpec((2, n_win, n_query, n_key), lambda i: (heads(i), 0, 0, 0)),
            anywhere, anywhere, anywhere,
        ] + [anywhere] * len(extra),
        out_specs=[
            row_block(at(a6, end)),
            pl.BlockSpec((2,) + tail, lambda i: (heads(i),) + zeros),
            pl.BlockSpec((8, width), lambda i: (0, 0)),
            anywhere,
            anywhere,
        ],
        out_shape=[
            jax.ShapeDtypeStruct((tokens, width), out_type),
            jax.ShapeDtypeStruct(spread_shape, F32),
            jax.ShapeDtypeStruct((8, width), F32),
            jax.ShapeDtypeStruct((12, nz, 2, 2, ROWS, COLS), BF16),
            jax.ShapeDtypeStruct((n_items, ROWS, COLS), F32),
        ],
        scratch_shapes=[
            pltpu.VMEM((tokens, width), BF16),
            pltpu.VMEM((tokens, width), BF16),
            pltpu.VMEM((tokens, width), F32),
            pltpu.VMEM((tokens, width), F32),
            pltpu.VMEM((tokens, width), BF16),
            pltpu.VMEM((tokens, 3 * width), BF16),
            pltpu.VMEM((2, n_query, n_key), F32),
            pltpu.VMEM((2, 4, 2, ROWS, COLS), BF16),
            pltpu.VMEM((2, nz, 2, 2, ROWS, CHUNK), BF16),
            dma,
            dma((2,)),
            dma((2,)),
        ] + reduce_scratch(nz),
        compiler_params=pltpu.CompilerParams(
            collective_id=cid, has_side_effects=True, vmem_limit_bytes=64 * MIB
        ),
        name="block_backward",
    )(grad, down, mid, proj, stream, mods, act, dact, weights, weights, qkv, qkv, qkv, probs,
      normed_m, att, normed_a, *extra)


def block_forward(stream, mods, weights, base, spread, key_ok, spatial, result_type):
    normed_a, qkv = qkv_forward(stream, mods, weights, base)
    att, probs = attention_forward(spatial, qkv, spread, key_ok)
    proj, mid, normed_m = proj_forward(att, stream, mods, weights, base)
    act, dact, down, result = mlp_forward(normed_m, mid, mods, weights, base, result_type)
    return result, (stream, normed_a, qkv, probs, att, proj, mid, normed_m, act, dact, down)


def swap_rows(values, me, swap):
    keep = lax.dynamic_index_in_dim(values, me, 1, keepdims=False)
    send = lax.dynamic_index_in_dim(values, 1 - me, 1, keepdims=False)
    recv = lax.ppermute(send.astype(BF16), "frame", swap).astype(values.dtype)
    first = jnp.where(me == 0, keep, recv)
    second = jnp.where(me == 0, recv, keep)
    full = jnp.concatenate([first, second], axis=0)
    return full.transpose(2, 0, 1, 3, 4).reshape(-1, values.shape[-1])


def unswap_rows(values, me, swap, n_cw, f_l):
    depth = values.shape[-1]
    full = values.reshape(n_cw, 2, f_l, TWIN, TWIN, depth)
    keep = lax.dynamic_index_in_dim(full, me, 1, keepdims=False)
    send = lax.dynamic_index_in_dim(full, 1 - me, 1, keepdims=False)
    recv = lax.ppermute(send.astype(BF16), "frame", swap).astype(values.dtype)
    first = jnp.where(me == 0, keep, recv)
    second = jnp.where(me == 0, recv, keep)
    both = jnp.stack([first, second], axis=0)
    return both.transpose(2, 0, 3, 1, 4, 5).reshape(-1, depth)


def pack_shards(shards, b):
    w_qkv, w_proj, w_up, w_down = [w[:, b] for w in shards]
    parts = []
    for w in (w_qkv, w_proj, w_up):
        parts.append(w.reshape(ROWS, -1, COLS).transpose(1, 0, 2))
    parts.append(w_down.reshape(-1, ROWS, COLS))
    return jnp.concatenate(parts, axis=0)


def on_device(
    frames_in, size_group, modulation, w_qkv, w_proj, w_up, w_down, table_sp, table_st, cotangent
):
    n_clips, f_l, n_rows, n_cols, width = frames_in.shape
    me = lax.axis_index("frame")
    swap = [(0, 1), (1, 0)]
    n_cw = n_cols // TWIN
    nz = lax.axis_size("clip") // 4
    natural = (f_l, 2, TWIN, n_cw, TWIN, width)
    shards = (w_qkv, w_proj, w_up, w_down)
    packed = jnp.concatenate([pack_shards(shards, b) for b in range(2)], axis=0)
    full = gather_all(packed, nz, 1).reshape(24, 16 * ROWS, COLS)
    limit = n_cols - 3 * (2 - size_group[0])
    wide = (jnp.arange(n_cols, dtype=jnp.int32) < limit).astype(F32)
    ok_sp = jnp.broadcast_to(wide[None, None, None, :], (f_l, 1, n_rows, n_cols))
    ok_sp = ok_sp.reshape(f_l, 1, n_rows * n_cols)
    frame_ok = (jnp.arange(KEYF) < FILLED).astype(F32)
    ok_st = wide.reshape(n_cw, 1, 1, TWIN) * frame_ok[None, :, None, None]
    ok_st = jnp.broadcast_to(ok_st, (n_cw, KEYF, TWIN, TWIN)).reshape(n_cw, 1, -1)
    spread0 = spread_sp(table_sp)
    spread1 = spread_st(table_st)
    mods = modulation[0].reshape(2, 6, width)
    mods = jnp.pad(mods, ((0, 0), (0, 2), (0, 0)))
    cot = swap_rows(cotangent.reshape(natural), me, swap)
    stream0 = frames_in.reshape(-1, width).astype(F32)
    mid_stream, saved0 = block_forward(stream0, mods[0], full, 0, spread0, ok_sp, True, F32)
    stream1 = swap_rows(mid_stream.reshape(natural), me, swap)
    end_stream, saved1 = block_forward(stream1, mods[1], full, 12, spread1, ok_st, False, BF16)
    mixed = unswap_rows(end_stream, me, swap, n_cw, f_l).reshape(frames_in.shape)
    starts = backward_plan(stream0.shape[0], width)
    ticks1 = tuple(range(starts[2], starts[6] + 4, 2))
    grad1, gspread1, rows1, gw1, shares1 = block_backward(
        cot, saved1, mods[1], full, 12, spread1.shape, False, F32, None, 8, ticks1, nz, 2
    )
    grad_mid = unswap_rows(grad1, me, swap, n_cw, f_l)
    ticks0 = (0,) + tuple(range(starts[1], starts[2], 3)) + tuple(range(starts[2], starts[6] + 4, 2))
    grad0, gspread0, rows0, gw0, shares0 = block_backward(
        grad_mid, saved0, mods[0], full, 0, spread0.shape, True, BF16, gw1, 8, ticks0, nz, 3
    )
    last = reduce_all([gw0], [(8, 4)], nz, 4)
    shares = jnp.stack([
        jnp.concatenate([shares0[4:12], last], axis=0),
        jnp.concatenate([shares1, shares0[0:4]], axis=0),
    ])

    def columns(lo, hi):
        part = shares[:, lo:hi]
        return part.transpose(2, 0, 1, 3).reshape(ROWS, 2, (hi - lo) * COLS)

    g_down = shares[:, 0:4].reshape(2, 4 * ROWS, COLS).transpose(1, 0, 2)
    outs = (columns(9, 12), columns(8, 9), columns(4, 8), g_down)
    mod_grad = lax.psum(jnp.concatenate([rows0[:6], rows1[:6]], axis=0), "frame")[None]
    g_sp = lax.psum(gather_sp(gspread0), ("clip", "frame"))
    g_st = lax.psum(gather_st(gspread1), ("clip", "frame"))
    grad_in = grad0.reshape(frames_in.shape)
    return (mixed, grad_in, mod_grad, outs[0], outs[1], outs[2], outs[3], g_sp, g_st)


HIGHEST = lax.Precision.HIGHEST


def layer_norm(values):
    centered = values - jnp.mean(values, axis=-1, keepdims=True)
    spread = jnp.mean(centered * centered, axis=-1, keepdims=True)
    return centered * lax.rsqrt(spread + NORM_EPS)


def modulate(values, shift_row, scale_row):
    return layer_norm(values) * (1.0 + scale_row) + shift_row


def gelu_tanh(values):
    return jax.nn.gelu(values, approximate=True)


def row_of(mod_rows, which):
    return mod_rows[:, which][:, None, None, None, :]


def clip_sum(values):
    return jnp.sum(values, axis=(1, 2, 3))


def flat_dot(values, weight):
    flat_in = values.reshape(-1, values.shape[-1])
    flat_out = jnp.dot(flat_in, weight, preferred_element_type=jnp.float32)
    return flat_out.reshape(values.shape[:-1] + (weight.shape[1],))


def back_dot(grad_values, weight):
    flat_in = grad_values.reshape(-1, grad_values.shape[-1])
    flat_out = jnp.einsum("nb,ab->na", flat_in, weight, preferred_element_type=jnp.float32)
    return flat_out.reshape(grad_values.shape[:-1] + (weight.shape[0],))


def outer_dot(left_values, right_values):
    left_flat = left_values.reshape(-1, left_values.shape[-1])
    right_flat = right_values.reshape(-1, right_values.shape[-1])
    return jnp.einsum("na,nb->ab", left_flat, right_flat, preferred_element_type=jnp.float32)


def split_heads(values, n_heads):
    return values.reshape(values.shape[0], values.shape[1], n_heads, -1)


def offset_pick(side_len):
    position = jnp.arange(side_len, dtype=jnp.int32)
    offsets = position[:, None] - position[None, :] + side_len - 1
    targets = jnp.arange(2 * side_len - 1, dtype=jnp.int32)
    return (offsets[:, :, None] == targets[None, None, :]).astype(jnp.float32)


def expand_bias(table, side_len):
    one_hot = offset_pick(side_len)
    rows_done = jnp.einsum("hab,xya->hxyb", table, one_hot, precision=HIGHEST)
    full_bias = jnp.einsum("hxyb,uvb->hxuyv", rows_done, one_hot, precision=HIGHEST)
    return full_bias.reshape(table.shape[0], side_len * side_len, side_len * side_len)


def cube_bias(table_st, first_frame, local_frames):
    n_heads = table_st.shape[0]
    span_frames = 2 * FRAMES - 1
    side_span = 2 * TWIN - 1
    table_cube = table_st.reshape(n_heads, span_frames, side_span * side_span)
    query_frames = first_frame + jnp.arange(local_frames, dtype=jnp.int32)
    key_frames = jnp.arange(FRAMES, dtype=jnp.int32)
    offsets = query_frames[:, None] - key_frames[None, :] + FRAMES - 1
    choose = (
        offsets[:, :, None] == jnp.arange(span_frames, dtype=jnp.int32)[None, None, :]
    ).astype(jnp.float32)
    picked = jnp.einsum("hoz,jfo->hjfz", table_cube, choose, precision=HIGHEST)
    squares = expand_bias(picked.reshape(-1, side_span, side_span), TWIN)
    squares = squares.reshape(n_heads, local_frames, FRAMES, TWIN * TWIN, TWIN * TWIN)
    squares = squares.transpose(0, 1, 3, 2, 4)
    return squares.reshape(n_heads, local_frames * TWIN * TWIN, FRAMES * TWIN * TWIN)


def spatial_windows(values):
    n_clips, n_frames, n_rows, n_cols, n_depth = values.shape
    blocked = values.reshape(n_clips, n_frames, n_rows // SWIN, SWIN, n_cols // SWIN, SWIN, n_depth)
    return blocked.transpose(0, 1, 2, 4, 3, 5, 6).reshape(-1, SWIN * SWIN, n_depth)


def spatial_unwindow(values, full_shape):
    n_clips, n_frames, n_rows, n_cols, n_depth = full_shape
    blocked = values.reshape(n_clips, n_frames, n_rows // SWIN, n_cols // SWIN, SWIN, SWIN, n_depth)
    return blocked.transpose(0, 1, 2, 4, 3, 5, 6).reshape(full_shape)


def cube_windows(values):
    n_clips, n_frames, n_rows, n_cols, n_depth = values.shape
    blocked = values.reshape(n_clips, n_frames, n_rows // TWIN, TWIN, n_cols // TWIN, TWIN, n_depth)
    blocked = blocked.transpose(0, 2, 4, 1, 3, 5, 6)
    return blocked.reshape(
        n_clips * (n_rows // TWIN) * (n_cols // TWIN), n_frames * TWIN * TWIN, n_depth
    )


def cube_unwindow(values, full_shape):
    n_clips, n_frames, n_rows, n_cols, n_depth = full_shape
    blocked = values.reshape(n_clips, n_rows // TWIN, n_cols // TWIN, n_frames, TWIN, TWIN, n_depth)
    return blocked.transpose(0, 3, 1, 4, 2, 5, 6).reshape(full_shape)


def soft_scores(query_win, key_win, bias, key_ok, score_scale):
    scores = jnp.einsum("nqhd,nkhd->nhqk", query_win, key_win, preferred_element_type=jnp.float32)
    scores = scores * score_scale + bias[None]
    scores = jnp.where(key_ok[:, None, None, :], scores, NEG_FILL)
    row_top = jnp.max(scores, axis=-1, keepdims=True)
    expo_values = jnp.exp(scores - row_top)
    return expo_values / jnp.sum(expo_values, axis=-1, keepdims=True)


def general_forward(
    stream,
    mod_rows,
    weights,
    n_heads,
    bias,
    key_ok,
    to_windows,
    from_windows,
    fetch_keys,
    score_scale,
):
    qkv_w, proj_w, up_w, down_w = weights
    width_d = stream.shape[-1]
    normed_a = modulate(stream, row_of(mod_rows, 0), row_of(mod_rows, 1)).astype(jnp.bfloat16)
    qkv_values = flat_dot(normed_a, qkv_w).astype(jnp.bfloat16)
    key_local = qkv_values[..., width_d : 2 * width_d]
    value_local = qkv_values[..., 2 * width_d :]
    query_win = split_heads(to_windows(qkv_values[..., :width_d]), n_heads)
    key_flat, value_flat = fetch_keys(key_local, value_local)
    key_win = split_heads(key_flat, n_heads)
    value_win = split_heads(value_flat, n_heads)
    soft_probs = soft_scores(query_win, key_win, bias, key_ok, score_scale)
    att_win = jnp.einsum(
        "nhqk,nkhd->nqhd",
        soft_probs.astype(jnp.bfloat16),
        value_win,
        preferred_element_type=jnp.float32,
    ).astype(jnp.bfloat16)
    att_out = from_windows(
        att_win.reshape(att_win.shape[0], att_win.shape[1], width_d), stream.shape
    )
    proj_out = flat_dot(att_out, proj_w)
    mid_stream = stream + row_of(mod_rows, 2) * proj_out
    normed_m = modulate(mid_stream, row_of(mod_rows, 3), row_of(mod_rows, 4)).astype(jnp.bfloat16)
    up_value = flat_dot(normed_m, up_w)
    active = gelu_tanh(up_value).astype(jnp.bfloat16)
    down_out = flat_dot(active, down_w)
    result = mid_stream + row_of(mod_rows, 5) * down_out
    saved = (
        stream,
        normed_a,
        query_win,
        key_win,
        value_win,
        key_local,
        value_local,
        att_out,
        proj_out,
        mid_stream,
        normed_m,
        up_value,
        active,
        down_out,
    )
    return (result, saved)


def general_backward(
    grad_out,
    saved,
    mod_rows,
    weights,
    n_heads,
    bias,
    key_ok,
    to_windows,
    from_windows,
    return_keys,
    key_win,
    value_win,
    score_scale,
):
    (
        stream,
        normed_a,
        query_win,
        unused_key,
        unused_value,
        key_local,
        value_local,
        att_out,
        proj_out,
        mid_stream,
        normed_m,
        up_value,
        active,
        down_out,
    ) = saved
    qkv_w, proj_w, up_w, down_w = weights
    n_clips = stream.shape[0]
    width_d = stream.shape[-1]
    grad_down_v = (row_of(mod_rows, 5) * grad_out).astype(jnp.bfloat16)
    gate_m_grad = clip_sum(grad_out * down_out)
    down_grad = outer_dot(active, grad_down_v)
    grad_act = back_dot(grad_down_v, down_w)
    unused_gelu, gelu_pull = jax.vjp(gelu_tanh, up_value)
    grad_up_v = gelu_pull(grad_act)[0].astype(jnp.bfloat16)
    up_grad = outer_dot(normed_m, grad_up_v)
    grad_normed = back_dot(grad_up_v, up_w)
    unused_norm, norm_pull = jax.vjp(modulate, mid_stream, row_of(mod_rows, 3), row_of(mod_rows, 4))
    grad_mid, shift_m_grad, scale_m_grad = norm_pull(grad_normed)
    grad_mid = grad_mid + grad_out
    grad_proj_v = (row_of(mod_rows, 2) * grad_mid).astype(jnp.bfloat16)
    gate_a_grad = clip_sum(grad_mid * proj_out)
    proj_grad = outer_dot(att_out, grad_proj_v)
    grad_att = back_dot(grad_proj_v, proj_w).astype(jnp.bfloat16)
    grad_att_win = split_heads(to_windows(grad_att), n_heads)
    soft_probs = soft_scores(query_win, key_win, bias, key_ok, score_scale)
    grad_probs = jnp.einsum(
        "nqhd,nkhd->nhqk", grad_att_win, value_win, preferred_element_type=jnp.float32
    )
    row_delta = jnp.sum(soft_probs * grad_probs, axis=-1, keepdims=True)
    grad_scores = (soft_probs * (grad_probs - row_delta)).astype(jnp.bfloat16)
    grad_bias = jnp.sum(grad_scores.astype(jnp.float32), axis=0)
    grad_query = (
        jnp.einsum("nhqk,nkhd->nqhd", grad_scores, key_win, preferred_element_type=jnp.float32)
        * score_scale
    )
    grad_key = (
        jnp.einsum("nhqk,nqhd->nkhd", grad_scores, query_win, preferred_element_type=jnp.float32)
        * score_scale
    )
    grad_value = jnp.einsum(
        "nhqk,nqhd->nkhd",
        soft_probs.astype(jnp.bfloat16),
        grad_att_win,
        preferred_element_type=jnp.float32,
    )
    n_win = grad_query.shape[0]
    grad_query = from_windows(grad_query.reshape(n_win, grad_query.shape[1], width_d), stream.shape)
    grad_key_full, grad_value_full = return_keys(
        grad_key.reshape(n_win, grad_key.shape[1], width_d),
        grad_value.reshape(n_win, grad_value.shape[1], width_d),
    )
    grad_qkv_v = jnp.concatenate([grad_query, grad_key_full, grad_value_full], axis=-1).astype(
        jnp.bfloat16
    )
    qkv_grad = outer_dot(normed_a, grad_qkv_v)
    grad_normed = back_dot(grad_qkv_v, qkv_w)
    unused_norm, norm_pull = jax.vjp(modulate, stream, row_of(mod_rows, 0), row_of(mod_rows, 1))
    grad_stream, shift_a_grad, scale_a_grad = norm_pull(grad_normed)
    grad_stream = grad_stream + grad_mid
    mod_grad = jnp.stack(
        [
            shift_a_grad.reshape(n_clips, width_d),
            scale_a_grad.reshape(n_clips, width_d),
            gate_a_grad,
            shift_m_grad.reshape(n_clips, width_d),
            scale_m_grad.reshape(n_clips, width_d),
            gate_m_grad,
        ],
        axis=1,
    )
    return (grad_stream, mod_grad, (qkv_grad, proj_grad, up_grad, down_grad), grad_bias)


def on_device_general(
    frames_in, size_group, modulation, w_qkv, w_proj, w_up, w_down, table_sp, table_st, cotangent
):
    n_clips, local_frames, n_rows, n_cols, width_d = frames_in.shape
    n_heads = table_sp.shape[0]
    score_scale = (width_d // n_heads) ** (-0.5)
    first_frame = lax.axis_index("frame") * local_frames
    local_shape = (n_clips, local_frames, n_rows, n_cols, width_d)
    whole_shape = (n_clips, FRAMES, n_rows, n_cols, width_d)
    gathered = (
        lax.all_gather(w_qkv, "clip", axis=0, tiled=True),
        lax.all_gather(w_proj, "clip", axis=0, tiled=True),
        lax.all_gather(w_up, "clip", axis=0, tiled=True),
        lax.all_gather(w_down, "clip", axis=0, tiled=True),
    )
    column_ids = jnp.arange(n_cols, dtype=jnp.int32)
    column_limit = n_cols - 3 * (2 - size_group)
    wide_ok = column_ids[None, :] < column_limit[:, None]
    local_ok = jnp.broadcast_to(wide_ok[:, None, None, :], (n_clips, local_frames, n_rows, n_cols))
    spatial_ok = spatial_windows(local_ok[..., None])[..., 0]
    frame_ok = jnp.arange(FRAMES, dtype=jnp.int32) < FILLED
    cube_grid = wide_ok[:, None, None, :] & frame_ok[None, :, None, None]
    cube_grid = jnp.broadcast_to(cube_grid, (n_clips, FRAMES, n_rows, n_cols))
    cube_ok = cube_windows(cube_grid[..., None])[..., 0]
    span_sp = 2 * SWIN - 1

    def build_spatial(table):
        return expand_bias(table.reshape(n_heads, span_sp, span_sp), SWIN)

    def build_cube(table):
        return cube_bias(table, first_frame, local_frames)

    bias_sp, pull_sp = jax.vjp(build_spatial, table_sp)
    bias_st, pull_st = jax.vjp(build_cube, table_st)

    def spatial_keys(key_local, value_local):
        return (spatial_windows(key_local), spatial_windows(value_local))

    def cube_keys(key_local, value_local):
        key_all, value_all = (
            lax.all_gather(key_local, "frame", axis=1, tiled=True),
            lax.all_gather(value_local, "frame", axis=1, tiled=True),
        )
        return (cube_windows(key_all), cube_windows(value_all))

    def spatial_return(grad_key, grad_value):
        return (spatial_unwindow(grad_key, local_shape), spatial_unwindow(grad_value, local_shape))

    def cube_return(grad_key, grad_value):
        key_whole = cube_unwindow(grad_key, whole_shape)
        value_whole = cube_unwindow(grad_value, whole_shape)
        return (
            lax.psum_scatter(
                key_whole.astype(jnp.bfloat16), "frame", scatter_dimension=1, tiled=True
            ).astype(jnp.float32),
            lax.psum_scatter(
                value_whole.astype(jnp.bfloat16), "frame", scatter_dimension=1, tiled=True
            ).astype(jnp.float32),
        )

    weights_sp = (gathered[0][:, 0], gathered[1][:, 0], gathered[2][:, 0], gathered[3][:, 0])
    weights_st = (gathered[0][:, 1], gathered[1][:, 1], gathered[2][:, 1], gathered[3][:, 1])
    stream_mid, saved_sp = general_forward(
        frames_in.astype(jnp.float32),
        modulation[:, 0:6],
        weights_sp,
        n_heads,
        bias_sp,
        spatial_ok,
        spatial_windows,
        spatial_unwindow,
        spatial_keys,
        score_scale,
    )
    stream_end, saved_st = general_forward(
        stream_mid,
        modulation[:, 6:12],
        weights_st,
        n_heads,
        bias_st,
        cube_ok,
        cube_windows,
        cube_unwindow,
        cube_keys,
        score_scale,
    )
    mixed = stream_end.astype(jnp.bfloat16)
    again = (
        lax.all_gather(w_qkv, "clip", axis=0, tiled=True),
        lax.all_gather(w_proj, "clip", axis=0, tiled=True),
        lax.all_gather(w_up, "clip", axis=0, tiled=True),
        lax.all_gather(w_down, "clip", axis=0, tiled=True),
    )
    back_sp = (again[0][:, 0], again[1][:, 0], again[2][:, 0], again[3][:, 0])
    back_st = (again[0][:, 1], again[1][:, 1], again[2][:, 1], again[3][:, 1])
    key_again, value_again = (
        lax.all_gather(saved_st[5], "frame", axis=1, tiled=True),
        lax.all_gather(saved_st[6], "frame", axis=1, tiled=True),
    )
    key_win_st = split_heads(cube_windows(key_again), n_heads)
    value_win_st = split_heads(cube_windows(value_again), n_heads)
    grad_stream, mod_grad_st, grads_st, bias_grad_st = general_backward(
        cotangent.astype(jnp.float32),
        saved_st,
        modulation[:, 6:12],
        back_st,
        n_heads,
        bias_st,
        cube_ok,
        cube_windows,
        cube_unwindow,
        cube_return,
        key_win_st,
        value_win_st,
        score_scale,
    )
    grad_stream, mod_grad_sp, grads_sp, bias_grad_sp = general_backward(
        grad_stream,
        saved_sp,
        modulation[:, 0:6],
        back_sp,
        n_heads,
        bias_sp,
        spatial_ok,
        spatial_windows,
        spatial_unwindow,
        spatial_return,
        saved_sp[3],
        saved_sp[4],
        score_scale,
    )
    table_sp_grad = pull_sp(bias_grad_sp)[0]
    table_st_grad = pull_st(bias_grad_st)[0]
    full_qkv = jnp.stack([grads_sp[0], grads_st[0]], axis=1)
    full_proj = jnp.stack([grads_sp[1], grads_st[1]], axis=1)
    full_up = jnp.stack([grads_sp[2], grads_st[2]], axis=1)
    full_down = jnp.stack([grads_sp[3], grads_st[3]], axis=1)
    shares = (
        lax.psum_scatter(
            full_qkv.astype(jnp.bfloat16), "clip", scatter_dimension=0, tiled=True
        ).astype(jnp.float32),
        lax.psum_scatter(
            full_proj.astype(jnp.bfloat16), "clip", scatter_dimension=0, tiled=True
        ).astype(jnp.float32),
        lax.psum_scatter(
            full_up.astype(jnp.bfloat16), "clip", scatter_dimension=0, tiled=True
        ).astype(jnp.float32),
        lax.psum_scatter(
            full_down.astype(jnp.bfloat16), "clip", scatter_dimension=0, tiled=True
        ).astype(jnp.float32),
    )
    mod_grad = jnp.concatenate([mod_grad_sp, mod_grad_st], axis=1)
    summed = (
        lax.psum(shares[0].astype(jnp.bfloat16), "frame").astype(jnp.float32),
        lax.psum(shares[1].astype(jnp.bfloat16), "frame").astype(jnp.float32),
        lax.psum(shares[2].astype(jnp.bfloat16), "frame").astype(jnp.float32),
        lax.psum(shares[3].astype(jnp.bfloat16), "frame").astype(jnp.float32),
        lax.psum(mod_grad.astype(jnp.bfloat16), "frame").astype(jnp.float32),
        lax.psum(table_sp_grad.astype(jnp.bfloat16), "frame").astype(jnp.float32),
        lax.psum(table_st_grad.astype(jnp.bfloat16), "frame").astype(jnp.float32),
    )
    tables = (
        lax.psum(summed[5].astype(jnp.bfloat16), "clip").astype(jnp.float32),
        lax.psum(summed[6].astype(jnp.bfloat16), "clip").astype(jnp.float32),
    )
    return (
        mixed,
        grad_stream.astype(jnp.bfloat16),
        summed[4],
        summed[0],
        summed[1],
        summed[2],
        summed[3],
        tables[0],
        tables[1],
    )


def solution(mesh):
    placed = (
        P("clip", "frame", None, None, None),
        P("clip"),
        P("clip", None, None),
        P("clip", None, None),
        P("clip", None, None),
        P("clip", None, None),
        P("clip", None, None),
        P(),
        P(),
        P("clip", "frame", None, None, None),
    )
    whole_windows = mesh.shape["frame"] == 2 and mesh.shape["clip"] == 16
    return jax.shard_map(
        on_device if whole_windows else on_device_general,
        mesh=mesh,
        in_specs=placed,
        out_specs=(
            P("clip", "frame", None, None, None),
            P("clip", "frame", None, None, None),
            P("clip", None, None),
            P("clip", None, None),
            P("clip", None, None),
            P("clip", None, None),
            P("clip", None, None),
            P(),
            P(),
        ),
        check_vma=False,
    )
```

```python
import functools

import jax
import jax.numpy as jnp
from jax import lax
from jax.experimental import pallas as pl
from jax.experimental.pallas import tpu as pltpu
from jax.sharding import PartitionSpec as P

SWIN = 16
TWIN = 8
FRAMES = 8
FILLED = 5
KEYF = 6
NEG_FILL = -1000000000.0
NORM_EPS = 1e-06
F32 = jnp.float32
BF16 = jnp.bfloat16
NT = (((1,), (1,)), ((), ()))
TN = (((0,), (0,)), ((), ()))


def dot_nn(a, b):
    return jnp.dot(a, b, preferred_element_type=F32)


def dot_nt(a, b):
    return lax.dot_general(a, b, NT, preferred_element_type=F32)


def dot_tn(a, b):
    return lax.dot_general(a, b, TN, preferred_element_type=F32)


def norm_stats(values):
    mean = jnp.mean(values, axis=-1, keepdims=True)
    centered = values - mean
    spread = jnp.mean(centered * centered, axis=-1, keepdims=True)
    inv = lax.rsqrt(spread + NORM_EPS)
    return centered * inv, inv


def pick_sp():
    span = 2 * SWIN - 1
    shape = (8 * span, SWIN, 128)
    source = lax.broadcasted_iota(jnp.int32, shape, 0)
    ci = lax.broadcasted_iota(jnp.int32, shape, 1)
    lane = lax.broadcasted_iota(jnp.int32, shape, 2)
    hit = (source // span == 7 - lane // SWIN) & (source % span == SWIN - 1 + ci - lane % SWIN)
    return hit.astype(F32).reshape(8 * span, SWIN * 128)


def pick_st():
    span = 2 * TWIN - 1
    shape = (span * span, TWIN, 128)
    source = lax.broadcasted_iota(jnp.int32, shape, 0)
    ci = lax.broadcasted_iota(jnp.int32, shape, 1)
    lane = lax.broadcasted_iota(jnp.int32, shape, 2)
    row = span - 1 - lane // TWIN
    hit = (source // span == row) & (source % span == TWIN - 1 + ci - lane % TWIN)
    return hit.astype(F32).reshape(span * span, TWIN * 128)


def spread_sp(table):
    n_heads = table.shape[0]
    span = 2 * SWIN - 1
    padded = jnp.pad(table, ((0, 0), (span, 0))).reshape(n_heads * 4, 8 * span)
    out = jnp.dot(padded, pick_sp(), precision=lax.Precision.HIGHEST)
    return out.reshape(n_heads, 4, SWIN, 128)


def spread_st(table):
    n_heads = table.shape[0]
    span = 2 * TWIN - 1
    fspan = 2 * FRAMES - 1
    flat = table.reshape(n_heads * fspan, span * span)
    out = jnp.dot(flat, pick_st(), precision=lax.Precision.HIGHEST)
    return out.reshape(n_heads, fspan, TWIN, 128)


def gather_sp(spread):
    n_heads = spread.shape[0]
    span = 2 * SWIN - 1
    flat = spread.reshape(n_heads * 4, SWIN * 128)
    out = lax.dot_general(flat, pick_sp(), NT, precision=lax.Precision.HIGHEST)
    return out.reshape(n_heads, 32 * span)[:, span:]


def gather_st(spread):
    n_heads = spread.shape[0]
    span = 2 * TWIN - 1
    fspan = 2 * FRAMES - 1
    flat = spread.reshape(n_heads * fspan, TWIN * 128)
    out = lax.dot_general(flat, pick_st(), NT, precision=lax.Precision.HIGHEST)
    return out.reshape(n_heads, fspan * span * span)


def fill_bias_sp(spread_ref, hh, bias_ref):
    spread = jnp.concatenate([spread_ref[hh, g] for g in (3, 2, 1, 0)], axis=1)
    width = spread.shape[1]
    win = SWIN * SWIN
    for ri in range(SWIN):
        shift = (width - (SWIN - 1 - ri) * SWIN) % width
        rolled = pltpu.roll(spread, shift, 1) if shift else spread
        bias_ref[ri * SWIN : (ri + 1) * SWIN, :] = rolled[:, :win]


def fold_bias_sp(grad_ref, out_ref, hh):
    win = SWIN * SWIN
    width = 2 * win
    total = None
    for ri in range(SWIN):
        rows = grad_ref[ri * SWIN : (ri + 1) * SWIN, :]
        rows = jnp.concatenate([rows, jnp.zeros((SWIN, width - win), F32)], axis=1)
        shift = (SWIN - 1 - ri) * SWIN
        rows = pltpu.roll(rows, shift, 1) if shift else rows
        total = rows if total is None else total + rows
    for g in range(4):
        out_ref[hh, g] = total[:, (3 - g) * 128 : (4 - g) * 128]


def fill_bias_st(spread_ref, hh, bias_ref):
    lanes = lax.broadcasted_iota(jnp.int32, (TWIN, 128), 1)
    half = TWIN * TWIN
    n_pairs = KEYF // 2
    for ri in range(TWIN):
        shift = (128 - (TWIN - 1 - ri) * TWIN) % 128
        cache = {}

        def low_of(f):
            if f not in cache:
                rows = spread_ref[hh, 2 * FRAMES - 2 - f]
                cache[f] = pltpu.roll(rows, shift, 1) if shift else rows
            return cache[f]

        pairs = {}
        for fi in range(FRAMES):
            for pair in range(n_pairs):
                f = FRAMES - 1 - fi + 2 * pair
                if f not in pairs:
                    pairs[f] = jnp.where(
                        lanes < half, low_of(f), pltpu.roll(low_of(f + 1), half, 1)
                    )
                row = fi * half + ri * TWIN
                bias_ref[row : row + TWIN, pair * 128 : (pair + 1) * 128] = pairs[f]


def fold_bias_st(grad_ref, out_ref, hh):
    lanes = lax.broadcasted_iota(jnp.int32, (TWIN, 128), 1)
    half = TWIN * TWIN
    n_pairs = KEYF // 2
    fspan = 2 * FRAMES - 1
    totals = [None] * fspan
    for ri in range(TWIN):
        sums = {}
        for fi in range(FRAMES):
            for pair in range(n_pairs):
                f = FRAMES - 1 - fi + 2 * pair
                row = fi * half + ri * TWIN
                part = grad_ref[row : row + TWIN, pair * 128 : (pair + 1) * 128]
                sums[f] = part if f not in sums else sums[f] + part
        for f in range(fspan):
            piece = None
            if f in sums:
                piece = jnp.where(lanes < half, sums[f], 0.0)
            if f - 1 in sums:
                upper = pltpu.roll(jnp.where(lanes >= half, sums[f - 1], 0.0), half, 1)
                piece = upper if piece is None else piece + upper
            if piece is None:
                continue
            shift = (TWIN - 1 - ri) * TWIN
            piece = pltpu.roll(piece, shift, 1) if shift else piece
            totals[f] = piece if totals[f] is None else totals[f] + piece
    for f in range(fspan):
        out_ref[hh, 2 * FRAMES - 2 - f] = jnp.zeros((TWIN, 128), F32) if totals[f] is None else totals[f]


def lane_mask(rows, hh):
    lanes = lax.broadcasted_iota(jnp.int32, (rows, 128), 1)
    return (lanes < 64) if hh == 0 else (lanes >= 64)


def attend_forward(spatial, n_win, n_query, n_key, chunk, q_ref, k_ref, v_ref, m_ref, ok_ref, att_ref, p_ref, bias_ref):
    for hh in range(2):
        if spatial:
            fill_bias_sp(m_ref, hh, bias_ref.at[hh])
        else:
            fill_bias_st(m_ref, hh, bias_ref.at[hh])
    own = lane_mask(chunk, 0)
    for n in range(n_win):
        key = k_ref[n * n_query : n * n_query + n_key, :]
        val = v_ref[n * n_query : n * n_query + n_key, :]
        ok = ok_ref[n] > 0.0
        for c in range(n_query // chunk):
            rows = slice(n * n_query + c * chunk, n * n_query + (c + 1) * chunk)
            query = q_ref[rows, :]
            query = query * jnp.asarray(0.125, BF16)
            outs = []
            for hh in range(2):
                mine = own if hh == 0 else jnp.logical_not(own)
                picked = jnp.where(mine, query, jnp.zeros_like(query))
                scores = dot_nt(picked, key) + bias_ref[hh, c * chunk : (c + 1) * chunk, :]
                scores = jnp.where(ok, scores, NEG_FILL)
                top = jnp.max(scores, axis=-1, keepdims=True)
                expo = jnp.exp(scores - top)
                probs = (expo * (1.0 / jnp.sum(expo, axis=-1, keepdims=True))).astype(BF16)
                p_ref[hh, n, c * chunk : (c + 1) * chunk, :] = probs
                outs.append(dot_nn(probs, val))
            att_ref[rows, :] = jnp.where(own, outs[0], outs[1]).astype(BF16)


def attend_backward(
    spatial, n_win, n_query, n_key, chunk, head, q_ref, k_ref, v_ref, do_ref, p_ref, g_ref, dm_ref, db_ref
):
    width = g_ref.shape[1] // 3
    own = lane_mask(chunk, 0)
    own_k = lane_mask(n_key, 0)

    def store(rows, which, values):
        g_ref[rows, pl.ds(pl.multiple_of(which * width + head * 128, 128), 128)] = values

    db_ref[...] = jnp.zeros_like(db_ref)
    for n in range(n_win):
        keys = slice(n * n_query, n * n_query + n_key)
        key = k_ref[keys, :]
        val = v_ref[keys, :]
        gk = [None, None]
        gv = [None, None]
        for c in range(n_query // chunk):
            rows = slice(n * n_query + c * chunk, n * n_query + (c + 1) * chunk)
            part = slice(c * chunk, (c + 1) * chunk)
            query = q_ref[rows, :]
            gout = do_ref[rows, :]
            gq = []
            for hh in range(2):
                mine = own if hh == 0 else jnp.logical_not(own)
                probs = p_ref[hh, n, part, :]
                gsel = jnp.where(mine, gout, jnp.zeros_like(gout))
                dprob = dot_nt(gsel, val)
                soft = probs.astype(F32)
                delta = jnp.sum(soft * dprob, axis=-1, keepdims=True)
                dscore = (soft * (dprob - delta)).astype(BF16)
                db_ref[hh, part, :] += dscore.astype(F32)
                gq.append(dot_nn(dscore, key))
                dk = dot_tn(dscore, query)
                dv = dot_tn(probs, gout)
                gk[hh] = dk if gk[hh] is None else gk[hh] + dk
                gv[hh] = dv if gv[hh] is None else gv[hh] + dv
            store(rows, 0, (jnp.where(own, gq[0], gq[1]) * 0.125).astype(BF16))
        store(keys, 1, (jnp.where(own_k, gk[0], gk[1]) * 0.125).astype(BF16))
        store(keys, 2, jnp.where(own_k, gv[0], gv[1]).astype(BF16))
        if n_key < n_query:
            rest = slice(n * n_query + n_key, (n + 1) * n_query)
            empty = jnp.zeros((n_query - n_key, 128), BF16)
            store(rest, 1, empty)
            store(rest, 2, empty)
    for hh in range(2):
        if spatial:
            fold_bias_sp(db_ref.at[hh], dm_ref, hh)
        else:
            fold_bias_st(db_ref.at[hh], dm_ref, hh)


def attention_shapes(spatial, tokens):
    n_query = SWIN * SWIN if spatial else FRAMES * TWIN * TWIN
    n_key = n_query if spatial else KEYF * TWIN * TWIN
    return tokens // n_query, n_query, n_key, n_query


ROWS = 64
COLS = 1024
MESH = pl.DeviceIdType.MESH


def place(n_clip):
    clip = lax.axis_index("clip")
    x = lax.axis_index("frame")
    z = clip // 4
    y = lax.rem(clip // 2, 2)
    c = lax.rem(clip, 2)
    return clip, z, y, c, x


def remote(src, dst, send, recv, clip, frame):
    return pltpu.make_async_remote_copy(
        src_ref=src,
        dst_ref=dst,
        send_sem=send,
        recv_sem=recv,
        device_id={"clip": clip, "frame": frame},
        device_id_type=MESH,
    )


def greet(targets):
    barrier = pltpu.get_barrier_semaphore()
    count = 0
    for clip, frame, valid in targets:
        if valid is None:
            pl.semaphore_signal(barrier, inc=1, device_id={"clip": clip, "frame": frame}, device_id_type=MESH)
            count = count + 1
        else:
            @pl.when(valid)
            def _():
                pl.semaphore_signal(barrier, inc=1, device_id={"clip": clip, "frame": frame}, device_id_type=MESH)
            count = count + valid.astype(jnp.int32)
    pl.semaphore_wait(barrier, count)


GATHER_TAIL = 6


def gather_tick(t, n, nz, where, shard, full, local, up_s, up_r, dn_s, dn_r, y_s, y_r, x_s, x_r, c_s, c_r):
    clip, z, y, c, x = where
    last = nz - 1
    steps = nz - 1

    def phases(i, hi):
        lo = COLS - hi
        fetch = pl.ds(pl.multiple_of(x * lo, 128), hi)
        give = pl.ds(pl.multiple_of(x * hi, 128), lo)

        def own():
            return pltpu.make_async_copy(
                shard.at[i, :, fetch], full.at[i, z, y, c, :, fetch], local.at[i]
            )

        def up(s, origin):
            src = shard.at[i, :, fetch] if s == 0 else full.at[i, origin, y, c, :, fetch]
            return remote(src, full.at[i, origin, y, c, :, fetch], up_s.at[s, i], up_r.at[s, i], clip + 4, x)

        def down(s, origin):
            src = shard.at[i, :, fetch] if s == 0 else full.at[i, origin, y, c, :, fetch]
            return remote(src, full.at[i, origin, y, c, :, fetch], dn_s.at[s, i], dn_r.at[s, i], clip - 4, x)

        def over_y():
            src = full.at[i, :, y, c, :, fetch]
            return remote(src, src, y_s.at[i], y_r.at[i], clip + 2 - 4 * y, x)

        def over_x():
            src = full.at[i, :, :, c, :, give]
            return remote(src, src, x_s.at[i], x_r.at[i], clip, 1 - x)

        def over_c():
            src = full.at[i, :, :, c]
            return remote(src, src, c_s.at[i], c_r.at[i], clip + 1 - 2 * c, x)

        def z_wait(s):
            @pl.when(z - 1 - s >= 0)
            def _():
                up(s, z - 1 - s).wait_recv()

            @pl.when(z + 1 + s <= last)
            def _():
                down(s, z + 1 + s).wait_recv()

        def z_start(s):
            @pl.when(jnp.logical_and(z < last, z - s >= 0))
            def _():
                up(s, z - s).start()

            @pl.when(jnp.logical_and(z > 0, z + s <= last))
            def _():
                down(s, z + s).start()

        def z_sent(s):
            @pl.when(jnp.logical_and(z < last, z - s >= 0))
            def _():
                up(s, z - s).wait_send()

            @pl.when(jnp.logical_and(z > 0, z + s <= last))
            def _():
                down(s, z + s).wait_send()

        def first():
            own().start()
            z_start(0)

        def along(s):
            z_wait(s - 1)
            z_start(s)

        def to_y():
            z_wait(steps - 1)
            own().wait()
            over_y().start()

        def to_x():
            over_y().wait_recv()
            over_x().start()

        def to_c():
            over_x().wait_recv()
            over_c().start()

        def finish():
            over_c().wait_recv()
            for s in range(steps):
                z_sent(s)
            over_y().wait_send()
            over_x().wait_send()
            over_c().wait_send()

        mids = [functools.partial(along, s) for s in range(1, steps)]
        return [first] + mids + [to_y, to_x, to_c, finish]

    for k in range(steps + 4):
        i = t - k
        valid = jnp.logical_and(i >= 0, i < n)
        third = lax.rem(i + 3, 3) == 2
        for hi, chosen in ((640, jnp.logical_not(third)), (768, third)):
            @pl.when(jnp.logical_and(valid, chosen))
            def _(i=i, hi=hi, k=k):
                phases(i, hi)[k]()


def greet_gather(nz, where):
    clip, z, y, c, x = where
    greet([
        (clip + 4, x, z < nz - 1),
        (clip - 4, x, z > 0),
        (clip + 2 - 4 * y, x, None),
        (clip, 1 - x, None),
        (clip + 1 - 2 * c, x, None),
    ])


def gather_sems(n, nz):
    dma = pltpu.SemaphoreType.DMA
    z = dma((nz - 1, n))
    one = dma((n,))
    return [one, z, z, z, z, one, one, one, one, one, one]


NBUF = 3
REDUCE_TAIL = 7
Y_FIRST = 640
NACC = 4


def reduce_tick(t, n, nz, where, sources, out, acc, cbuf, ya, xa, yb, xb, tb, zb, sb, fb, ob,
                loc, c_s, c_r, ya_s, ya_r, xa_s, xa_r, yb_s, yb_r, xb_s, xb_r, z_s, z_r, f_s, f_r, o_s,
                cred_c, cred_y, cred_x, cred_z, cred_f):
    clip, z, y, c, x = where
    half = ROWS // 2
    peer_c = clip + 1 - 2 * c
    peer_y = clip + 2 - 4 * y
    mine = pl.ds(pl.multiple_of(x * half, half), half)
    theirs = pl.ds(pl.multiple_of((1 - x) * half, half), half)
    left = pl.ds(0, Y_FIRST)
    right = pl.ds(Y_FIRST, COLS - Y_FIRST)

    def slot(i):
        return lax.rem(i, NBUF)

    def aslot(i):
        return lax.rem(i, NACC)

    def load(i, source, first):
        return pltpu.make_async_copy(source.at[i - first, :, :, c], acc.at[aslot(i)], loc.at[slot(i)])

    def over_c(i, source, first):
        src = source.at[i - first, :, :, 1 - c]
        return remote(src, cbuf.at[slot(i)], c_s.at[slot(i)], c_r.at[slot(i)], peer_c, x)

    def over_ya(i):
        return remote(acc.at[aslot(i), :, 1 - y, :, left], ya.at[slot(i)], ya_s.at[slot(i)], ya_r.at[slot(i)], peer_y, x)

    def over_xa(i):
        return remote(acc.at[aslot(i), :, :, theirs, right], xa.at[slot(i)], xa_s.at[slot(i)], xa_r.at[slot(i)], clip, 1 - x)

    def over_xb(i):
        return remote(acc.at[aslot(i), :, y, theirs, left], xb.at[slot(i)], xb_s.at[slot(i)], xb_r.at[slot(i)], clip, 1 - x)

    def over_yb(i):
        return remote(acc.at[aslot(i), :, 1 - y, mine, right], yb.at[slot(i)], yb_s.at[slot(i)], yb_r.at[slot(i)], peer_y, x)

    def over_z(i, k):
        to = lax.rem(z + k, nz)
        return remote(tb.at[slot(i), to], zb.at[slot(i), k - 1], z_s.at[slot(i), k - 1], z_r.at[slot(i), k - 1],
                      clip + 4 * (to - z), x)

    def over_f(i):
        return remote(sb.at[slot(i)], fb.at[slot(i)], f_s.at[slot(i)], f_r.at[slot(i)], clip, 1 - x)

    def write(i):
        return pltpu.make_async_copy(ob.at[slot(i)], out.at[i], o_s.at[slot(i)])

    def credit(sem, who, frame, i):
        @pl.when(i + NBUF < n)
        def _():
            pl.semaphore_signal(sem, inc=1, device_id={"clip": who, "frame": frame}, device_id_type=MESH)

    def need(sem, i):
        @pl.when(i >= NBUF)
        def _():
            pl.semaphore_wait(sem, 1)

    def item(i):
        return jnp.logical_and(i >= 0, i < n)

    i = t - 6

    @pl.when(item(i))
    def _(i=i):
        write(i).wait()

    i = t

    @pl.when(item(i))
    def _(i=i):
        need(cred_c, i)
        first = 0
        for source, skip, count in sources:

            @pl.when(jnp.logical_and(i >= first, i < first + count))
            def _(source=source, offset=first - skip):
                over_c(i, source, offset).start()
                load(i, source, offset).start()

            first += count

    i = t - 1

    @pl.when(item(i))
    def _(i=i):
        over_c(i, sources[0][0], i).wait()
        load(i, sources[0][0], i).wait()
        a, b = aslot(i), slot(i)

        def body(k, carry):
            acc[a, k] = acc[a, k] + cbuf[b, k]
            return carry

        lax.fori_loop(0, nz, body, 0)
        credit(cred_c, peer_c, x, i)
        need(cred_y, i)
        need(cred_x, i)
        over_ya(i).start()
        over_xa(i).start()

    i = t - 2

    @pl.when(item(i))
    def _(i=i):
        over_ya(i).wait()
        over_xa(i).wait()
        a, b = aslot(i), slot(i)

        def body(k, carry):
            acc[a, k, y, :, left] = acc[a, k, y, :, left] + ya[b, k]
            acc[a, k, :, mine, right] = acc[a, k, :, mine, right] + xa[b, k]
            return carry

        lax.fori_loop(0, nz, body, 0)
        over_xb(i).start()
        over_yb(i).start()

    i = t - 3

    @pl.when(item(i))
    def _(i=i):
        over_xb(i).wait()
        over_yb(i).wait()
        a, b = aslot(i), slot(i)

        def body(k, carry):
            tb[b, k, :, left] = acc[a, k, y, mine, left] + xb[b, k]
            tb[b, k, :, right] = acc[a, k, y, mine, right] + yb[b, k]
            return carry

        lax.fori_loop(0, nz, body, 0)
        credit(cred_y, peer_y, x, i)
        credit(cred_x, clip, 1 - x, i)
        for k in range(1, nz):
            need(cred_z.at[k - 1], i)
            over_z(i, k).start()

    i = t - 4

    @pl.when(item(i))
    def _(i=i):
        for k in range(1, nz):
            over_z(i, k).wait()
        b = slot(i)
        total = tb[b, z].astype(F32)
        for k in range(1, nz):
            total = total + zb[b, k - 1].astype(F32)
        sb[b] = total.astype(BF16)
        for k in range(1, nz):
            sender = lax.rem(z + nz - k, nz)
            credit(cred_z.at[k - 1], clip + 4 * (sender - z), x, i)
        need(cred_f, i)
        over_f(i).start()

    i = t - 5

    @pl.when(item(i))
    def _(i=i):
        over_f(i).wait()
        b = slot(i)
        ob[b, mine, :] = sb[b].astype(F32)
        ob[b, theirs, :] = fb[b].astype(F32)
        credit(cred_f, clip, 1 - x, i)
        write(i).start()


def greet_reduce(nz, where):
    clip, z, y, c, x = where
    others = [(clip + 4 * (lax.rem(z + k, nz) - z), x, None) for k in range(1, nz)]
    greet(others + [
        (clip + 2 - 4 * y, x, None),
        (clip, 1 - x, None),
        (clip + 1 - 2 * c, x, None),
    ])


def exchange_tick(t, nz, where, small, totals, boxes, mod_box, sems):
    clip, z, y, c, x = where
    steps = [(clip, 1 - x), (clip + 1 - 2 * c, x), (clip + 2 - 4 * y, x)]
    bit = 1
    while bit < nz:
        flip = lax.rem(z // bit, 2)
        steps.append((clip + 4 * bit * (1 - 2 * flip), x))
        bit *= 2

    def copies(k):
        to, frame = steps[k]
        found = [
            remote(boxes[j].at[k, 0], boxes[j].at[k, 1], sems.at[j, 0, k], sems.at[j, 1, k], to, frame)
            for j in range(2)
        ]
        if k == 0:
            found.append(remote(small[0], mod_box, sems.at[2, 0, 0], sems.at[2, 1, 0], to, frame))
        return found

    for k in range(len(steps)):
        @pl.when(t == k + 1)
        def _(k=k):
            for copy in copies(k):
                copy.wait()
            for j in range(2):
                totals[1 + j][...] = boxes[j][k, 0].astype(F32) + boxes[j][k, 1].astype(F32)
            if k == 0:
                totals[0][...] = small[0][...] + mod_box[...]

        @pl.when(t == k)
        def _(k=k):
            for j in range(2):
                source = small[1 + j] if k == 0 else totals[1 + j]
                boxes[j][k, 0] = source[...].astype(BF16)
            for copy in copies(k):
                copy.start()


def exchange_steps(nz):
    return 3 + (nz - 1).bit_length()


def reduce_kernel(pick, nz, grads, small0, small1, small2, out, total0, total1, total2, *rest):
    n_comm = len(reduce_scratch(nz))
    comm, (box0, box1, mod_box, sems) = rest[:n_comm], rest[n_comm:]
    skip, n = pick
    where = place(4 * nz)
    clip, z, y, c, x = where
    greet_reduce(nz, where)

    def step(t, carry):
        exchange_tick(
            t, nz, where, (small0, small1, small2), (total0, total1, total2), (box0, box1), mod_box, sems
        )
        reduce_tick(t, n, nz, where, [(grads, skip, n)], out, *comm)
        return carry

    lax.fori_loop(0, n + REDUCE_TAIL, step, 0)


def reduce_scratch(nz):
    half = ROWS // 2
    rest = COLS - Y_FIRST
    dma = pltpu.SemaphoreType.DMA
    one = dma((NBUF,))
    regular = pltpu.SemaphoreType.REGULAR
    return [
        pltpu.VMEM((NACC, nz, 2, ROWS, COLS), BF16),
        pltpu.VMEM((NBUF, nz, 2, ROWS, COLS), BF16),
        pltpu.VMEM((NBUF, nz, ROWS, Y_FIRST), BF16),
        pltpu.VMEM((NBUF, nz, 2, half, rest), BF16),
        pltpu.VMEM((NBUF, nz, half, rest), BF16),
        pltpu.VMEM((NBUF, nz, half, Y_FIRST), BF16),
        pltpu.VMEM((NBUF, nz, half, COLS), BF16),
        pltpu.VMEM((NBUF, nz - 1, half, COLS), BF16),
        pltpu.VMEM((NBUF, half, COLS), BF16),
        pltpu.VMEM((NBUF, half, COLS), BF16),
        pltpu.VMEM((NBUF, ROWS, COLS), F32),
        one, one, one, one, one, one, one, one, one, one, one,
        dma((NBUF, nz - 1)), dma((NBUF, nz - 1)),
        one, one, one,
        regular, regular, regular, regular((nz - 1,)), regular,
    ]


def reduce_last(grads, pick, small, nz, cid):
    n = pick[1]
    steps = exchange_steps(nz)
    vmem = pl.BlockSpec(memory_space=pltpu.VMEM)
    return pl.pallas_call(
        functools.partial(reduce_kernel, pick, nz),
        out_shape=[jax.ShapeDtypeStruct((n, ROWS, COLS), F32)]
        + [jax.ShapeDtypeStruct(v.shape, F32) for v in small],
        in_specs=[pl.BlockSpec(memory_space=pl.ANY), vmem, vmem, vmem],
        out_specs=[pl.BlockSpec(memory_space=pl.ANY), vmem, vmem, vmem],
        scratch_shapes=reduce_scratch(nz)
        + [pltpu.VMEM((steps, 2) + v.shape, BF16) for v in small[1:]]
        + [pltpu.VMEM(small[0].shape, F32), pltpu.SemaphoreType.DMA((3, 2, steps))],
        compiler_params=pltpu.CompilerParams(
            collective_id=cid, has_side_effects=True, vmem_limit_bytes=48 * 1024 * 1024
        ),
        name="reduce_last",
    )(grads, *small)


CHUNK = 512
STEP_ROWS = 128
MIB = 1024 * 1024
GELU_C = 0.7978845608028654
GELU_A = 0.044715


def fixed(shape, **kw):
    zeros = (0,) * len(shape)
    return pl.BlockSpec(shape, lambda i: zeros, pipeline_mode=pl.Buffered(1), **kw)


def over_rows(tokens, body):
    def step(k, carry):
        body(pl.ds(pl.multiple_of(k * STEP_ROWS, STEP_ROWS), STEP_ROWS))
        return carry

    lax.fori_loop(0, tokens // STEP_ROWS, step, 0)


def down_rows(w_ref):
    groups = w_ref.shape[1] // ROWS
    return jnp.concatenate(
        [w_ref[s, c * ROWS : (c + 1) * ROWS, :] for c in range(groups) for s in range(2)], axis=0
    )


FRONT_ROWS = 256
GATHER_US = 8.5


def forward_plan(tokens, width):
    rows = tokens // FRONT_ROWS
    sizes = (rows, 3, width // 128, 1, rows, 4, rows)
    starts = [0]
    for size in sizes:
        starts.append(starts[-1] + size)
    return starts


def plan_gather(starts, spatial, need, n_items, nz):
    takes = (1.0, 2.6, 1.9 if spatial else 3.6, 2.2, 1.3, 6.5, 0.8)
    total = n_items + nz + 2
    counts, done, clock, last = [], 0, 0.0, -GATHER_US
    for section, (lo, hi) in enumerate(zip(starts, starts[1:])):
        for step in range(lo, hi):
            before = done
            while done < total and (done < need.get(step, 0) or clock - last >= GATHER_US):
                early = 4.0 if done < 7 else GATHER_US
                clock = max(clock, last + early)
                last = clock
                done += 1
            counts.append(done - before)
            clock += takes[section]
    return counts, total


def forward_body(
    spatial, shapes, n_own, own_first, counts, total, nz,
    s_ref, m_ref, b_ref, ok_ref, shard_hbm, prev_hbm,
    na_ref, qkv_ref, att_ref, p_ref, proj_ref, mid_ref, nm_ref, act_ref, dact_ref, down_ref, res_ref, full_hbm,
    n_scr, q_scr, a_scr, acc_ref, mid_scr, bias_ref, w_scr, d_scr, w_sem, d_sem, *sems,
):
    n_win, n_query, n_key, chunk = shapes
    tokens, width = acc_ref.shape
    starts = forward_plan(tokens, width)
    a0, a1, a2, a3, a4, a5, a6, end = starts
    step = pl.program_id(0)
    where = place(4 * nz)

    @pl.when(step == 0)
    def _():
        greet_gather(nz, where)

    lo = jnp.zeros((), jnp.int32)
    hi = jnp.zeros((), jnp.int32)
    for s, count in enumerate(counts):
        if count:
            lo = lo + count * (step > s).astype(jnp.int32)
            hi = hi + count * (step >= s).astype(jnp.int32)

    def tick(t, carry):
        gather_tick(t, n_own, nz, where, shard_hbm, full_hbm, *sems)
        return carry

    lax.fori_loop(lo, hi, tick, 0)

    def item_ref(item):
        if item >= own_first:
            return full_hbm.at[item - own_first]
        return prev_hbm.at[PREV_ITEMS + item]

    ready = []
    done = 0
    for count in counts:
        done += count
        ready.append(done)

    def start_of(item, use):
        if item < own_first:
            return max(use - 1, 0)
        for s in range(max(use - 1, 0), use + 1):
            if ready[s] >= item - own_first + nz + 3:
                return s
        raise ValueError("late item")

    jobs = []
    uses = [(a1, 0), (a1 + 1, 1), (a1 + 2, 2), (a3, 3)] + [(a5 + i, UP_ITEMS[i]) for i in range(4)]
    for k, (use, item) in enumerate(uses):
        copy = pltpu.make_async_copy(item_ref(item), w_scr.at[k % 2], w_sem.at[k % 2])
        jobs.append((start_of(item, use), use, copy))
    for i in range(4):
        items = (DOWN_ITEMS[2 * (i // 2)], DOWN_ITEMS[2 * (i // 2) + 1])
        first = max(start_of(item, a5 + i) for item in items)
        for k, item in enumerate(items):
            source = item_ref(item).at[pl.ds((nz // 2) * (i % 2), nz // 2)]
            copy = pltpu.make_async_copy(source, d_scr.at[i % 2, k], d_sem.at[i % 2, k])
            jobs.append((first, a5 + i, copy))
    for first, use, copy in jobs:
        @pl.when(step == first)
        def _(copy=copy):
            copy.start()
    for first, use, copy in jobs:
        @pl.when(step == use)
        def _(copy=copy):
            copy.wait()

    def weight(k):
        return w_scr[k].reshape(width, width)

    def rows_at(i):
        return pl.ds(pl.multiple_of(i * FRONT_ROWS, FRONT_ROWS), FRONT_ROWS)

    @pl.when(step < a1)
    def _():
        normed, _ = norm_stats(s_ref[...].astype(F32))
        value = (normed * (1.0 + m_ref[1:2, :]) + m_ref[0:1, :]).astype(BF16)
        n_scr[rows_at(step), :] = value
        na_ref[...] = value

    @pl.when(jnp.logical_and(step >= a1, step < a2))
    def _():
        i = step - a1
        value = dot_nn(n_scr[...], weight(lax.rem(i, 2))).astype(BF16)
        q_scr[:, pl.ds(pl.multiple_of(i * width, width), width)] = value
        qkv_ref[...] = value

    @pl.when(jnp.logical_and(step >= a2, step < a3))
    def _():
        def lanes(k):
            return q_scr.at[:, pl.ds(pl.multiple_of(k * width + (step - a2) * 128, 128), 128)]

        attend_forward(
            spatial, n_win, n_query, n_key, chunk, lanes(0), lanes(1), lanes(2), b_ref, ok_ref, att_ref, p_ref, bias_ref
        )
        a_scr[:, pl.ds(pl.multiple_of((step - a2) * 128, 128), 128)] = att_ref[...]

    @pl.when(step == a3)
    def _():
        acc_ref[...] = dot_nn(a_scr[...], weight(1))

    @pl.when(jnp.logical_and(step >= a4, step < a5))
    def _():
        rows = rows_at(step - a4)
        proj = acc_ref[rows, :]
        proj_ref[...] = proj.astype(BF16)
        mid = s_ref[...].astype(F32) + m_ref[2:3, :] * proj
        mid_ref[...] = mid
        mid_scr[rows, :] = mid
        normed, _ = norm_stats(mid)
        value = (normed * (1.0 + m_ref[4:5, :]) + m_ref[3:4, :]).astype(BF16)
        n_scr[rows, :] = value
        nm_ref[...] = value

    @pl.when(jnp.logical_and(step >= a5, step < a6))
    def _():
        i = step - a5
        slot = lax.rem(i, 2)
        w_up = weight(slot)
        first = d_scr[slot, 0].reshape(-1, ROWS, width)
        second = d_scr[slot, 1].reshape(-1, ROWS, width)
        w_down = jnp.concatenate(
            [part for k in range(first.shape[0]) for part in (first[k], second[k])], axis=0
        )
        pieces = 4
        each = tokens // pieces
        ups = [dot_nn(n_scr[k * each : (k + 1) * each, :], w_up) for k in range(pieces)]
        for k in range(pieces):
            rows = slice(k * each, (k + 1) * each)
            up = ups[k]
            square = up * up
            tanh = jnp.tanh(up * (GELU_C + (GELU_C * GELU_A) * square))
            half = 0.5 + 0.5 * tanh
            act = up * half
            dact_ref[rows, :] = (
                half + act * (1.0 - tanh) * (GELU_C + (3.0 * GELU_C * GELU_A) * square)
            ).astype(BF16)
            act = act.astype(BF16)
            act_ref[rows, :] = act
            acc_ref[rows, :] = jnp.where(i == 0, 0.0, acc_ref[rows, :]) + dot_nn(act, w_down)

    @pl.when(step >= a6)
    def _():
        rows = rows_at(step - a6)
        down = acc_ref[rows, :]
        down_ref[...] = down.astype(BF16)
        res_ref[...] = (mid_scr[rows, :] + m_ref[5:6, :] * down).astype(res_ref.dtype)

    @pl.when(step == end - 1)
    def _():
        lax.fori_loop(sum(counts), total, tick, 0)


DOWN_ITEMS = (4, 5, 8, 9)
UP_ITEMS = (6, 7, 10, 11)
PREV_ITEMS = 12


def block_forward(stream, mods, shard, prev, own_first, spread, key_ok, spatial, result_type, nz, cid):
    tokens, width = stream.shape
    shapes = attention_shapes(spatial, tokens)
    n_win, n_query, n_key, _ = shapes
    pairs = width // 128
    a0, a1, a2, a3, a4, a5, a6, end = starts = forward_plan(tokens, width)
    n_own = shard.shape[0]
    tail = spread.shape[1:]
    zeros = (0,) * len(tail)
    need = {}
    for i in range(3):
        need[a1 + i] = i
    need[a3] = 3
    for i in range(4):
        need[a5 + i] = max(UP_ITEMS[i], DOWN_ITEMS[2 * (i // 2) + 1])
    need = {s: item - own_first + nz + 3 for s, item in need.items() if item >= own_first}
    counts, total = plan_gather(starts, spatial, need, n_own, nz)

    def at(start, stop):
        return lambda i: jnp.clip(i - start, 0, stop - start - 1)

    def row_block(place_of):
        return pl.BlockSpec((FRONT_ROWS, width), lambda i: (place_of(i), 0))

    def s_at(i):
        return jnp.where(i < a1, i, at(a4, a5)(i))

    heads = at(a2, a3)
    anywhere = pl.BlockSpec(memory_space=pl.ANY)
    hidden = pl.BlockSpec((tokens, width), lambda i: (0, at(a5, a6)(i)))
    body = functools.partial(forward_body, spatial, shapes, n_own, own_first, counts, total, nz)
    extra = [] if prev is None else [prev]
    if prev is None:
        whole = body

        def body(*refs):
            return whole(*refs[:5], None, *refs[5:])

    dma = pltpu.SemaphoreType.DMA
    bf16_rows = jax.ShapeDtypeStruct((tokens, width), BF16)
    outs = pl.pallas_call(
        body,
        grid=(end,),
        in_specs=[
            row_block(s_at),
            fixed(mods.shape),
            pl.BlockSpec((2,) + tail, lambda i: (heads(i),) + zeros),
            pl.BlockSpec((n_win, 1, n_key), lambda i: (0, 0, 0)),
            anywhere,
        ] + [anywhere] * len(extra),
        out_specs=[
            row_block(at(a0, a1)),
            pl.BlockSpec((tokens, width), lambda i: (0, at(a1, a2)(i))),
            pl.BlockSpec((tokens, 128), lambda i: (0, heads(i))),
            pl.BlockSpec((2, n_win, n_query, n_key), lambda i: (heads(i), 0, 0, 0)),
            row_block(at(a4, a5)),
            row_block(at(a4, a5)),
            row_block(at(a4, a5)),
            hidden,
            hidden,
            row_block(at(a6, end)),
            row_block(at(a6, end)),
            anywhere,
        ],
        out_shape=[
            bf16_rows,
            jax.ShapeDtypeStruct((tokens, 3 * width), BF16),
            bf16_rows,
            jax.ShapeDtypeStruct((2 * pairs, n_win, n_query, n_key), BF16),
            bf16_rows,
            jax.ShapeDtypeStruct((tokens, width), F32),
            bf16_rows,
            jax.ShapeDtypeStruct((tokens, 4 * width), BF16),
            jax.ShapeDtypeStruct((tokens, 4 * width), BF16),
            bf16_rows,
            jax.ShapeDtypeStruct((tokens, width), result_type),
            jax.ShapeDtypeStruct((n_own, nz, 2, 2, ROWS, COLS), BF16),
        ],
        scratch_shapes=[
            pltpu.VMEM((tokens, width), BF16),
            pltpu.VMEM((tokens, 3 * width), BF16),
            pltpu.VMEM((tokens, width), BF16),
            pltpu.VMEM((tokens, width), F32),
            pltpu.VMEM((tokens, width), F32),
            pltpu.VMEM((2, n_query, n_key), F32),
            pltpu.VMEM((2, nz, 2, 2, ROWS, COLS), BF16),
            pltpu.VMEM((2, 2, nz // 2, 2, 2, ROWS, COLS), BF16),
            dma((2,)),
            dma((2, 2)),
        ] + gather_sems(n_own, nz),
        compiler_params=pltpu.CompilerParams(
            collective_id=cid, has_side_effects=True, vmem_limit_bytes=64 * MIB
        ),
        name="block_forward",
    )(stream, mods, spread, key_ok, shard, *extra)
    normed_a, qkv, att, probs, proj, mid, normed_m, act, dact, down, result, full = outs
    return result, (stream, normed_a, qkv, probs, att, proj, mid, normed_m, act, dact, down), full


def norm_back_rows(values, scale_row, grad):
    normed, inv = norm_stats(values)
    u = grad * (1.0 + scale_row)
    out = (
        u
        - jnp.mean(u, axis=-1, keepdims=True)
        - normed * jnp.mean(u * normed, axis=-1, keepdims=True)
    ) * inv
    return out, jnp.sum(grad, axis=0, keepdims=True), jnp.sum(grad * normed, axis=0, keepdims=True)


BLOCK_ROWS = 128
TICK_US = 8.0


def backward_plan(tokens, width):
    rows = tokens // BLOCK_ROWS
    chunks = 4 * width // CHUNK
    halves = width // CHUNK
    pairs = width // 128
    sizes = (rows, chunks, rows, halves, pairs, 3 * halves, rows)
    starts = [0]
    for size in sizes:
        starts.append(starts[-1] + size)
    return starts


def backward_body(
    spatial, shapes, n_prev, n_own, tick_steps, nz,
    g_ref, down_ref, mid_ref, proj_ref, s_ref, m_ref, act_ref, dact_ref, w_ref, up_ref, dn_ref,
    q_ref, k_ref, v_ref, p_ref, nm_hbm, att_hbm, na_hbm, prev_hbm,
    out_ref, dm_ref, rows_ref, grads_hbm, share_hbm,
    res_ref, gv_ref, e_ref, gm_ref, ga_ref, gq_ref, db_ref, gdb_ref, gub_ref,
    res_sem, gd_sem, gu_sem, *comm,
):
    n_win, n_query, n_key, chunk = shapes
    tokens, width = e_ref.shape
    starts = backward_plan(tokens, width)
    a0, a1, a2, a3, a4, a5, a6, end = starts
    halves = width // CHUNK
    step = pl.program_id(0)
    where = place(4 * nz)
    n_items = n_prev + n_own
    sources = []
    if n_prev:
        sources.append((prev_hbm, 8, n_prev))
    sources.append((grads_hbm, 0, n_own))

    @pl.when(step == 0)
    def _():
        greet_reduce(nz, where)

    def tick(t):
        reduce_tick(t, n_items, nz, where, sources, share_hbm, *comm)

    due = jnp.zeros((), jnp.bool_)
    passed = jnp.zeros((), jnp.int32)
    for s in tick_steps:
        due = jnp.logical_or(due, step == s)
        passed = passed + (step > s).astype(jnp.int32)

    def resident(source):
        return pltpu.make_async_copy(source, res_ref, res_sem)

    def put_down(i):
        slot = lax.rem(i, 2)
        target = grads_hbm.at[pl.ds(4 * (i // 4) + 2, 2), pl.ds(lax.rem(i, 4), 1)]
        return pltpu.make_async_copy(gdb_ref.at[slot], target, gd_sem.at[slot])

    def put_cols(i, item, half):
        slot = lax.rem(i, 2)
        cols = pl.ds(pl.multiple_of(half * CHUNK, CHUNK), CHUNK)
        target = grads_hbm.at[item, :, :, :, :, cols]
        return pltpu.make_async_copy(gub_ref.at[slot], target, gu_sem.at[slot])

    def keep_cols(i, values):
        gub_ref[lax.rem(i, 2)] = values.reshape(gub_ref.shape[1:])

    def rows_at(i):
        return pl.ds(pl.multiple_of(i * BLOCK_ROWS, BLOCK_ROWS), BLOCK_ROWS)

    def add_e(first, left, right):
        part = tokens // 2
        for k in range(2):
            rows = slice(k * part, (k + 1) * part)
            value = dot_nt(left[rows], right)

            @pl.when(first)
            def _(rows=rows, value=value):
                e_ref[rows, :] = value

            @pl.when(jnp.logical_not(first))
            def _(rows=rows, value=value):
                e_ref[rows, :] += value

    @pl.when(step == 0)
    def _():
        resident(nm_hbm).start()
        rows_ref[...] = jnp.zeros_like(rows_ref)

    @pl.when(step < a1)
    def _():
        grad = g_ref[...].astype(F32)
        gv_ref[rows_at(step), :] = (m_ref[5:6, :] * grad).astype(BF16)
        rows_ref[5:6, :] += jnp.sum(grad * down_ref[...].astype(F32), axis=0, keepdims=True)

    @pl.when(step == a1)
    def _():
        resident(nm_hbm).wait()

    @pl.when(jnp.logical_and(step >= a1, step < a2))
    def _():
        i = step - a1

        @pl.when(i >= 2)
        def _():
            put_down(i).wait()
            put_cols(i, 4, 0).wait()

        gdv = gv_ref[...]
        grad_act = dot_nt(gdv, down_rows(dn_ref))
        gup = (grad_act * dact_ref[...].astype(F32)).astype(BF16)
        slot = lax.rem(i, 2)
        grad_down = dot_tn(act_ref[...], gdv).astype(BF16)
        for k in range(CHUNK // ROWS):
            gdb_ref[slot, k % 2, 0, k // 4, (k // 2) % 2] = grad_down[k * ROWS : (k + 1) * ROWS, :]
        put_down(i).start()
        keep_cols(i, dot_tn(res_ref[...], gup).astype(BF16))
        put_cols(i, 4 * (i // 4) + lax.rem(i // 2, 2), lax.rem(i, halves)).start()
        add_e(i == 0, gup, up_ref[0])

    @pl.when(step == a2)
    def _():
        resident(att_hbm).start()
        for k in range(2):
            put_down(k).wait()
            put_cols(k, 4, 0).wait()

    @pl.when(jnp.logical_and(step >= a2, step < a3))
    def _():
        rows = rows_at(step - a2)
        out, shift, scale = norm_back_rows(mid_ref[...], m_ref[4:5, :], e_ref[rows, :])
        grad_mid = out + g_ref[...].astype(F32)
        gm_ref[rows, :] = grad_mid
        gv_ref[rows, :] = (m_ref[2:3, :] * grad_mid).astype(BF16)
        rows_ref[3:4, :] += shift
        rows_ref[4:5, :] += scale
        rows_ref[2:3, :] += jnp.sum(grad_mid * proj_ref[...].astype(F32), axis=0, keepdims=True)

    @pl.when(step == a3)
    def _():
        resident(att_hbm).wait()

    @pl.when(jnp.logical_and(step >= a3, step < a4))
    def _():
        i = step - a3
        part = gv_ref[:, pl.ds(pl.multiple_of(i * CHUNK, CHUNK), CHUNK)]
        keep_cols(i, dot_tn(res_ref[...], part).astype(BF16))
        put_cols(i, 8, i).start()
        add_e(i == 0, part, w_ref[0])

    @pl.when(step == a4)
    def _():
        resident(na_hbm).start()
        ga_ref[...] = e_ref[...].astype(BF16)

    @pl.when(jnp.logical_and(step >= a4, step < a5))
    def _():
        head = step - a4
        lanes = pl.ds(pl.multiple_of(head * 128, 128), 128)
        attend_backward(
            spatial, n_win, n_query, n_key, chunk, head,
            q_ref, k_ref, v_ref, ga_ref.at[:, lanes], p_ref, gq_ref, dm_ref, db_ref,
        )

    @pl.when(step == a5)
    def _():
        resident(na_hbm).wait()

    @pl.when(jnp.logical_and(step >= a5, step < a6))
    def _():
        i = step - a5
        put_cols(i, 8, 0).wait()
        part = gq_ref[:, pl.ds(pl.multiple_of(i * CHUNK, CHUNK), CHUNK)]
        keep_cols(i, dot_tn(res_ref[...], part).astype(BF16))
        put_cols(i, 9 + i // halves, lax.rem(i, halves)).start()
        add_e(i == 0, part, w_ref[0])

    @pl.when(step >= a6)
    def _():
        rows = rows_at(step - a6)
        out, shift, scale = norm_back_rows(s_ref[...].astype(F32), m_ref[1:2, :], e_ref[rows, :])
        out_ref[...] = (out + gm_ref[rows, :]).astype(out_ref.dtype)
        rows_ref[0:1, :] += shift
        rows_ref[1:2, :] += scale

    @pl.when(due)
    def _():
        tick(passed)

    @pl.when(step == end - 1)
    def _():
        for k in range(2):
            put_cols(k, 8, 0).wait()

        def rest(t, carry):
            tick(t)
            return carry

        lax.fori_loop(len(tick_steps), n_items + REDUCE_TAIL, rest, 0)


def plan_ticks(starts, spatial, ready, spacing):
    takes = (0.6, 5.0, 0.9, 2.5, 3.6 if spatial else 4.6, 3.0, 0.9)
    steps, clock, last = [], 0.0, -spacing
    for section, (lo, hi) in enumerate(zip(starts, starts[1:])):
        for step in range(lo, hi):
            clock += takes[section]
            k = len(steps)
            if (k >= len(ready) or step >= ready[k]) and clock - last >= spacing:
                steps.append(step)
                last = clock
    return tuple(steps)


def block_backward(grad, saved, mods, w_first, first_base, w_second, second_base, spread_shape, spatial, out_type, prev, n_own, nz, cid):
    stream, normed_a, qkv, probs, att, proj, mid, normed_m, act, dact, down = saved
    tokens, width = mid.shape
    shapes = attention_shapes(spatial, tokens)
    n_win, n_query, n_key, _ = shapes
    pairs = width // 128
    halves = width // CHUNK
    a0, a1, a2, a3, a4, a5, a6, end = backward_plan(tokens, width)
    tail = spread_shape[1:]
    zeros = (0,) * len(tail)

    def at(start, stop):
        return lambda i: jnp.clip(i - start, 0, max(stop - start - 1, 0))

    def row_block(place_of):
        return pl.BlockSpec((BLOCK_ROWS, width), lambda i: (place_of(i), 0))

    def g_at(i):
        return jnp.where(i < a1, i, at(a2, a3)(i))

    def first_at(i):
        third = at(a5, a6)(i)
        item = jnp.where(i < a5, 3, third // halves)
        half = jnp.where(i < a5, at(a3, a4)(i), third % halves)
        return (first_base + item, 0, half)

    def up_at(i):
        k = at(a1, a2)(i)
        return (second_base + 2 + 4 * (k // 4) + (k // 2) % 2, 0, k % 2)

    def down_at(i):
        k = at(a1, a2)(i)
        return (second_base // 2 + 2 * (k // 4), k % 4, 0)

    heads = at(a4, a5)
    hidden = pl.BlockSpec((tokens, CHUNK), lambda i: (0, at(a1, a2)(i)))
    anywhere = pl.BlockSpec(memory_space=pl.ANY)
    n_prev = 0 if prev is None else 4
    n_items = n_prev + n_own
    ready = [0] * n_prev
    for done in (2, 4, 4, 4, 6, 8, 8, 8)[:n_own]:
        ready.append(min(a1 + done + 1, a2))
    tick_steps = plan_ticks((a0, a1, a2, a3, a4, a5, a6, end), spatial, ready, TICK_US)
    extra = [] if prev is None else [prev]
    body = functools.partial(backward_body, spatial, shapes, n_prev, n_own, tick_steps, nz)
    if prev is None:
        whole = body

        def body(*refs):
            return whole(*refs[:18], None, *refs[18:])

    dma = pltpu.SemaphoreType.DMA
    return pl.pallas_call(
        body,
        grid=(end,),
        in_specs=[
            row_block(g_at),
            row_block(at(a0, a1)),
            row_block(at(a2, a3)),
            row_block(at(a2, a3)),
            row_block(at(a6, end)),
            fixed(mods.shape),
            hidden,
            hidden,
            pl.BlockSpec((1, width, CHUNK), first_at),
            pl.BlockSpec((1, width, CHUNK), up_at),
            pl.BlockSpec((2, CHUNK // 2, width), down_at),
            pl.BlockSpec((tokens, 128), lambda i: (0, heads(i))),
            pl.BlockSpec((tokens, 128), lambda i: (0, pairs + heads(i))),
            pl.BlockSpec((tokens, 128), lambda i: (0, 2 * pairs + heads(i))),
            pl.BlockSpec((2, n_win, n_query, n_key), lambda i: (heads(i), 0, 0, 0)),
            anywhere, anywhere, anywhere,
        ] + [anywhere] * len(extra),
        out_specs=[
            row_block(at(a6, end)),
            pl.BlockSpec((2,) + tail, lambda i: (heads(i),) + zeros),
            pl.BlockSpec((8, width), lambda i: (0, 0)),
            anywhere,
            anywhere,
        ],
        out_shape=[
            jax.ShapeDtypeStruct((tokens, width), out_type),
            jax.ShapeDtypeStruct(spread_shape, F32),
            jax.ShapeDtypeStruct((8, width), F32),
            jax.ShapeDtypeStruct((12, nz, 2, 2, ROWS, COLS), BF16),
            jax.ShapeDtypeStruct((n_items, ROWS, COLS), F32),
        ],
        scratch_shapes=[
            pltpu.VMEM((tokens, width), BF16),
            pltpu.VMEM((tokens, width), BF16),
            pltpu.VMEM((tokens, width), F32),
            pltpu.VMEM((tokens, width), F32),
            pltpu.VMEM((tokens, width), BF16),
            pltpu.VMEM((tokens, 3 * width), BF16),
            pltpu.VMEM((2, n_query, n_key), F32),
            pltpu.VMEM((2, 2, 1, 2, 2, ROWS, COLS), BF16),
            pltpu.VMEM((2, nz, 2, 2, ROWS, CHUNK), BF16),
            dma,
            dma((2,)),
            dma((2,)),
        ] + reduce_scratch(nz),
        compiler_params=pltpu.CompilerParams(
            collective_id=cid, has_side_effects=True, vmem_limit_bytes=64 * MIB
        ),
        name="block_backward",
    )(grad, down, mid, proj, stream, mods, act, dact, w_first, w_second, w_second, qkv, qkv, qkv, probs,
      normed_m, att, normed_a, *extra)


def swap_rows(values, me, swap):
    keep = lax.dynamic_index_in_dim(values, me, 1, keepdims=False)
    send = lax.dynamic_index_in_dim(values, 1 - me, 1, keepdims=False)
    recv = lax.ppermute(send.astype(BF16), "frame", swap).astype(values.dtype)
    first = jnp.where(me == 0, keep, recv)
    second = jnp.where(me == 0, recv, keep)
    full = jnp.concatenate([first, second], axis=0)
    return full.transpose(2, 0, 1, 3, 4).reshape(-1, values.shape[-1])


def unswap_rows(values, me, swap, n_cw, f_l):
    depth = values.shape[-1]
    full = values.reshape(n_cw, 2, f_l, TWIN, TWIN, depth)
    keep = lax.dynamic_index_in_dim(full, me, 1, keepdims=False)
    send = lax.dynamic_index_in_dim(full, 1 - me, 1, keepdims=False)
    recv = lax.ppermute(send.astype(BF16), "frame", swap).astype(values.dtype)
    first = jnp.where(me == 0, keep, recv)
    second = jnp.where(me == 0, recv, keep)
    both = jnp.stack([first, second], axis=0)
    return both.transpose(2, 0, 3, 1, 4, 5).reshape(-1, depth)


def pack_shards(shards, b):
    w_qkv, w_proj, w_up, w_down = [w[:, b] for w in shards]
    parts = []
    for w in (w_qkv, w_proj):
        parts.append(w.reshape(ROWS, -1, COLS).transpose(1, 0, 2))
    parts.append(w_up.reshape(ROWS, 2, 8, 2, 128).transpose(3, 1, 0, 2, 4).reshape(4, ROWS, COLS))
    downs = w_down.reshape(-1, ROWS, COLS)
    ups = parts.pop()
    parts += [downs[0:2], ups[0:2], downs[2:4], ups[2:4]]
    return jnp.concatenate(parts, axis=0)


def on_device(
    frames_in, size_group, modulation, w_qkv, w_proj, w_up, w_down, table_sp, table_st, cotangent
):
    n_clips, f_l, n_rows, n_cols, width = frames_in.shape
    me = lax.axis_index("frame")
    swap = [(0, 1), (1, 0)]
    n_cw = n_cols // TWIN
    nz = lax.axis_size("clip") // 4
    natural = (f_l, 2, TWIN, n_cw, TWIN, width)
    shards = (w_qkv, w_proj, w_up, w_down)
    packed = [pack_shards(shards, b) for b in range(2)]
    early = jnp.concatenate([packed[0], packed[1][:4]], axis=0)
    limit = n_cols - 3 * (2 - size_group[0])
    wide = (jnp.arange(n_cols, dtype=jnp.int32) < limit).astype(F32)
    ok_sp = jnp.broadcast_to(wide[None, None, None, :], (f_l, 1, n_rows, n_cols))
    ok_sp = ok_sp.reshape(f_l, 1, n_rows * n_cols)
    frame_ok = (jnp.arange(KEYF) < FILLED).astype(F32)
    ok_st = wide.reshape(n_cw, 1, 1, TWIN) * frame_ok[None, :, None, None]
    ok_st = jnp.broadcast_to(ok_st, (n_cw, KEYF, TWIN, TWIN)).reshape(n_cw, 1, -1)
    spread0 = spread_sp(table_sp)
    spread1 = spread_st(table_st)
    mods = modulation[0].reshape(2, 6, width)
    mods = jnp.pad(mods, ((0, 0), (0, 2), (0, 0)))
    cot = swap_rows(cotangent.reshape(natural), me, swap)
    stream0 = frames_in.reshape(-1, width).astype(F32)
    mid_stream, saved0, full0 = block_forward(
        stream0, mods[0], early, None, 0, spread0, ok_sp, True, F32, nz, 1
    )
    stream1 = swap_rows(mid_stream.reshape(natural), me, swap)
    end_stream, saved1, full1 = block_forward(
        stream1, mods[1], packed[1][4:], full0, 4, spread1, ok_st, False, BF16, nz, 5
    )
    full0 = full0.reshape(-1, width, width)
    full1 = full1.reshape(-1, width, width)
    mixed = unswap_rows(end_stream, me, swap, n_cw, f_l).reshape(frames_in.shape)
    grad1, gspread1, rows1, gw1, shares1 = block_backward(
        cot, saved1, mods[1], full0, 12, full1, 0, spread1.shape, False, F32, None, 8, nz, 2
    )
    grad_mid = unswap_rows(grad1, me, swap, n_cw, f_l)
    grad0, gspread0, rows0, gw0, shares0 = block_backward(
        grad_mid, saved0, mods[0], full0, 0, full0, 4, spread0.shape, True, BF16, gw1, 8, nz, 3
    )
    def wide_pad(table):
        return jnp.pad(table, ((0, 0), (0, -table.shape[1] % 128)))

    small = (
        jnp.pad(jnp.concatenate([rows0[:6], rows1[:6]], axis=0), ((0, 4), (0, 0))),
        wide_pad(gather_sp(gspread0)),
        wide_pad(gather_st(gspread1)),
    )
    last, mods_sum, sp_sum, st_sum = reduce_last(gw0, (8, 4), small, nz, 4)
    def pair(first, second):
        return jnp.stack([first, second], axis=1)

    def qkv_of(items):
        return jnp.concatenate([items[0], items[1], items[2]], axis=-1)

    def up_of(items):
        parts = jnp.stack([items[0], items[1], items[4], items[5]]).reshape(2, 2, ROWS, 8, 128)
        return parts.transpose(2, 1, 3, 0, 4).reshape(ROWS, 4 * COLS)

    def down_of(items):
        return jnp.concatenate([items[2], items[3], items[6], items[7]], axis=0)

    own0 = shares0[4:]
    outs = (
        pair(qkv_of(last[1:]), qkv_of(shares0[1:4])),
        pair(last[0], shares0[0]),
        pair(up_of(own0), up_of(shares1)),
        pair(down_of(own0), down_of(shares1)),
    )
    mod_grad = mods_sum[:12][None]
    g_sp = sp_sum[:, : table_sp.shape[1]]
    g_st = st_sum[:, : table_st.shape[1]]
    grad_in = grad0.reshape(frames_in.shape)
    return (mixed, grad_in, mod_grad, outs[0], outs[1], outs[2], outs[3], g_sp, g_st)


HIGHEST = lax.Precision.HIGHEST


def layer_norm(values):
    centered = values - jnp.mean(values, axis=-1, keepdims=True)
    spread = jnp.mean(centered * centered, axis=-1, keepdims=True)
    return centered * lax.rsqrt(spread + NORM_EPS)


def modulate(values, shift_row, scale_row):
    return layer_norm(values) * (1.0 + scale_row) + shift_row


def gelu_tanh(values):
    return jax.nn.gelu(values, approximate=True)


def row_of(mod_rows, which):
    return mod_rows[:, which][:, None, None, None, :]


def clip_sum(values):
    return jnp.sum(values, axis=(1, 2, 3))


def flat_dot(values, weight):
    flat_in = values.reshape(-1, values.shape[-1])
    flat_out = jnp.dot(flat_in, weight, preferred_element_type=jnp.float32)
    return flat_out.reshape(values.shape[:-1] + (weight.shape[1],))


def back_dot(grad_values, weight):
    flat_in = grad_values.reshape(-1, grad_values.shape[-1])
    flat_out = jnp.einsum("nb,ab->na", flat_in, weight, preferred_element_type=jnp.float32)
    return flat_out.reshape(grad_values.shape[:-1] + (weight.shape[0],))


def outer_dot(left_values, right_values):
    left_flat = left_values.reshape(-1, left_values.shape[-1])
    right_flat = right_values.reshape(-1, right_values.shape[-1])
    return jnp.einsum("na,nb->ab", left_flat, right_flat, preferred_element_type=jnp.float32)


def split_heads(values, n_heads):
    return values.reshape(values.shape[0], values.shape[1], n_heads, -1)


def offset_pick(side_len):
    position = jnp.arange(side_len, dtype=jnp.int32)
    offsets = position[:, None] - position[None, :] + side_len - 1
    targets = jnp.arange(2 * side_len - 1, dtype=jnp.int32)
    return (offsets[:, :, None] == targets[None, None, :]).astype(jnp.float32)


def expand_bias(table, side_len):
    one_hot = offset_pick(side_len)
    rows_done = jnp.einsum("hab,xya->hxyb", table, one_hot, precision=HIGHEST)
    full_bias = jnp.einsum("hxyb,uvb->hxuyv", rows_done, one_hot, precision=HIGHEST)
    return full_bias.reshape(table.shape[0], side_len * side_len, side_len * side_len)


def cube_bias(table_st, first_frame, local_frames):
    n_heads = table_st.shape[0]
    span_frames = 2 * FRAMES - 1
    side_span = 2 * TWIN - 1
    table_cube = table_st.reshape(n_heads, span_frames, side_span * side_span)
    query_frames = first_frame + jnp.arange(local_frames, dtype=jnp.int32)
    key_frames = jnp.arange(FRAMES, dtype=jnp.int32)
    offsets = query_frames[:, None] - key_frames[None, :] + FRAMES - 1
    choose = (
        offsets[:, :, None] == jnp.arange(span_frames, dtype=jnp.int32)[None, None, :]
    ).astype(jnp.float32)
    picked = jnp.einsum("hoz,jfo->hjfz", table_cube, choose, precision=HIGHEST)
    squares = expand_bias(picked.reshape(-1, side_span, side_span), TWIN)
    squares = squares.reshape(n_heads, local_frames, FRAMES, TWIN * TWIN, TWIN * TWIN)
    squares = squares.transpose(0, 1, 3, 2, 4)
    return squares.reshape(n_heads, local_frames * TWIN * TWIN, FRAMES * TWIN * TWIN)


def spatial_windows(values):
    n_clips, n_frames, n_rows, n_cols, n_depth = values.shape
    blocked = values.reshape(n_clips, n_frames, n_rows // SWIN, SWIN, n_cols // SWIN, SWIN, n_depth)
    return blocked.transpose(0, 1, 2, 4, 3, 5, 6).reshape(-1, SWIN * SWIN, n_depth)


def spatial_unwindow(values, full_shape):
    n_clips, n_frames, n_rows, n_cols, n_depth = full_shape
    blocked = values.reshape(n_clips, n_frames, n_rows // SWIN, n_cols // SWIN, SWIN, SWIN, n_depth)
    return blocked.transpose(0, 1, 2, 4, 3, 5, 6).reshape(full_shape)


def cube_windows(values):
    n_clips, n_frames, n_rows, n_cols, n_depth = values.shape
    blocked = values.reshape(n_clips, n_frames, n_rows // TWIN, TWIN, n_cols // TWIN, TWIN, n_depth)
    blocked = blocked.transpose(0, 2, 4, 1, 3, 5, 6)
    return blocked.reshape(
        n_clips * (n_rows // TWIN) * (n_cols // TWIN), n_frames * TWIN * TWIN, n_depth
    )


def cube_unwindow(values, full_shape):
    n_clips, n_frames, n_rows, n_cols, n_depth = full_shape
    blocked = values.reshape(n_clips, n_rows // TWIN, n_cols // TWIN, n_frames, TWIN, TWIN, n_depth)
    return blocked.transpose(0, 3, 1, 4, 2, 5, 6).reshape(full_shape)


def soft_scores(query_win, key_win, bias, key_ok, score_scale):
    scores = jnp.einsum("nqhd,nkhd->nhqk", query_win, key_win, preferred_element_type=jnp.float32)
    scores = scores * score_scale + bias[None]
    scores = jnp.where(key_ok[:, None, None, :], scores, NEG_FILL)
    row_top = jnp.max(scores, axis=-1, keepdims=True)
    expo_values = jnp.exp(scores - row_top)
    return expo_values / jnp.sum(expo_values, axis=-1, keepdims=True)


def general_forward(
    stream,
    mod_rows,
    weights,
    n_heads,
    bias,
    key_ok,
    to_windows,
    from_windows,
    fetch_keys,
    score_scale,
):
    qkv_w, proj_w, up_w, down_w = weights
    width_d = stream.shape[-1]
    normed_a = modulate(stream, row_of(mod_rows, 0), row_of(mod_rows, 1)).astype(jnp.bfloat16)
    qkv_values = flat_dot(normed_a, qkv_w).astype(jnp.bfloat16)
    key_local = qkv_values[..., width_d : 2 * width_d]
    value_local = qkv_values[..., 2 * width_d :]
    query_win = split_heads(to_windows(qkv_values[..., :width_d]), n_heads)
    key_flat, value_flat = fetch_keys(key_local, value_local)
    key_win = split_heads(key_flat, n_heads)
    value_win = split_heads(value_flat, n_heads)
    soft_probs = soft_scores(query_win, key_win, bias, key_ok, score_scale)
    att_win = jnp.einsum(
        "nhqk,nkhd->nqhd",
        soft_probs.astype(jnp.bfloat16),
        value_win,
        preferred_element_type=jnp.float32,
    ).astype(jnp.bfloat16)
    att_out = from_windows(
        att_win.reshape(att_win.shape[0], att_win.shape[1], width_d), stream.shape
    )
    proj_out = flat_dot(att_out, proj_w)
    mid_stream = stream + row_of(mod_rows, 2) * proj_out
    normed_m = modulate(mid_stream, row_of(mod_rows, 3), row_of(mod_rows, 4)).astype(jnp.bfloat16)
    up_value = flat_dot(normed_m, up_w)
    active = gelu_tanh(up_value).astype(jnp.bfloat16)
    down_out = flat_dot(active, down_w)
    result = mid_stream + row_of(mod_rows, 5) * down_out
    saved = (
        stream,
        normed_a,
        query_win,
        key_win,
        value_win,
        key_local,
        value_local,
        att_out,
        proj_out,
        mid_stream,
        normed_m,
        up_value,
        active,
        down_out,
    )
    return (result, saved)


def general_backward(
    grad_out,
    saved,
    mod_rows,
    weights,
    n_heads,
    bias,
    key_ok,
    to_windows,
    from_windows,
    return_keys,
    key_win,
    value_win,
    score_scale,
):
    (
        stream,
        normed_a,
        query_win,
        unused_key,
        unused_value,
        key_local,
        value_local,
        att_out,
        proj_out,
        mid_stream,
        normed_m,
        up_value,
        active,
        down_out,
    ) = saved
    qkv_w, proj_w, up_w, down_w = weights
    n_clips = stream.shape[0]
    width_d = stream.shape[-1]
    grad_down_v = (row_of(mod_rows, 5) * grad_out).astype(jnp.bfloat16)
    gate_m_grad = clip_sum(grad_out * down_out)
    down_grad = outer_dot(active, grad_down_v)
    grad_act = back_dot(grad_down_v, down_w)
    unused_gelu, gelu_pull = jax.vjp(gelu_tanh, up_value)
    grad_up_v = gelu_pull(grad_act)[0].astype(jnp.bfloat16)
    up_grad = outer_dot(normed_m, grad_up_v)
    grad_normed = back_dot(grad_up_v, up_w)
    unused_norm, norm_pull = jax.vjp(modulate, mid_stream, row_of(mod_rows, 3), row_of(mod_rows, 4))
    grad_mid, shift_m_grad, scale_m_grad = norm_pull(grad_normed)
    grad_mid = grad_mid + grad_out
    grad_proj_v = (row_of(mod_rows, 2) * grad_mid).astype(jnp.bfloat16)
    gate_a_grad = clip_sum(grad_mid * proj_out)
    proj_grad = outer_dot(att_out, grad_proj_v)
    grad_att = back_dot(grad_proj_v, proj_w).astype(jnp.bfloat16)
    grad_att_win = split_heads(to_windows(grad_att), n_heads)
    soft_probs = soft_scores(query_win, key_win, bias, key_ok, score_scale)
    grad_probs = jnp.einsum(
        "nqhd,nkhd->nhqk", grad_att_win, value_win, preferred_element_type=jnp.float32
    )
    row_delta = jnp.sum(soft_probs * grad_probs, axis=-1, keepdims=True)
    grad_scores = (soft_probs * (grad_probs - row_delta)).astype(jnp.bfloat16)
    grad_bias = jnp.sum(grad_scores.astype(jnp.float32), axis=0)
    grad_query = (
        jnp.einsum("nhqk,nkhd->nqhd", grad_scores, key_win, preferred_element_type=jnp.float32)
        * score_scale
    )
    grad_key = (
        jnp.einsum("nhqk,nqhd->nkhd", grad_scores, query_win, preferred_element_type=jnp.float32)
        * score_scale
    )
    grad_value = jnp.einsum(
        "nhqk,nqhd->nkhd",
        soft_probs.astype(jnp.bfloat16),
        grad_att_win,
        preferred_element_type=jnp.float32,
    )
    n_win = grad_query.shape[0]
    grad_query = from_windows(grad_query.reshape(n_win, grad_query.shape[1], width_d), stream.shape)
    grad_key_full, grad_value_full = return_keys(
        grad_key.reshape(n_win, grad_key.shape[1], width_d),
        grad_value.reshape(n_win, grad_value.shape[1], width_d),
    )
    grad_qkv_v = jnp.concatenate([grad_query, grad_key_full, grad_value_full], axis=-1).astype(
        jnp.bfloat16
    )
    qkv_grad = outer_dot(normed_a, grad_qkv_v)
    grad_normed = back_dot(grad_qkv_v, qkv_w)
    unused_norm, norm_pull = jax.vjp(modulate, stream, row_of(mod_rows, 0), row_of(mod_rows, 1))
    grad_stream, shift_a_grad, scale_a_grad = norm_pull(grad_normed)
    grad_stream = grad_stream + grad_mid
    mod_grad = jnp.stack(
        [
            shift_a_grad.reshape(n_clips, width_d),
            scale_a_grad.reshape(n_clips, width_d),
            gate_a_grad,
            shift_m_grad.reshape(n_clips, width_d),
            scale_m_grad.reshape(n_clips, width_d),
            gate_m_grad,
        ],
        axis=1,
    )
    return (grad_stream, mod_grad, (qkv_grad, proj_grad, up_grad, down_grad), grad_bias)


def on_device_general(
    frames_in, size_group, modulation, w_qkv, w_proj, w_up, w_down, table_sp, table_st, cotangent
):
    n_clips, local_frames, n_rows, n_cols, width_d = frames_in.shape
    n_heads = table_sp.shape[0]
    score_scale = (width_d // n_heads) ** (-0.5)
    first_frame = lax.axis_index("frame") * local_frames
    local_shape = (n_clips, local_frames, n_rows, n_cols, width_d)
    whole_shape = (n_clips, FRAMES, n_rows, n_cols, width_d)
    gathered = (
        lax.all_gather(w_qkv, "clip", axis=0, tiled=True),
        lax.all_gather(w_proj, "clip", axis=0, tiled=True),
        lax.all_gather(w_up, "clip", axis=0, tiled=True),
        lax.all_gather(w_down, "clip", axis=0, tiled=True),
    )
    column_ids = jnp.arange(n_cols, dtype=jnp.int32)
    column_limit = n_cols - 3 * (2 - size_group)
    wide_ok = column_ids[None, :] < column_limit[:, None]
    local_ok = jnp.broadcast_to(wide_ok[:, None, None, :], (n_clips, local_frames, n_rows, n_cols))
    spatial_ok = spatial_windows(local_ok[..., None])[..., 0]
    frame_ok = jnp.arange(FRAMES, dtype=jnp.int32) < FILLED
    cube_grid = wide_ok[:, None, None, :] & frame_ok[None, :, None, None]
    cube_grid = jnp.broadcast_to(cube_grid, (n_clips, FRAMES, n_rows, n_cols))
    cube_ok = cube_windows(cube_grid[..., None])[..., 0]
    span_sp = 2 * SWIN - 1

    def build_spatial(table):
        return expand_bias(table.reshape(n_heads, span_sp, span_sp), SWIN)

    def build_cube(table):
        return cube_bias(table, first_frame, local_frames)

    bias_sp, pull_sp = jax.vjp(build_spatial, table_sp)
    bias_st, pull_st = jax.vjp(build_cube, table_st)

    def spatial_keys(key_local, value_local):
        return (spatial_windows(key_local), spatial_windows(value_local))

    def cube_keys(key_local, value_local):
        key_all, value_all = (
            lax.all_gather(key_local, "frame", axis=1, tiled=True),
            lax.all_gather(value_local, "frame", axis=1, tiled=True),
        )
        return (cube_windows(key_all), cube_windows(value_all))

    def spatial_return(grad_key, grad_value):
        return (spatial_unwindow(grad_key, local_shape), spatial_unwindow(grad_value, local_shape))

    def cube_return(grad_key, grad_value):
        key_whole = cube_unwindow(grad_key, whole_shape)
        value_whole = cube_unwindow(grad_value, whole_shape)
        return (
            lax.psum_scatter(
                key_whole.astype(jnp.bfloat16), "frame", scatter_dimension=1, tiled=True
            ).astype(jnp.float32),
            lax.psum_scatter(
                value_whole.astype(jnp.bfloat16), "frame", scatter_dimension=1, tiled=True
            ).astype(jnp.float32),
        )

    weights_sp = (gathered[0][:, 0], gathered[1][:, 0], gathered[2][:, 0], gathered[3][:, 0])
    weights_st = (gathered[0][:, 1], gathered[1][:, 1], gathered[2][:, 1], gathered[3][:, 1])
    stream_mid, saved_sp = general_forward(
        frames_in.astype(jnp.float32),
        modulation[:, 0:6],
        weights_sp,
        n_heads,
        bias_sp,
        spatial_ok,
        spatial_windows,
        spatial_unwindow,
        spatial_keys,
        score_scale,
    )
    stream_end, saved_st = general_forward(
        stream_mid,
        modulation[:, 6:12],
        weights_st,
        n_heads,
        bias_st,
        cube_ok,
        cube_windows,
        cube_unwindow,
        cube_keys,
        score_scale,
    )
    mixed = stream_end.astype(jnp.bfloat16)
    again = (
        lax.all_gather(w_qkv, "clip", axis=0, tiled=True),
        lax.all_gather(w_proj, "clip", axis=0, tiled=True),
        lax.all_gather(w_up, "clip", axis=0, tiled=True),
        lax.all_gather(w_down, "clip", axis=0, tiled=True),
    )
    back_sp = (again[0][:, 0], again[1][:, 0], again[2][:, 0], again[3][:, 0])
    back_st = (again[0][:, 1], again[1][:, 1], again[2][:, 1], again[3][:, 1])
    key_again, value_again = (
        lax.all_gather(saved_st[5], "frame", axis=1, tiled=True),
        lax.all_gather(saved_st[6], "frame", axis=1, tiled=True),
    )
    key_win_st = split_heads(cube_windows(key_again), n_heads)
    value_win_st = split_heads(cube_windows(value_again), n_heads)
    grad_stream, mod_grad_st, grads_st, bias_grad_st = general_backward(
        cotangent.astype(jnp.float32),
        saved_st,
        modulation[:, 6:12],
        back_st,
        n_heads,
        bias_st,
        cube_ok,
        cube_windows,
        cube_unwindow,
        cube_return,
        key_win_st,
        value_win_st,
        score_scale,
    )
    grad_stream, mod_grad_sp, grads_sp, bias_grad_sp = general_backward(
        grad_stream,
        saved_sp,
        modulation[:, 0:6],
        back_sp,
        n_heads,
        bias_sp,
        spatial_ok,
        spatial_windows,
        spatial_unwindow,
        spatial_return,
        saved_sp[3],
        saved_sp[4],
        score_scale,
    )
    table_sp_grad = pull_sp(bias_grad_sp)[0]
    table_st_grad = pull_st(bias_grad_st)[0]
    full_qkv = jnp.stack([grads_sp[0], grads_st[0]], axis=1)
    full_proj = jnp.stack([grads_sp[1], grads_st[1]], axis=1)
    full_up = jnp.stack([grads_sp[2], grads_st[2]], axis=1)
    full_down = jnp.stack([grads_sp[3], grads_st[3]], axis=1)
    shares = (
        lax.psum_scatter(
            full_qkv.astype(jnp.bfloat16), "clip", scatter_dimension=0, tiled=True
        ).astype(jnp.float32),
        lax.psum_scatter(
            full_proj.astype(jnp.bfloat16), "clip", scatter_dimension=0, tiled=True
        ).astype(jnp.float32),
        lax.psum_scatter(
            full_up.astype(jnp.bfloat16), "clip", scatter_dimension=0, tiled=True
        ).astype(jnp.float32),
        lax.psum_scatter(
            full_down.astype(jnp.bfloat16), "clip", scatter_dimension=0, tiled=True
        ).astype(jnp.float32),
    )
    mod_grad = jnp.concatenate([mod_grad_sp, mod_grad_st], axis=1)
    summed = (
        lax.psum(shares[0].astype(jnp.bfloat16), "frame").astype(jnp.float32),
        lax.psum(shares[1].astype(jnp.bfloat16), "frame").astype(jnp.float32),
        lax.psum(shares[2].astype(jnp.bfloat16), "frame").astype(jnp.float32),
        lax.psum(shares[3].astype(jnp.bfloat16), "frame").astype(jnp.float32),
        lax.psum(mod_grad.astype(jnp.bfloat16), "frame").astype(jnp.float32),
        lax.psum(table_sp_grad.astype(jnp.bfloat16), "frame").astype(jnp.float32),
        lax.psum(table_st_grad.astype(jnp.bfloat16), "frame").astype(jnp.float32),
    )
    tables = (
        lax.psum(summed[5].astype(jnp.bfloat16), "clip").astype(jnp.float32),
        lax.psum(summed[6].astype(jnp.bfloat16), "clip").astype(jnp.float32),
    )
    return (
        mixed,
        grad_stream.astype(jnp.bfloat16),
        summed[4],
        summed[0],
        summed[1],
        summed[2],
        summed[3],
        tables[0],
        tables[1],
    )


def solution(mesh):
    placed = (
        P("clip", "frame", None, None, None),
        P("clip"),
        P("clip", None, None),
        P("clip", None, None),
        P("clip", None, None),
        P("clip", None, None),
        P("clip", None, None),
        P(),
        P(),
        P("clip", "frame", None, None, None),
    )
    whole_windows = mesh.shape["frame"] == 2 and mesh.shape["clip"] == 16
    return jax.shard_map(
        on_device if whole_windows else on_device_general,
        mesh=mesh,
        in_specs=placed,
        out_specs=(
            P("clip", "frame", None, None, None),
            P("clip", "frame", None, None, None),
            P("clip", None, None),
            P("clip", None, None),
            P("clip", None, None),
            P("clip", None, None),
            P("clip", None, None),
            P(),
            P(),
        ),
        check_vma=False,
    )
```

```python
import functools

import jax
import jax.numpy as jnp
import numpy as np
from jax import lax
from jax.experimental import pallas as pl
from jax.experimental.pallas import tpu as pltpu
from jax.sharding import PartitionSpec as P

SWIN = 16
TWIN = 8
FRAMES = 8
FILLED = 5
KEYF = 6
NEG_FILL = -1000000000.0
NORM_EPS = 1e-06
F32 = jnp.float32
BF16 = jnp.bfloat16
NT = (((1,), (1,)), ((), ()))
TN = (((0,), (0,)), ((), ()))


def dot_nn(a, b):
    return jnp.dot(a, b, preferred_element_type=F32)


def dot_nt(a, b):
    return lax.dot_general(a, b, NT, preferred_element_type=F32)


def dot_tn(a, b):
    return lax.dot_general(a, b, TN, preferred_element_type=F32)


def norm_stats(values):
    mean = jnp.mean(values, axis=-1, keepdims=True)
    centered = values - mean
    spread = jnp.mean(centered * centered, axis=-1, keepdims=True)
    inv = lax.rsqrt(spread + NORM_EPS)
    return centered * inv, inv


def pick_sp():
    span = 2 * SWIN - 1
    k, b, ci, lane = np.ogrid[0:8, 0:span, 0:SWIN, 0:128]
    hit = (k == 7 - lane // SWIN) & (b == SWIN - 1 + ci - lane % SWIN)
    return hit.reshape(8 * span, SWIN * 128).astype(np.float32)


def pick_st():
    span = 2 * TWIN - 1
    r, b, ci, lane = np.ogrid[0:span, 0:span, 0:TWIN, 0:128]
    hit = (r == span - 1 - lane // TWIN) & (b == TWIN - 1 + ci - lane % TWIN)
    return hit.reshape(span * span, TWIN * 128).astype(np.float32)


def spread_sp(table):
    n_heads = table.shape[0]
    span = 2 * SWIN - 1
    padded = jnp.pad(table, ((0, 0), (span, 0))).reshape(n_heads * 4, 8 * span)
    out = jnp.dot(padded, pick_sp(), precision=lax.Precision.HIGHEST)
    return out.reshape(n_heads, 4, SWIN, 128)


def spread_st(table):
    n_heads = table.shape[0]
    span = 2 * TWIN - 1
    fspan = 2 * FRAMES - 1
    flat = table.reshape(n_heads * fspan, span * span)
    out = jnp.dot(flat, pick_st(), precision=lax.Precision.HIGHEST)
    return out.reshape(n_heads, fspan, TWIN, 128)


def gather_sp(spread):
    n_heads = spread.shape[0]
    span = 2 * SWIN - 1
    flat = spread.reshape(n_heads * 4, SWIN * 128)
    out = lax.dot_general(flat, pick_sp(), NT, precision=lax.Precision.HIGHEST)
    return out.reshape(n_heads, 32 * span)[:, span:]


def gather_st(spread):
    n_heads = spread.shape[0]
    span = 2 * TWIN - 1
    fspan = 2 * FRAMES - 1
    flat = spread.reshape(n_heads * fspan, TWIN * 128)
    out = lax.dot_general(flat, pick_st(), NT, precision=lax.Precision.HIGHEST)
    return out.reshape(n_heads, fspan * span * span)


def fill_bias_sp(spread_ref, hh, bias_ref):
    spread = jnp.concatenate([spread_ref[hh, g] for g in (3, 2, 1, 0)], axis=1)
    width = spread.shape[1]
    win = SWIN * SWIN
    for ri in range(SWIN):
        shift = (width - (SWIN - 1 - ri) * SWIN) % width
        rolled = pltpu.roll(spread, shift, 1) if shift else spread
        bias_ref[ri * SWIN : (ri + 1) * SWIN, :] = rolled[:, :win]


def fold_bias_sp(grad_ref, out_ref, hh):
    win = SWIN * SWIN
    width = 2 * win
    total = None
    for ri in range(SWIN):
        rows = grad_ref[ri * SWIN : (ri + 1) * SWIN, :]
        rows = jnp.concatenate([rows, jnp.zeros((SWIN, width - win), F32)], axis=1)
        shift = (SWIN - 1 - ri) * SWIN
        rows = pltpu.roll(rows, shift, 1) if shift else rows
        total = rows if total is None else total + rows
    for g in range(4):
        out_ref[hh, g] = total[:, (3 - g) * 128 : (4 - g) * 128]


def fill_bias_st(spread_ref, hh, bias_ref):
    lanes = lax.broadcasted_iota(jnp.int32, (TWIN, 128), 1)
    half = TWIN * TWIN
    n_pairs = KEYF // 2
    for ri in range(TWIN):
        shift = (128 - (TWIN - 1 - ri) * TWIN) % 128
        cache = {}

        def low_of(f):
            if f not in cache:
                rows = spread_ref[hh, 2 * FRAMES - 2 - f]
                cache[f] = pltpu.roll(rows, shift, 1) if shift else rows
            return cache[f]

        pairs = {}
        for fi in range(FRAMES):
            for pair in range(n_pairs):
                f = FRAMES - 1 - fi + 2 * pair
                if f not in pairs:
                    pairs[f] = jnp.where(
                        lanes < half, low_of(f), pltpu.roll(low_of(f + 1), half, 1)
                    )
                row = fi * half + ri * TWIN
                bias_ref[row : row + TWIN, pair * 128 : (pair + 1) * 128] = pairs[f]


def fold_bias_st(grad_ref, out_ref, hh):
    lanes = lax.broadcasted_iota(jnp.int32, (TWIN, 128), 1)
    half = TWIN * TWIN
    n_pairs = KEYF // 2
    fspan = 2 * FRAMES - 1
    totals = [None] * fspan
    for ri in range(TWIN):
        sums = {}
        for fi in range(FRAMES):
            for pair in range(n_pairs):
                f = FRAMES - 1 - fi + 2 * pair
                row = fi * half + ri * TWIN
                part = grad_ref[row : row + TWIN, pair * 128 : (pair + 1) * 128]
                sums[f] = part if f not in sums else sums[f] + part
        for f in range(fspan):
            piece = None
            if f in sums:
                piece = jnp.where(lanes < half, sums[f], 0.0)
            if f - 1 in sums:
                upper = pltpu.roll(jnp.where(lanes >= half, sums[f - 1], 0.0), half, 1)
                piece = upper if piece is None else piece + upper
            if piece is None:
                continue
            shift = (TWIN - 1 - ri) * TWIN
            piece = pltpu.roll(piece, shift, 1) if shift else piece
            totals[f] = piece if totals[f] is None else totals[f] + piece
    for f in range(fspan):
        out_ref[hh, 2 * FRAMES - 2 - f] = jnp.zeros((TWIN, 128), F32) if totals[f] is None else totals[f]


def lane_mask(rows, hh):
    lanes = lax.broadcasted_iota(jnp.int32, (rows, 128), 1)
    return (lanes < 64) if hh == 0 else (lanes >= 64)


def attend_forward(spatial, n_win, n_query, n_key, chunk, q_ref, k_ref, v_ref, m_ref, ok_ref, att_ref, p_ref, bias_ref):
    for hh in range(2):
        if spatial:
            fill_bias_sp(m_ref, hh, bias_ref.at[hh])
        else:
            fill_bias_st(m_ref, hh, bias_ref.at[hh])
    own = lane_mask(chunk, 0)
    for n in range(n_win):
        key = k_ref[n * n_query : n * n_query + n_key, :]
        val = v_ref[n * n_query : n * n_query + n_key, :]
        ok = ok_ref[n] > 0.0
        for c in range(n_query // chunk):
            rows = slice(n * n_query + c * chunk, n * n_query + (c + 1) * chunk)
            query = q_ref[rows, :]
            query = query * jnp.asarray(0.125, BF16)
            outs = []
            for hh in range(2):
                mine = own if hh == 0 else jnp.logical_not(own)
                picked = jnp.where(mine, query, jnp.zeros_like(query))
                scores = dot_nt(picked, key) + bias_ref[hh, c * chunk : (c + 1) * chunk, :]
                scores = jnp.where(ok, scores, NEG_FILL)
                top = jnp.max(scores, axis=-1, keepdims=True)
                expo = jnp.exp(scores - top)
                probs = (expo * (1.0 / jnp.sum(expo, axis=-1, keepdims=True))).astype(BF16)
                p_ref[hh, n, c * chunk : (c + 1) * chunk, :] = probs
                outs.append(dot_nn(probs, val))
            att_ref[rows, :] = jnp.where(own, outs[0], outs[1]).astype(BF16)


def attend_backward(
    spatial, n_win, n_query, n_key, chunk, head, q_ref, k_ref, v_ref, do_ref, p_ref, g_ref, dm_ref, db_ref
):
    width = g_ref.shape[1] // 3
    own = lane_mask(chunk, 0)
    own_k = lane_mask(n_key, 0)

    def store(rows, which, values):
        g_ref[rows, pl.ds(pl.multiple_of(which * width + head * 128, 128), 128)] = values

    db_ref[...] = jnp.zeros_like(db_ref)
    for n in range(n_win):
        keys = slice(n * n_query, n * n_query + n_key)
        key = k_ref[keys, :]
        val = v_ref[keys, :]
        gk = [None, None]
        gv = [None, None]
        for c in range(n_query // chunk):
            rows = slice(n * n_query + c * chunk, n * n_query + (c + 1) * chunk)
            part = slice(c * chunk, (c + 1) * chunk)
            query = q_ref[rows, :]
            gout = do_ref[rows, :]
            gq = []
            for hh in range(2):
                mine = own if hh == 0 else jnp.logical_not(own)
                probs = p_ref[hh, n, part, :]
                gsel = jnp.where(mine, gout, jnp.zeros_like(gout))
                dprob = dot_nt(gsel, val)
                soft = probs.astype(F32)
                delta = jnp.sum(soft * dprob, axis=-1, keepdims=True)
                dscore = (soft * (dprob - delta)).astype(BF16)
                db_ref[hh, part, :] += dscore.astype(F32)
                gq.append(dot_nn(dscore, key))
                dk = dot_tn(dscore, query)
                dv = dot_tn(probs, gout)
                gk[hh] = dk if gk[hh] is None else gk[hh] + dk
                gv[hh] = dv if gv[hh] is None else gv[hh] + dv
            store(rows, 0, (jnp.where(own, gq[0], gq[1]) * 0.125).astype(BF16))
        store(keys, 1, (jnp.where(own_k, gk[0], gk[1]) * 0.125).astype(BF16))
        store(keys, 2, jnp.where(own_k, gv[0], gv[1]).astype(BF16))
        if n_key < n_query:
            rest = slice(n * n_query + n_key, (n + 1) * n_query)
            empty = jnp.zeros((n_query - n_key, 128), BF16)
            store(rest, 1, empty)
            store(rest, 2, empty)
    for hh in range(2):
        if spatial:
            fold_bias_sp(db_ref.at[hh], dm_ref, hh)
        else:
            fold_bias_st(db_ref.at[hh], dm_ref, hh)


def attention_shapes(spatial, tokens):
    n_query = SWIN * SWIN if spatial else FRAMES * TWIN * TWIN
    n_key = n_query if spatial else KEYF * TWIN * TWIN
    return tokens // n_query, n_query, n_key, n_query


ROWS = 64
COLS = 1024
MESH = pl.DeviceIdType.MESH


def place(n_clip):
    clip = lax.axis_index("clip")
    x = lax.axis_index("frame")
    z = clip // 4
    y = lax.rem(clip // 2, 2)
    c = lax.rem(clip, 2)
    return clip, z, y, c, x


def remote(src, dst, send, recv, clip, frame):
    return pltpu.make_async_remote_copy(
        src_ref=src,
        dst_ref=dst,
        send_sem=send,
        recv_sem=recv,
        device_id={"clip": clip, "frame": frame},
        device_id_type=MESH,
    )


def greet(targets):
    barrier = pltpu.get_barrier_semaphore()
    count = 0
    for clip, frame, valid in targets:
        if valid is None:
            pl.semaphore_signal(barrier, inc=1, device_id={"clip": clip, "frame": frame}, device_id_type=MESH)
            count = count + 1
        else:
            @pl.when(valid)
            def _():
                pl.semaphore_signal(barrier, inc=1, device_id={"clip": clip, "frame": frame}, device_id_type=MESH)
            count = count + valid.astype(jnp.int32)
    pl.semaphore_wait(barrier, count)


GATHER_TAIL = 6


def gather_tick(t, n, nz, where, wide, shard, full, local, up_s, up_r, dn_s, dn_r, y_s, y_r, x_s, x_r, c_s, c_r):
    clip, z, y, c, x = where
    last = nz - 1
    steps = nz - 1

    def phases(i, hi):
        lo = COLS - hi
        fetch = pl.ds(pl.multiple_of(x * lo, 128), hi)
        give = pl.ds(pl.multiple_of(x * hi, 128), lo)

        def own():
            return pltpu.make_async_copy(
                shard.at[i, :, fetch], full.at[i, z, y, c, :, fetch], local.at[i]
            )

        def up(s, origin):
            src = shard.at[i, :, fetch] if s == 0 else full.at[i, origin, y, c, :, fetch]
            return remote(src, full.at[i, origin, y, c, :, fetch], up_s.at[s, i], up_r.at[s, i], clip + 4, x)

        def down(s, origin):
            src = shard.at[i, :, fetch] if s == 0 else full.at[i, origin, y, c, :, fetch]
            return remote(src, full.at[i, origin, y, c, :, fetch], dn_s.at[s, i], dn_r.at[s, i], clip - 4, x)

        def over_y():
            src = full.at[i, :, y, c, :, fetch]
            return remote(src, src, y_s.at[i], y_r.at[i], clip + 2 - 4 * y, x)

        def over_x():
            src = full.at[i, :, :, c, :, give]
            return remote(src, src, x_s.at[i], x_r.at[i], clip, 1 - x)

        def over_c():
            src = full.at[i, :, :, c]
            return remote(src, src, c_s.at[i], c_r.at[i], clip + 1 - 2 * c, x)

        def z_wait(s):
            @pl.when(z - 1 - s >= 0)
            def _():
                up(s, z - 1 - s).wait_recv()

            @pl.when(z + 1 + s <= last)
            def _():
                down(s, z + 1 + s).wait_recv()

        def z_start(s):
            @pl.when(jnp.logical_and(z < last, z - s >= 0))
            def _():
                up(s, z - s).start()

            @pl.when(jnp.logical_and(z > 0, z + s <= last))
            def _():
                down(s, z + s).start()

        def z_sent(s):
            @pl.when(jnp.logical_and(z < last, z - s >= 0))
            def _():
                up(s, z - s).wait_send()

            @pl.when(jnp.logical_and(z > 0, z + s <= last))
            def _():
                down(s, z + s).wait_send()

        def first():
            own().start()
            z_start(0)

        def along(s):
            z_wait(s - 1)
            z_start(s)

        def to_y():
            z_wait(steps - 1)
            own().wait()
            over_y().start()

        def to_x():
            over_y().wait_recv()
            over_x().start()

        def to_c():
            over_x().wait_recv()
            over_c().start()

        def finish():
            over_c().wait_recv()
            for s in range(steps):
                z_sent(s)
            over_y().wait_send()
            over_x().wait_send()
            over_c().wait_send()

        mids = [functools.partial(along, s) for s in range(1, steps)]
        return [first] + mids + [to_y, to_x, to_c, finish]

    for k in range(steps + 4):
        i = t - k
        valid = jnp.logical_and(i >= 0, i < n)
        larger = lax.rem(i + 3, 3) < wide
        for hi, chosen in ((640, jnp.logical_not(larger)), (768, larger)):
            @pl.when(jnp.logical_and(valid, chosen))
            def _(i=i, hi=hi, k=k):
                phases(i, hi)[k]()


def greet_gather(nz, where):
    clip, z, y, c, x = where
    greet([
        (clip + 4, x, z < nz - 1),
        (clip - 4, x, z > 0),
        (clip + 2 - 4 * y, x, None),
        (clip, 1 - x, None),
        (clip + 1 - 2 * c, x, None),
    ])


def gather_sems(n, nz):
    dma = pltpu.SemaphoreType.DMA
    z = dma((nz - 1, n))
    one = dma((n,))
    return [one, z, z, z, z, one, one, one, one, one, one]


NBUF = 3
REDUCE_TAIL = 7
Y_FIRST = 640
NACC = 4


def reduce_tick(t, n, nz, where, sources, out, acc, cbuf, ya, xa, yb, xb, tb, zb, sb, fb, ob,
                loc, c_s, c_r, ya_s, ya_r, xa_s, xa_r, yb_s, yb_r, xb_s, xb_r, z_s, z_r, f_s, f_r, o_s,
                cred_c, cred_y, cred_x, cred_z, cred_f):
    clip, z, y, c, x = where
    half = ROWS // 2
    peer_c = clip + 1 - 2 * c
    peer_y = clip + 2 - 4 * y
    mine = pl.ds(pl.multiple_of(x * half, half), half)
    theirs = pl.ds(pl.multiple_of((1 - x) * half, half), half)
    left = pl.ds(0, Y_FIRST)
    right = pl.ds(Y_FIRST, COLS - Y_FIRST)

    def slot(i):
        return lax.rem(i, NBUF)

    def aslot(i):
        return lax.rem(i, NACC)

    def load(i, source, first):
        return pltpu.make_async_copy(source.at[i - first, :, :, c], acc.at[aslot(i)], loc.at[slot(i)])

    def over_c(i, source, first):
        src = source.at[i - first, :, :, 1 - c]
        return remote(src, cbuf.at[slot(i)], c_s.at[slot(i)], c_r.at[slot(i)], peer_c, x)

    def over_ya(i):
        return remote(acc.at[aslot(i), :, 1 - y, :, left], ya.at[slot(i)], ya_s.at[slot(i)], ya_r.at[slot(i)], peer_y, x)

    def over_xa(i):
        return remote(acc.at[aslot(i), :, :, theirs, right], xa.at[slot(i)], xa_s.at[slot(i)], xa_r.at[slot(i)], clip, 1 - x)

    def over_xb(i):
        return remote(acc.at[aslot(i), :, y, theirs, left], xb.at[slot(i)], xb_s.at[slot(i)], xb_r.at[slot(i)], clip, 1 - x)

    def over_yb(i):
        return remote(acc.at[aslot(i), :, 1 - y, mine, right], yb.at[slot(i)], yb_s.at[slot(i)], yb_r.at[slot(i)], peer_y, x)

    def over_z(i, k):
        to = lax.rem(z + k, nz)
        return remote(tb.at[slot(i), to], zb.at[slot(i), k - 1], z_s.at[slot(i), k - 1], z_r.at[slot(i), k - 1],
                      clip + 4 * (to - z), x)

    def over_f(i):
        return remote(sb.at[slot(i)], fb.at[slot(i)], f_s.at[slot(i)], f_r.at[slot(i)], clip, 1 - x)

    def write(i):
        return pltpu.make_async_copy(ob.at[slot(i)], out.at[i], o_s.at[slot(i)])

    def credit(sem, who, frame, i):
        @pl.when(i + NBUF < n)
        def _():
            pl.semaphore_signal(sem, inc=1, device_id={"clip": who, "frame": frame}, device_id_type=MESH)

    def need(sem, i):
        @pl.when(i >= NBUF)
        def _():
            pl.semaphore_wait(sem, 1)

    def item(i):
        return jnp.logical_and(i >= 0, i < n)

    i = t - 6

    @pl.when(item(i))
    def _(i=i):
        write(i).wait()

    i = t

    @pl.when(item(i))
    def _(i=i):
        need(cred_c, i)
        first = 0
        for source, skip, count in sources:

            @pl.when(jnp.logical_and(i >= first, i < first + count))
            def _(source=source, offset=first - skip):
                over_c(i, source, offset).start()
                load(i, source, offset).start()

            first += count

    i = t - 1

    @pl.when(item(i))
    def _(i=i):
        over_c(i, sources[0][0], i).wait()
        load(i, sources[0][0], i).wait()
        a, b = aslot(i), slot(i)

        def body(k, carry):
            acc[a, k] = acc[a, k] + cbuf[b, k]
            return carry

        lax.fori_loop(0, nz, body, 0)
        credit(cred_c, peer_c, x, i)
        need(cred_y, i)
        need(cred_x, i)
        over_ya(i).start()
        over_xa(i).start()

    i = t - 2

    @pl.when(item(i))
    def _(i=i):
        over_ya(i).wait()
        over_xa(i).wait()
        a, b = aslot(i), slot(i)

        def body(k, carry):
            acc[a, k, y, :, left] = acc[a, k, y, :, left] + ya[b, k]
            acc[a, k, :, mine, right] = acc[a, k, :, mine, right] + xa[b, k]
            return carry

        lax.fori_loop(0, nz, body, 0)
        over_xb(i).start()
        over_yb(i).start()

    i = t - 3

    @pl.when(item(i))
    def _(i=i):
        over_xb(i).wait()
        over_yb(i).wait()
        a, b = aslot(i), slot(i)

        def body(k, carry):
            tb[b, k, :, left] = acc[a, k, y, mine, left] + xb[b, k]
            tb[b, k, :, right] = acc[a, k, y, mine, right] + yb[b, k]
            return carry

        lax.fori_loop(0, nz, body, 0)
        credit(cred_y, peer_y, x, i)
        credit(cred_x, clip, 1 - x, i)
        for k in range(1, nz):
            need(cred_z.at[k - 1], i)
            over_z(i, k).start()

    i = t - 4

    @pl.when(item(i))
    def _(i=i):
        for k in range(1, nz):
            over_z(i, k).wait()
        b = slot(i)
        total = tb[b, z].astype(F32)
        for k in range(1, nz):
            total = total + zb[b, k - 1].astype(F32)
        sb[b] = total.astype(BF16)
        for k in range(1, nz):
            sender = lax.rem(z + nz - k, nz)
            credit(cred_z.at[k - 1], clip + 4 * (sender - z), x, i)
        need(cred_f, i)
        over_f(i).start()

    i = t - 5

    @pl.when(item(i))
    def _(i=i):
        over_f(i).wait()
        b = slot(i)
        ob[b, mine, :] = sb[b].astype(F32)
        ob[b, theirs, :] = fb[b].astype(F32)
        credit(cred_f, clip, 1 - x, i)
        write(i).start()


def greet_reduce(nz, where):
    clip, z, y, c, x = where
    others = [(clip + 4 * (lax.rem(z + k, nz) - z), x, None) for k in range(1, nz)]
    greet(others + [
        (clip + 2 - 4 * y, x, None),
        (clip, 1 - x, None),
        (clip + 1 - 2 * c, x, None),
    ])


def exchange_tick(t, nz, where, small, totals, boxes, mod_box, sems):
    clip, z, y, c, x = where
    steps = [(clip, 1 - x), (clip + 1 - 2 * c, x), (clip + 2 - 4 * y, x)]
    bit = 1
    while bit < nz:
        flip = lax.rem(z // bit, 2)
        steps.append((clip + 4 * bit * (1 - 2 * flip), x))
        bit *= 2

    def copies(k):
        to, frame = steps[k]
        found = [
            remote(boxes[j].at[k, 0], boxes[j].at[k, 1], sems.at[j, 0, k], sems.at[j, 1, k], to, frame)
            for j in range(2)
        ]
        if k == 0:
            found.append(remote(small[0], mod_box, sems.at[2, 0, 0], sems.at[2, 1, 0], to, frame))
        return found

    for k in range(len(steps)):
        @pl.when(t == k + 1)
        def _(k=k):
            for copy in copies(k):
                copy.wait()
            for j in range(2):
                totals[1 + j][...] = boxes[j][k, 0].astype(F32) + boxes[j][k, 1].astype(F32)
            if k == 0:
                totals[0][...] = small[0][...] + mod_box[...]

        @pl.when(t == k)
        def _(k=k):
            for j in range(2):
                source = small[1 + j] if k == 0 else totals[1 + j]
                boxes[j][k, 0] = source[...].astype(BF16)
            for copy in copies(k):
                copy.start()


def exchange_steps(nz):
    return 3 + (nz - 1).bit_length()


def reduce_kernel(pick, nz, grads, small0, small1, small2, out, total0, total1, total2, *rest):
    n_comm = len(reduce_scratch(nz))
    comm, (box0, box1, mod_box, sems) = rest[:n_comm], rest[n_comm:]
    skip, n = pick
    where = place(4 * nz)
    clip, z, y, c, x = where
    greet_reduce(nz, where)

    def step(t, carry):
        exchange_tick(
            t, nz, where, (small0, small1, small2), (total0, total1, total2), (box0, box1), mod_box, sems
        )
        reduce_tick(t, n, nz, where, [(grads, skip, n)], out, *comm)
        return carry

    lax.fori_loop(0, n + REDUCE_TAIL, step, 0)


def reduce_scratch(nz):
    half = ROWS // 2
    rest = COLS - Y_FIRST
    dma = pltpu.SemaphoreType.DMA
    one = dma((NBUF,))
    regular = pltpu.SemaphoreType.REGULAR
    return [
        pltpu.VMEM((NACC, nz, 2, ROWS, COLS), BF16),
        pltpu.VMEM((NBUF, nz, 2, ROWS, COLS), BF16),
        pltpu.VMEM((NBUF, nz, ROWS, Y_FIRST), BF16),
        pltpu.VMEM((NBUF, nz, 2, half, rest), BF16),
        pltpu.VMEM((NBUF, nz, half, rest), BF16),
        pltpu.VMEM((NBUF, nz, half, Y_FIRST), BF16),
        pltpu.VMEM((NBUF, nz, half, COLS), BF16),
        pltpu.VMEM((NBUF, nz - 1, half, COLS), BF16),
        pltpu.VMEM((NBUF, half, COLS), BF16),
        pltpu.VMEM((NBUF, half, COLS), BF16),
        pltpu.VMEM((NBUF, ROWS, COLS), F32),
        one, one, one, one, one, one, one, one, one, one, one,
        dma((NBUF, nz - 1)), dma((NBUF, nz - 1)),
        one, one, one,
        regular, regular, regular, regular((nz - 1,)), regular,
    ]


def reduce_last(grads, pick, small, nz, cid):
    n = pick[1]
    steps = exchange_steps(nz)
    vmem = pl.BlockSpec(memory_space=pltpu.VMEM)
    return pl.pallas_call(
        functools.partial(reduce_kernel, pick, nz),
        out_shape=[jax.ShapeDtypeStruct((n, ROWS, COLS), F32)]
        + [jax.ShapeDtypeStruct(v.shape, F32) for v in small],
        in_specs=[pl.BlockSpec(memory_space=pl.ANY), vmem, vmem, vmem],
        out_specs=[pl.BlockSpec(memory_space=pl.ANY), vmem, vmem, vmem],
        scratch_shapes=reduce_scratch(nz)
        + [pltpu.VMEM((steps, 2) + v.shape, BF16) for v in small[1:]]
        + [pltpu.VMEM(small[0].shape, F32), pltpu.SemaphoreType.DMA((3, 2, steps))],
        compiler_params=pltpu.CompilerParams(
            collective_id=cid, has_side_effects=True, vmem_limit_bytes=48 * 1024 * 1024
        ),
        name="reduce_last",
    )(grads, *small)


CHUNK = 512
STEP_ROWS = 128
MIB = 1024 * 1024
GELU_C = 0.7978845608028654
GELU_A = 0.044715


def fixed(shape, **kw):
    zeros = (0,) * len(shape)
    return pl.BlockSpec(shape, lambda i: zeros, pipeline_mode=pl.Buffered(1), **kw)


def over_rows(tokens, body):
    def step(k, carry):
        body(pl.ds(pl.multiple_of(k * STEP_ROWS, STEP_ROWS), STEP_ROWS))
        return carry

    lax.fori_loop(0, tokens // STEP_ROWS, step, 0)


def down_rows(w_ref):
    groups = w_ref.shape[1] // ROWS
    return jnp.concatenate(
        [w_ref[s, c * ROWS : (c + 1) * ROWS, :] for c in range(groups) for s in range(2)], axis=0
    )


FRONT_ROWS = 256
GATHER_US = 6.0


def forward_plan(tokens, width):
    rows = tokens // FRONT_ROWS
    sizes = (rows, 3, width // 128, 1, rows, 4, rows)
    starts = [0]
    for size in sizes:
        starts.append(starts[-1] + size)
    return starts


def plan_gather(starts, spatial, need, n_items, nz):
    takes = (1.0, 2.6, 1.9 if spatial else 3.6, 2.2, 1.3, 6.5, 0.8)
    total = n_items + nz + 2
    counts, done, clock, last = [], 0, 0.0, -GATHER_US
    for section, (lo, hi) in enumerate(zip(starts, starts[1:])):
        for step in range(lo, hi):
            before = done
            while done < total and (done < need.get(step, 0) or clock - last >= GATHER_US):
                early = 3.0 if done < 6 else GATHER_US
                clock = max(clock, last + early)
                last = clock
                done += 1
            counts.append(done - before)
            clock += takes[section]
    return counts, total


def forward_body(
    spatial, shapes, wide, n_own, own_first, counts, total, nz,
    s_ref, m_ref, b_ref, ok_ref, shard_hbm, prev_hbm,
    na_ref, qkv_ref, att_ref, p_ref, proj_ref, mid_ref, nm_ref, act_ref, dact_ref, down_ref, res_ref, full_hbm, peer_hbm,
    n_scr, q_scr, a_scr, acc_ref, mid_scr, bias_ref, w_scr, d_scr, w_sem, d_sem, send_ref, send_sem, peer_sem, *sems,
):
    n_win, n_query, n_key, chunk = shapes
    tokens, width = acc_ref.shape
    starts = forward_plan(tokens, width)
    a0, a1, a2, a3, a4, a5, a6, end = starts
    step = pl.program_id(0)
    where = place(4 * nz)

    @pl.when(step == 0)
    def _():
        greet_gather(nz, where)

    lo = jnp.zeros((), jnp.int32)
    hi = jnp.zeros((), jnp.int32)
    for s, count in enumerate(counts):
        if count:
            lo = lo + count * (step > s).astype(jnp.int32)
            hi = hi + count * (step >= s).astype(jnp.int32)

    def tick(t, carry):
        gather_tick(t, n_own, nz, where, wide, shard_hbm, full_hbm, *sems)
        return carry

    lax.fori_loop(lo, hi, tick, 0)

    def item_ref(item):
        if item >= own_first:
            return full_hbm.at[item - own_first]
        return prev_hbm.at[PREV_ITEMS + item]

    ready = []
    done = 0
    for count in counts:
        done += count
        ready.append(done)

    def start_of(item, use):
        if item < own_first:
            return max(use - 1, 0)
        for s in range(max(use - 1, 0), use + 1):
            if ready[s] >= item - own_first + nz + 3:
                return s
        raise ValueError("late item")

    jobs = []
    uses = [(a1, 0), (a1 + 1, 1), (a1 + 2, 2), (a3, 3)] + [(a5 + i, UP_ITEMS[i]) for i in range(4)]
    for k, (use, item) in enumerate(uses):
        copy = pltpu.make_async_copy(item_ref(item), w_scr.at[k % 2], w_sem.at[k % 2])
        jobs.append((start_of(item, use), use, copy))
    for i in range(4):
        items = (DOWN_ITEMS[2 * (i // 2)], DOWN_ITEMS[2 * (i // 2) + 1])
        first = max(start_of(item, a5 + i) for item in items)
        for k, item in enumerate(items):
            source = item_ref(item).at[pl.ds((nz // 2) * (i % 2), nz // 2)]
            copy = pltpu.make_async_copy(source, d_scr.at[i % 2, k], d_sem.at[i % 2, k])
            jobs.append((first, a5 + i, copy))
    for first, use, copy in jobs:
        @pl.when(step == first)
        def _(copy=copy):
            copy.start()
    for first, use, copy in jobs:
        @pl.when(step == use)
        def _(copy=copy):
            copy.wait()

    def weight(k):
        return w_scr[k].reshape(width, width)

    def rows_at(i):
        return pl.ds(pl.multiple_of(i * FRONT_ROWS, FRONT_ROWS), FRONT_ROWS)

    @pl.when(step < a1)
    def _():
        normed, _ = norm_stats(s_ref[...].astype(F32))
        value = (normed * (1.0 + m_ref[1:2, :]) + m_ref[0:1, :]).astype(BF16)
        n_scr[rows_at(step), :] = value
        na_ref[...] = value

    @pl.when(jnp.logical_and(step >= a1, step < a2))
    def _():
        i = step - a1
        value = dot_nn(n_scr[...], weight(lax.rem(i, 2))).astype(BF16)
        q_scr[:, pl.ds(pl.multiple_of(i * width, width), width)] = value
        qkv_ref[...] = value

    @pl.when(jnp.logical_and(step >= a2, step < a3))
    def _():
        def lanes(k):
            return q_scr.at[:, pl.ds(pl.multiple_of(k * width + (step - a2) * 128, 128), 128)]

        attend_forward(
            spatial, n_win, n_query, n_key, chunk, lanes(0), lanes(1), lanes(2), b_ref, ok_ref, att_ref, p_ref, bias_ref
        )
        a_scr[:, pl.ds(pl.multiple_of((step - a2) * 128, 128), 128)] = att_ref[...]

    @pl.when(step == a3)
    def _():
        acc_ref[...] = dot_nn(a_scr[...], weight(1))

    @pl.when(jnp.logical_and(step >= a4, step < a5))
    def _():
        rows = rows_at(step - a4)
        proj = acc_ref[rows, :]
        proj_ref[...] = proj.astype(BF16)
        mid = s_ref[...].astype(F32) + m_ref[2:3, :] * proj
        mid_ref[...] = mid
        mid_scr[rows, :] = mid
        normed, _ = norm_stats(mid)
        value = (normed * (1.0 + m_ref[4:5, :]) + m_ref[3:4, :]).astype(BF16)
        n_scr[rows, :] = value
        nm_ref[...] = value

    @pl.when(jnp.logical_and(step >= a5, step < a6))
    def _():
        i = step - a5
        slot = lax.rem(i, 2)
        w_up = weight(slot)
        first = d_scr[slot, 0].reshape(-1, ROWS, width)
        second = d_scr[slot, 1].reshape(-1, ROWS, width)
        w_down = jnp.concatenate(
            [part for k in range(first.shape[0]) for part in (first[k], second[k])], axis=0
        )
        pieces = 4
        each = tokens // pieces
        ups = [dot_nn(n_scr[k * each : (k + 1) * each, :], w_up) for k in range(pieces)]
        for k in range(pieces):
            rows = slice(k * each, (k + 1) * each)
            up = ups[k]
            square = up * up
            tanh = jnp.tanh(up * (GELU_C + (GELU_C * GELU_A) * square))
            half = 0.5 + 0.5 * tanh
            act = up * half
            dact_ref[rows, :] = (
                half + act * (1.0 - tanh) * (GELU_C + (3.0 * GELU_C * GELU_A) * square)
            ).astype(BF16)
            act = act.astype(BF16)
            act_ref[rows, :] = act
            acc_ref[rows, :] = jnp.where(i == 0, 0.0, acc_ref[rows, :]) + dot_nn(act, w_down)

    @pl.when(step >= a6)
    def _():
        rows = rows_at(step - a6)
        down = acc_ref[rows, :]
        down_ref[...] = down.astype(BF16)
        res_ref[...] = (mid_scr[rows, :] + m_ref[5:6, :] * down).astype(res_ref.dtype)

    clip, _, _, _, x = where

    def to_peer(k):
        return remote(send_ref.at[k], peer_hbm.at[k], send_sem.at[k], peer_sem.at[k], clip, 1 - x)

    if spatial:
        @pl.when(step >= a6)
        def _():
            half = FRONT_ROWS // 2
            theirs = pl.ds(pl.multiple_of((1 - x) * half, half), half)
            send_ref[step - a6] = res_ref[theirs, :].astype(BF16)
            to_peer(step - a6).start()

    @pl.when(step == end - 1)
    def _():
        lax.fori_loop(sum(counts), total, tick, 0)
        if spatial:
            for k in range(send_ref.shape[0]):
                to_peer(k).wait()


DOWN_ITEMS = (4, 5, 8, 9)
UP_ITEMS = (6, 7, 10, 11)
PREV_ITEMS = 12


def block_forward(stream, mods, shard, wide, n_own, prev, own_first, spread, key_ok, spatial, result_type, nz, cid):
    tokens, width = stream.shape
    shapes = attention_shapes(spatial, tokens)
    n_win, n_query, n_key, _ = shapes
    pairs = width // 128
    a0, a1, a2, a3, a4, a5, a6, end = starts = forward_plan(tokens, width)
    n_send = tokens // FRONT_ROWS
    tail = spread.shape[1:]
    zeros = (0,) * len(tail)
    need = {}
    for i in range(3):
        need[a1 + i] = i
    need[a3] = 3
    for i in range(4):
        need[a5 + i] = max(UP_ITEMS[i], DOWN_ITEMS[2 * (i // 2) + 1])
    need = {s: item - own_first + nz + 3 for s, item in need.items() if item >= own_first}
    counts, total = plan_gather(starts, spatial, need, n_own, nz)

    def at(start, stop):
        return lambda i: jnp.clip(i - start, 0, stop - start - 1)

    def row_block(place_of):
        return pl.BlockSpec((FRONT_ROWS, width), lambda i: (place_of(i), 0))

    def s_at(i):
        return jnp.where(i < a1, i, at(a4, a5)(i))

    heads = at(a2, a3)
    anywhere = pl.BlockSpec(memory_space=pl.ANY)
    hidden = pl.BlockSpec((tokens, width), lambda i: (0, at(a5, a6)(i)))
    body = functools.partial(forward_body, spatial, shapes, wide, n_own, own_first, counts, total, nz)
    extra = [] if prev is None else [prev]
    if prev is None:
        whole = body

        def body(*refs):
            return whole(*refs[:5], None, *refs[5:])

    dma = pltpu.SemaphoreType.DMA
    bf16_rows = jax.ShapeDtypeStruct((tokens, width), BF16)
    outs = pl.pallas_call(
        body,
        grid=(end,),
        in_specs=[
            row_block(s_at),
            fixed(mods.shape),
            pl.BlockSpec((2,) + tail, lambda i: (heads(i),) + zeros),
            pl.BlockSpec((n_win, 1, n_key), lambda i: (0, 0, 0)),
            anywhere,
        ] + [anywhere] * len(extra),
        out_specs=[
            row_block(at(a0, a1)),
            pl.BlockSpec((tokens, width), lambda i: (0, at(a1, a2)(i))),
            pl.BlockSpec((tokens, 128), lambda i: (0, heads(i))),
            pl.BlockSpec((2, n_win, n_query, n_key), lambda i: (heads(i), 0, 0, 0)),
            row_block(at(a4, a5)),
            row_block(at(a4, a5)),
            row_block(at(a4, a5)),
            hidden,
            hidden,
            row_block(at(a6, end)),
            row_block(at(a6, end)),
            anywhere,
            anywhere,
        ],
        out_shape=[
            bf16_rows,
            jax.ShapeDtypeStruct((tokens, 3 * width), BF16),
            bf16_rows,
            jax.ShapeDtypeStruct((2 * pairs, n_win, n_query, n_key), BF16),
            bf16_rows,
            jax.ShapeDtypeStruct((tokens, width), F32),
            bf16_rows,
            jax.ShapeDtypeStruct((tokens, 4 * width), BF16),
            jax.ShapeDtypeStruct((tokens, 4 * width), BF16),
            bf16_rows,
            jax.ShapeDtypeStruct((tokens, width), result_type),
            jax.ShapeDtypeStruct((n_own, nz, 2, 2, ROWS, COLS), BF16),
            jax.ShapeDtypeStruct((n_send, FRONT_ROWS // 2, width), BF16),
        ],
        scratch_shapes=[
            pltpu.VMEM((tokens, width), BF16),
            pltpu.VMEM((tokens, 3 * width), BF16),
            pltpu.VMEM((tokens, width), BF16),
            pltpu.VMEM((tokens, width), F32),
            pltpu.VMEM((tokens, width), F32),
            pltpu.VMEM((2, n_query, n_key), F32),
            pltpu.VMEM((2, nz, 2, 2, ROWS, COLS), BF16),
            pltpu.VMEM((2, 2, nz // 2, 2, 2, ROWS, COLS), BF16),
            dma((2,)),
            dma((2, 2)),
            pltpu.VMEM((n_send, FRONT_ROWS // 2, width), BF16),
            dma((n_send,)),
            dma((n_send,)),
        ] + gather_sems(n_own, nz),
        compiler_params=pltpu.CompilerParams(
            collective_id=cid, has_side_effects=True, vmem_limit_bytes=64 * MIB
        ),
        name="block_forward",
    )(stream, mods, spread, key_ok, shard, *extra)
    normed_a, qkv, att, probs, proj, mid, normed_m, act, dact, down, result, full, peer = outs
    saved = (stream, normed_a, qkv, probs, att, proj, mid, normed_m, act, dact, down)
    return result, saved, full, peer


def norm_back_rows(values, scale_row, grad):
    normed, inv = norm_stats(values)
    u = grad * (1.0 + scale_row)
    out = (
        u
        - jnp.mean(u, axis=-1, keepdims=True)
        - normed * jnp.mean(u * normed, axis=-1, keepdims=True)
    ) * inv
    return out, jnp.sum(grad, axis=0, keepdims=True), jnp.sum(grad * normed, axis=0, keepdims=True)


BLOCK_ROWS = 128
TICK_US = (5.5, 6.5)


def backward_plan(tokens, width):
    rows = tokens // BLOCK_ROWS
    chunks = 4 * width // CHUNK
    halves = width // CHUNK
    pairs = width // 128
    sizes = (rows, chunks, rows, halves, pairs, 3 * halves, rows, 3 * halves)
    starts = [0]
    for size in sizes:
        starts.append(starts[-1] + size)
    return starts


def backward_body(
    spatial, shapes, n_prev, n_own, tick_steps, nz,
    g_ref, down_ref, mid_ref, proj_ref, s_ref, m_ref, act_ref, dact_ref, w_ref, up_ref, dn_ref,
    q_ref, k_ref, v_ref, p_ref, nm_hbm, att_hbm, na_hbm, mixed_hbm, prev_hbm,
    out_ref, dm_ref, rows_ref, grads_hbm, share_hbm, peer_hbm, swap_hbm,
    res_ref, gv_ref, e_ref, gm_ref, ga_ref, gq_ref, db_ref, gdb_ref, gub_ref,
    res_sem, gd_sem, gu_sem, send_ref, send_sem, peer_sem, mix_sem, swap_sem, *comm,
):
    n_win, n_query, n_key, chunk = shapes
    tokens, width = e_ref.shape
    starts = backward_plan(tokens, width)
    a0, a1, a2, a3, a4, a5, a6, a7, end = starts
    halves = width // CHUNK
    step = pl.program_id(0)
    where = place(4 * nz)
    n_items = n_prev + n_own
    sources = [(prev_hbm, 9, n_prev)] if n_prev else []
    sources.append((grads_hbm, 0, n_own))

    @pl.when(step == 0)
    def _():
        greet_reduce(nz, where)

    def tick(t):
        reduce_tick(t, n_items, nz, where, sources, share_hbm, *comm)

    due = jnp.zeros((), jnp.bool_)
    passed = jnp.zeros((), jnp.int32)
    for s in tick_steps:
        due = jnp.logical_or(due, step == s)
        passed = passed + (step > s).astype(jnp.int32)

    def resident(source):
        return pltpu.make_async_copy(source, res_ref, res_sem)

    def put_down(i):
        slot = lax.rem(i, 2)
        target = grads_hbm.at[pl.ds(4 * (i // 4) + 2, 2), pl.ds(lax.rem(i, 4), 1)]
        return pltpu.make_async_copy(gdb_ref.at[slot], target, gd_sem.at[slot])

    def put_cols(i, item, half):
        slot = lax.rem(i, 2)
        cols = pl.ds(pl.multiple_of(half * CHUNK, CHUNK), CHUNK)
        target = grads_hbm.at[item, :, :, :, :, cols]
        return pltpu.make_async_copy(gub_ref.at[slot], target, gu_sem.at[slot])

    def keep_cols(i, values):
        gub_ref[lax.rem(i, 2)] = values.reshape(gub_ref.shape[1:])

    def rows_at(i):
        return pl.ds(pl.multiple_of(i * BLOCK_ROWS, BLOCK_ROWS), BLOCK_ROWS)

    def add_e(first, left, right):
        part = tokens // 2
        for k in range(2):
            rows = slice(k * part, (k + 1) * part)
            value = dot_nt(left[rows], right)

            @pl.when(first)
            def _(rows=rows, value=value):
                e_ref[rows, :] = value

            @pl.when(jnp.logical_not(first))
            def _(rows=rows, value=value):
                e_ref[rows, :] += value

    @pl.when(step == 0)
    def _():
        resident(nm_hbm).start()
        rows_ref[...] = jnp.zeros_like(rows_ref)

    @pl.when(step < a1)
    def _():
        grad = g_ref[...].astype(F32)
        gv_ref[rows_at(step), :] = (m_ref[5:6, :] * grad).astype(BF16)
        rows_ref[5:6, :] += jnp.sum(grad * down_ref[...].astype(F32), axis=0, keepdims=True)

    @pl.when(step == a1)
    def _():
        resident(nm_hbm).wait()

    @pl.when(jnp.logical_and(step >= a1, step < a2))
    def _():
        i = step - a1

        @pl.when(i >= 2)
        def _():
            put_down(i).wait()
            put_cols(i, 4, 0).wait()

        gdv = gv_ref[...]
        grad_act = dot_nt(gdv, down_rows(dn_ref))
        gup = (grad_act * dact_ref[...].astype(F32)).astype(BF16)
        slot = lax.rem(i, 2)
        grad_down = dot_tn(act_ref[...], gdv).astype(BF16)
        for k in range(CHUNK // ROWS):
            gdb_ref[slot, k % 2, 0, k // 4, (k // 2) % 2] = grad_down[k * ROWS : (k + 1) * ROWS, :]
        put_down(i).start()
        keep_cols(i, dot_tn(res_ref[...], gup).astype(BF16))
        put_cols(i, 4 * (i // 4) + lax.rem(i // 2, 2), lax.rem(i, halves)).start()
        add_e(i == 0, gup, up_ref[0])

    @pl.when(step == a2)
    def _():
        resident(att_hbm).start()
        for k in range(2):
            put_down(k).wait()
            put_cols(k, 4, 0).wait()

    @pl.when(jnp.logical_and(step >= a2, step < a3))
    def _():
        rows = rows_at(step - a2)
        out, shift, scale = norm_back_rows(mid_ref[...], m_ref[4:5, :], e_ref[rows, :])
        grad_mid = out + g_ref[...].astype(F32)
        gm_ref[rows, :] = grad_mid
        gv_ref[rows, :] = (m_ref[2:3, :] * grad_mid).astype(BF16)
        rows_ref[3:4, :] += shift
        rows_ref[4:5, :] += scale
        rows_ref[2:3, :] += jnp.sum(grad_mid * proj_ref[...].astype(F32), axis=0, keepdims=True)

    @pl.when(step == a3)
    def _():
        resident(att_hbm).wait()

    @pl.when(jnp.logical_and(step >= a3, step < a4))
    def _():
        i = step - a3
        part = gv_ref[:, pl.ds(pl.multiple_of(i * CHUNK, CHUNK), CHUNK)]
        keep_cols(i, dot_tn(res_ref[...], part).astype(BF16))
        put_cols(i, 8, i).start()
        add_e(i == 0, part, w_ref[0])

    @pl.when(step == a4)
    def _():
        resident(na_hbm).start()
        ga_ref[...] = e_ref[...].astype(BF16)
        for k in range(2):
            put_cols(k, 8, 0).wait()

    @pl.when(jnp.logical_and(step >= a4, step < a5))
    def _():
        head = step - a4
        lanes = pl.ds(pl.multiple_of(head * 128, 128), 128)
        attend_backward(
            spatial, n_win, n_query, n_key, chunk, head,
            q_ref, k_ref, v_ref, ga_ref.at[:, lanes], p_ref, gq_ref, dm_ref, db_ref,
        )

    @pl.when(jnp.logical_and(step >= a5, step < a6))
    def _():
        i = step - a5
        add_e(i == 0, gq_ref[:, pl.ds(pl.multiple_of(i * CHUNK, CHUNK), CHUNK)], w_ref[0])

    clip, _, _, _, x = where

    def to_peer(k):
        return remote(send_ref.at[k], peer_hbm.at[k], send_sem.at[k], peer_sem.at[k], clip, 1 - x)

    def mixed_to_peer(k):
        block = 4 * (k // 2) + 2 * (1 - x) + k % 2
        rows = pl.ds(pl.multiple_of(block * BLOCK_ROWS, BLOCK_ROWS), BLOCK_ROWS)
        return remote(mixed_hbm.at[rows], swap_hbm.at[k], mix_sem.at[k], swap_sem.at[k], clip, 1 - x)

    if not spatial:
        @pl.when(step == 0)
        def _():
            for k in range(send_ref.shape[0]):
                mixed_to_peer(k).start()

    @pl.when(jnp.logical_and(step >= a6, step < a7))
    def _():
        rows = rows_at(step - a6)
        out, shift, scale = norm_back_rows(s_ref[...].astype(F32), m_ref[1:2, :], e_ref[rows, :])
        out_ref[...] = (out + gm_ref[rows, :]).astype(out_ref.dtype)
        rows_ref[0:1, :] += shift
        rows_ref[1:2, :] += scale

    if not spatial:
        block = step - a6
        half = lax.rem(block, 4) // 2

        @pl.when(jnp.logical_and(jnp.logical_and(step >= a6, step < a7), half == 1 - x))
        def _():
            k = 2 * (block // 4) + lax.rem(block, 2)
            send_ref[k] = out_ref[...].astype(BF16)
            to_peer(k).start()

    @pl.when(step == a7)
    def _():
        resident(na_hbm).wait()

    @pl.when(step >= a7)
    def _():
        i = step - a7

        @pl.when(i >= 2)
        def _():
            put_cols(i, 8, 0).wait()

        part = gq_ref[:, pl.ds(pl.multiple_of(i * CHUNK, CHUNK), CHUNK)]
        keep_cols(i, dot_tn(res_ref[...], part).astype(BF16))
        put_cols(i, 9 + i // halves, lax.rem(i, halves)).start()

    @pl.when(due)
    def _():
        tick(passed)

    @pl.when(step == end - 1)
    def _():
        for k in range(2):
            put_cols(k, 8, 0).wait()

        def rest(t, carry):
            tick(t)
            return carry

        lax.fori_loop(len(tick_steps), n_items + REDUCE_TAIL, rest, 0)
        if not spatial:
            for k in range(send_ref.shape[0]):
                to_peer(k).wait()
                mixed_to_peer(k).wait()


def plan_ticks(starts, spatial, ready, spacing):
    takes = (0.6, 5.0, 0.9, 2.5, 3.6 if spatial else 4.6, 1.7, 0.9, 1.7)
    steps, clock, last = [], 0.0, -spacing
    for section, (lo, hi) in enumerate(zip(starts, starts[1:])):
        for step in range(lo, hi):
            clock += takes[section]
            k = len(steps)
            if (k >= len(ready) or step >= ready[k]) and clock - last >= spacing:
                steps.append(step)
                last = clock
    return tuple(steps)


def block_backward(grad, saved, mods, w_first, first_base, w_second, second_base, spread_shape, spatial, out_type, mixed, prev, nz, cid):
    stream, normed_a, qkv, probs, att, proj, mid, normed_m, act, dact, down = saved
    tokens, width = mid.shape
    shapes = attention_shapes(spatial, tokens)
    n_win, n_query, n_key, _ = shapes
    pairs = width // 128
    halves = width // CHUNK
    a0, a1, a2, a3, a4, a5, a6, a7, end = backward_plan(tokens, width)
    tail = spread_shape[1:]
    zeros = (0,) * len(tail)

    def at(start, stop):
        return lambda i: jnp.clip(i - start, 0, max(stop - start - 1, 0))

    def row_block(place_of):
        return pl.BlockSpec((BLOCK_ROWS, width), lambda i: (place_of(i), 0))

    def g_at(i):
        return jnp.where(i < a1, i, at(a2, a3)(i))

    def first_at(i):
        third = at(a5, a6)(i)
        item = jnp.where(i < a5, 3, third // halves)
        half = jnp.where(i < a5, at(a3, a4)(i), third % halves)
        return (first_base + item, 0, half)

    def up_at(i):
        k = at(a1, a2)(i)
        return (second_base + 2 + 4 * (k // 4) + (k // 2) % 2, 0, k % 2)

    def down_at(i):
        k = at(a1, a2)(i)
        return (second_base // 2 + 2 * (k // 4), k % 4, 0)

    heads = at(a4, a5)
    hidden = pl.BlockSpec((tokens, CHUNK), lambda i: (0, at(a1, a2)(i)))
    anywhere = pl.BlockSpec(memory_space=pl.ANY)
    n_own = 9
    n_prev = 0 if prev is None else 3
    n_items = n_prev + n_own
    extra = [] if prev is None else [prev]
    n_send = tokens // (2 * BLOCK_ROWS)
    ready = [0] * n_prev + [a1 + 3, a1 + 5, a1 + 5, a1 + 5, a1 + 7, a2, a2, a2, a4]
    tick_steps = plan_ticks((a0, a1, a2, a3, a4, a5, a6, a7, end), spatial, ready, TICK_US[spatial])
    body = functools.partial(backward_body, spatial, shapes, n_prev, n_own, tick_steps, nz)
    if prev is None:
        whole = body

        def body(*refs):
            return whole(*refs[:19], None, *refs[19:])

    dma = pltpu.SemaphoreType.DMA
    return pl.pallas_call(
        body,
        grid=(end,),
        in_specs=[
            row_block(g_at),
            row_block(at(a0, a1)),
            row_block(at(a2, a3)),
            row_block(at(a2, a3)),
            row_block(at(a6, a7)),
            fixed(mods.shape),
            hidden,
            hidden,
            pl.BlockSpec((1, width, CHUNK), first_at),
            pl.BlockSpec((1, width, CHUNK), up_at),
            pl.BlockSpec((2, CHUNK // 2, width), down_at),
            pl.BlockSpec((tokens, 128), lambda i: (0, heads(i))),
            pl.BlockSpec((tokens, 128), lambda i: (0, pairs + heads(i))),
            pl.BlockSpec((tokens, 128), lambda i: (0, 2 * pairs + heads(i))),
            pl.BlockSpec((2, n_win, n_query, n_key), lambda i: (heads(i), 0, 0, 0)),
            anywhere, anywhere, anywhere, anywhere,
        ] + [anywhere] * len(extra),
        out_specs=[
            row_block(at(a6, a7)),
            pl.BlockSpec((2,) + tail, lambda i: (heads(i),) + zeros),
            pl.BlockSpec((8, width), lambda i: (0, 0)),
            anywhere,
            anywhere,
            anywhere,
            anywhere,
        ],
        out_shape=[
            jax.ShapeDtypeStruct((tokens, width), out_type),
            jax.ShapeDtypeStruct(spread_shape, F32),
            jax.ShapeDtypeStruct((8, width), F32),
            jax.ShapeDtypeStruct((12, nz, 2, 2, ROWS, COLS), BF16),
            jax.ShapeDtypeStruct((n_items, ROWS, COLS), F32),
            jax.ShapeDtypeStruct((n_send, BLOCK_ROWS, width), BF16),
            jax.ShapeDtypeStruct((n_send, BLOCK_ROWS, width), BF16),
        ],
        scratch_shapes=[
            pltpu.VMEM((tokens, width), BF16),
            pltpu.VMEM((tokens, width), BF16),
            pltpu.VMEM((tokens, width), F32),
            pltpu.VMEM((tokens, width), F32),
            pltpu.VMEM((tokens, width), BF16),
            pltpu.VMEM((tokens, 3 * width), BF16),
            pltpu.VMEM((2, n_query, n_key), F32),
            pltpu.VMEM((2, 2, 1, 2, 2, ROWS, COLS), BF16),
            pltpu.VMEM((2, nz, 2, 2, ROWS, CHUNK), BF16),
            dma,
            dma((2,)),
            dma((2,)),
            pltpu.VMEM((n_send, BLOCK_ROWS, width), BF16),
            dma((n_send,)),
            dma((n_send,)),
            dma((n_send,)),
            dma((n_send,)),
        ] + reduce_scratch(nz),
        compiler_params=pltpu.CompilerParams(
            collective_id=cid, has_side_effects=True, vmem_limit_bytes=64 * MIB
        ),
        name="block_backward",
    )(grad, down, mid, proj, stream, mods, act, dact, w_first, w_second, w_second, qkv, qkv, qkv, probs,
      normed_m, att, normed_a, mixed, *extra)


def swap_rows(values, me, swap, recv=None):
    keep = lax.dynamic_index_in_dim(values, me, 1, keepdims=False)
    if recv is None:
        send = lax.dynamic_index_in_dim(values, 1 - me, 1, keepdims=False)
        recv = lax.ppermute(send.astype(BF16), "frame", swap)
    recv = recv.reshape(keep.shape).astype(values.dtype)
    first = jnp.where(me == 0, keep, recv)
    second = jnp.where(me == 0, recv, keep)
    full = jnp.concatenate([first, second], axis=0)
    return full.transpose(2, 0, 1, 3, 4).reshape(-1, values.shape[-1])


def unswap_rows(values, me, swap, n_cw, f_l, recv=None):
    depth = values.shape[-1]
    full = values.reshape(n_cw, 2, f_l, TWIN, TWIN, depth)
    keep = lax.dynamic_index_in_dim(full, me, 1, keepdims=False)
    if recv is None:
        send = lax.dynamic_index_in_dim(full, 1 - me, 1, keepdims=False)
        recv = lax.ppermute(send.astype(BF16), "frame", swap)
    recv = recv.reshape(keep.shape).astype(values.dtype)
    first = jnp.where(me == 0, keep, recv)
    second = jnp.where(me == 0, recv, keep)
    both = jnp.stack([first, second], axis=0)
    return both.transpose(2, 0, 3, 1, 4, 5).reshape(-1, depth)


def pack_shards(shards, b):
    w_qkv, w_proj, w_up, w_down = [w[:, b] for w in shards]
    first = w_qkv.reshape(ROWS, 3, COLS).transpose(1, 0, 2)
    ups = w_up.reshape(ROWS, 2, 8, 2, 128).transpose(3, 1, 0, 2, 4).reshape(4, ROWS, COLS)
    downs = w_down.reshape(-1, ROWS, COLS)
    return [first, w_proj[None]], [downs[0:2], ups[0:2], downs[2:4], ups[2:4]]


def on_device(
    frames_in, size_group, modulation, w_qkv, w_proj, w_up, w_down, table_sp, table_st, cotangent
):
    n_clips, f_l, n_rows, n_cols, width = frames_in.shape
    me = lax.axis_index("frame")
    swap = [(0, 1), (1, 0)]
    n_cw = n_cols // TWIN
    nz = lax.axis_size("clip") // 4
    natural = (f_l, 2, TWIN, n_cw, TWIN, width)
    shards = (w_qkv, w_proj, w_up, w_down)
    packed = [pack_shards(shards, b) for b in range(2)]
    early = jnp.concatenate(packed[0][0] + packed[0][1] + packed[1][0], axis=0)
    late = jnp.concatenate(packed[1][1], axis=0)
    limit = n_cols - 3 * (2 - size_group[0])
    wide = (jnp.arange(n_cols, dtype=jnp.int32) < limit).astype(F32)
    ok_sp = jnp.broadcast_to(wide[None, None, None, :], (f_l, 1, n_rows, n_cols))
    ok_sp = ok_sp.reshape(f_l, 1, n_rows * n_cols)
    frame_ok = (jnp.arange(KEYF) < FILLED).astype(F32)
    ok_st = wide.reshape(n_cw, 1, 1, TWIN) * frame_ok[None, :, None, None]
    ok_st = jnp.broadcast_to(ok_st, (n_cw, KEYF, TWIN, TWIN)).reshape(n_cw, 1, -1)
    spread0 = spread_sp(table_sp)
    spread1 = spread_st(table_st)
    mods = modulation[0].reshape(2, 6, width)
    mods = jnp.pad(mods, ((0, 0), (0, 2), (0, 0)))
    cot = swap_rows(cotangent.reshape(natural), me, swap)
    stream0 = frames_in.reshape(-1, width)
    mid_stream, saved0, full0, peer0 = block_forward(
        stream0, mods[0], early, 2, 16, None, 0, spread0, ok_sp, True, F32, nz, 1
    )
    stream1 = swap_rows(mid_stream.reshape(natural), me, swap, peer0)
    end_stream, saved1, full1, _ = block_forward(
        stream1, mods[1], late, 1, 8, full0, 4, spread1, ok_st, False, BF16, nz, 5
    )
    full0 = full0.reshape(-1, width, width)
    full1 = full1.reshape(-1, width, width)
    grad1, gspread1, rows1, gw1, shares1, peer1, mixed1 = block_backward(
        cot, saved1, mods[1], full0, 12, full1, 0, spread1.shape, False, F32, end_stream, None, nz, 2
    )
    mixed = unswap_rows(end_stream, me, swap, n_cw, f_l, mixed1).reshape(frames_in.shape)
    grad_mid = unswap_rows(grad1, me, swap, n_cw, f_l, peer1)
    grad0, gspread0, rows0, gw0, shares0, _, _ = block_backward(
        grad_mid, saved0, mods[0], full0, 0, full0, 4, spread0.shape, True, BF16, end_stream, gw1, nz, 3
    )

    def wide_pad(table):
        return jnp.pad(table, ((0, 0), (0, -table.shape[1] % 128)))

    small = (
        jnp.pad(jnp.concatenate([rows0[:6], rows1[:6]], axis=0), ((0, 4), (0, 0))),
        wide_pad(gather_sp(gspread0)),
        wide_pad(gather_st(gspread1)),
    )
    last, mods_sum, sp_sum, st_sum = reduce_last(gw0, (9, 3), small, nz, 4)

    def pair(first, second):
        return jnp.stack([first, second], axis=1)

    def qkv_of(items):
        return jnp.concatenate([items[0], items[1], items[2]], axis=-1)

    def up_of(items):
        parts = jnp.stack([items[0], items[1], items[4], items[5]]).reshape(2, 2, ROWS, 8, 128)
        return parts.transpose(2, 1, 3, 0, 4).reshape(ROWS, 4 * COLS)

    def down_of(items):
        return jnp.concatenate([items[2], items[3], items[6], items[7]], axis=0)

    own0 = shares0[3:]
    outs = (
        pair(qkv_of(last), qkv_of(shares0[0:3])),
        pair(own0[8], shares1[8]),
        pair(up_of(own0), up_of(shares1)),
        pair(down_of(own0), down_of(shares1)),
    )
    mod_grad = mods_sum[:12][None]
    g_sp = sp_sum[:, : table_sp.shape[1]]
    g_st = st_sum[:, : table_st.shape[1]]
    grad_in = grad0.reshape(frames_in.shape)
    return (mixed, grad_in, mod_grad, outs[0], outs[1], outs[2], outs[3], g_sp, g_st)


HIGHEST = lax.Precision.HIGHEST


def layer_norm(values):
    centered = values - jnp.mean(values, axis=-1, keepdims=True)
    spread = jnp.mean(centered * centered, axis=-1, keepdims=True)
    return centered * lax.rsqrt(spread + NORM_EPS)


def modulate(values, shift_row, scale_row):
    return layer_norm(values) * (1.0 + scale_row) + shift_row


def gelu_tanh(values):
    return jax.nn.gelu(values, approximate=True)


def row_of(mod_rows, which):
    return mod_rows[:, which][:, None, None, None, :]


def clip_sum(values):
    return jnp.sum(values, axis=(1, 2, 3))


def flat_dot(values, weight):
    flat_in = values.reshape(-1, values.shape[-1])
    flat_out = jnp.dot(flat_in, weight, preferred_element_type=jnp.float32)
    return flat_out.reshape(values.shape[:-1] + (weight.shape[1],))


def back_dot(grad_values, weight):
    flat_in = grad_values.reshape(-1, grad_values.shape[-1])
    flat_out = jnp.einsum("nb,ab->na", flat_in, weight, preferred_element_type=jnp.float32)
    return flat_out.reshape(grad_values.shape[:-1] + (weight.shape[0],))


def outer_dot(left_values, right_values):
    left_flat = left_values.reshape(-1, left_values.shape[-1])
    right_flat = right_values.reshape(-1, right_values.shape[-1])
    return jnp.einsum("na,nb->ab", left_flat, right_flat, preferred_element_type=jnp.float32)


def split_heads(values, n_heads):
    return values.reshape(values.shape[0], values.shape[1], n_heads, -1)


def offset_pick(side_len):
    position = jnp.arange(side_len, dtype=jnp.int32)
    offsets = position[:, None] - position[None, :] + side_len - 1
    targets = jnp.arange(2 * side_len - 1, dtype=jnp.int32)
    return (offsets[:, :, None] == targets[None, None, :]).astype(jnp.float32)


def expand_bias(table, side_len):
    one_hot = offset_pick(side_len)
    rows_done = jnp.einsum("hab,xya->hxyb", table, one_hot, precision=HIGHEST)
    full_bias = jnp.einsum("hxyb,uvb->hxuyv", rows_done, one_hot, precision=HIGHEST)
    return full_bias.reshape(table.shape[0], side_len * side_len, side_len * side_len)


def cube_bias(table_st, first_frame, local_frames):
    n_heads = table_st.shape[0]
    span_frames = 2 * FRAMES - 1
    side_span = 2 * TWIN - 1
    table_cube = table_st.reshape(n_heads, span_frames, side_span * side_span)
    query_frames = first_frame + jnp.arange(local_frames, dtype=jnp.int32)
    key_frames = jnp.arange(FRAMES, dtype=jnp.int32)
    offsets = query_frames[:, None] - key_frames[None, :] + FRAMES - 1
    choose = (
        offsets[:, :, None] == jnp.arange(span_frames, dtype=jnp.int32)[None, None, :]
    ).astype(jnp.float32)
    picked = jnp.einsum("hoz,jfo->hjfz", table_cube, choose, precision=HIGHEST)
    squares = expand_bias(picked.reshape(-1, side_span, side_span), TWIN)
    squares = squares.reshape(n_heads, local_frames, FRAMES, TWIN * TWIN, TWIN * TWIN)
    squares = squares.transpose(0, 1, 3, 2, 4)
    return squares.reshape(n_heads, local_frames * TWIN * TWIN, FRAMES * TWIN * TWIN)


def spatial_windows(values):
    n_clips, n_frames, n_rows, n_cols, n_depth = values.shape
    blocked = values.reshape(n_clips, n_frames, n_rows // SWIN, SWIN, n_cols // SWIN, SWIN, n_depth)
    return blocked.transpose(0, 1, 2, 4, 3, 5, 6).reshape(-1, SWIN * SWIN, n_depth)


def spatial_unwindow(values, full_shape):
    n_clips, n_frames, n_rows, n_cols, n_depth = full_shape
    blocked = values.reshape(n_clips, n_frames, n_rows // SWIN, n_cols // SWIN, SWIN, SWIN, n_depth)
    return blocked.transpose(0, 1, 2, 4, 3, 5, 6).reshape(full_shape)


def cube_windows(values):
    n_clips, n_frames, n_rows, n_cols, n_depth = values.shape
    blocked = values.reshape(n_clips, n_frames, n_rows // TWIN, TWIN, n_cols // TWIN, TWIN, n_depth)
    blocked = blocked.transpose(0, 2, 4, 1, 3, 5, 6)
    return blocked.reshape(
        n_clips * (n_rows // TWIN) * (n_cols // TWIN), n_frames * TWIN * TWIN, n_depth
    )


def cube_unwindow(values, full_shape):
    n_clips, n_frames, n_rows, n_cols, n_depth = full_shape
    blocked = values.reshape(n_clips, n_rows // TWIN, n_cols // TWIN, n_frames, TWIN, TWIN, n_depth)
    return blocked.transpose(0, 3, 1, 4, 2, 5, 6).reshape(full_shape)


def soft_scores(query_win, key_win, bias, key_ok, score_scale):
    scores = jnp.einsum("nqhd,nkhd->nhqk", query_win, key_win, preferred_element_type=jnp.float32)
    scores = scores * score_scale + bias[None]
    scores = jnp.where(key_ok[:, None, None, :], scores, NEG_FILL)
    row_top = jnp.max(scores, axis=-1, keepdims=True)
    expo_values = jnp.exp(scores - row_top)
    return expo_values / jnp.sum(expo_values, axis=-1, keepdims=True)


def general_forward(
    stream,
    mod_rows,
    weights,
    n_heads,
    bias,
    key_ok,
    to_windows,
    from_windows,
    fetch_keys,
    score_scale,
):
    qkv_w, proj_w, up_w, down_w = weights
    width_d = stream.shape[-1]
    normed_a = modulate(stream, row_of(mod_rows, 0), row_of(mod_rows, 1)).astype(jnp.bfloat16)
    qkv_values = flat_dot(normed_a, qkv_w).astype(jnp.bfloat16)
    key_local = qkv_values[..., width_d : 2 * width_d]
    value_local = qkv_values[..., 2 * width_d :]
    query_win = split_heads(to_windows(qkv_values[..., :width_d]), n_heads)
    key_flat, value_flat = fetch_keys(key_local, value_local)
    key_win = split_heads(key_flat, n_heads)
    value_win = split_heads(value_flat, n_heads)
    soft_probs = soft_scores(query_win, key_win, bias, key_ok, score_scale)
    att_win = jnp.einsum(
        "nhqk,nkhd->nqhd",
        soft_probs.astype(jnp.bfloat16),
        value_win,
        preferred_element_type=jnp.float32,
    ).astype(jnp.bfloat16)
    att_out = from_windows(
        att_win.reshape(att_win.shape[0], att_win.shape[1], width_d), stream.shape
    )
    proj_out = flat_dot(att_out, proj_w)
    mid_stream = stream + row_of(mod_rows, 2) * proj_out
    normed_m = modulate(mid_stream, row_of(mod_rows, 3), row_of(mod_rows, 4)).astype(jnp.bfloat16)
    up_value = flat_dot(normed_m, up_w)
    active = gelu_tanh(up_value).astype(jnp.bfloat16)
    down_out = flat_dot(active, down_w)
    result = mid_stream + row_of(mod_rows, 5) * down_out
    saved = (
        stream,
        normed_a,
        query_win,
        key_win,
        value_win,
        key_local,
        value_local,
        att_out,
        proj_out,
        mid_stream,
        normed_m,
        up_value,
        active,
        down_out,
    )
    return (result, saved)


def general_backward(
    grad_out,
    saved,
    mod_rows,
    weights,
    n_heads,
    bias,
    key_ok,
    to_windows,
    from_windows,
    return_keys,
    key_win,
    value_win,
    score_scale,
):
    (
        stream,
        normed_a,
        query_win,
        unused_key,
        unused_value,
        key_local,
        value_local,
        att_out,
        proj_out,
        mid_stream,
        normed_m,
        up_value,
        active,
        down_out,
    ) = saved
    qkv_w, proj_w, up_w, down_w = weights
    n_clips = stream.shape[0]
    width_d = stream.shape[-1]
    grad_down_v = (row_of(mod_rows, 5) * grad_out).astype(jnp.bfloat16)
    gate_m_grad = clip_sum(grad_out * down_out)
    down_grad = outer_dot(active, grad_down_v)
    grad_act = back_dot(grad_down_v, down_w)
    unused_gelu, gelu_pull = jax.vjp(gelu_tanh, up_value)
    grad_up_v = gelu_pull(grad_act)[0].astype(jnp.bfloat16)
    up_grad = outer_dot(normed_m, grad_up_v)
    grad_normed = back_dot(grad_up_v, up_w)
    unused_norm, norm_pull = jax.vjp(modulate, mid_stream, row_of(mod_rows, 3), row_of(mod_rows, 4))
    grad_mid, shift_m_grad, scale_m_grad = norm_pull(grad_normed)
    grad_mid = grad_mid + grad_out
    grad_proj_v = (row_of(mod_rows, 2) * grad_mid).astype(jnp.bfloat16)
    gate_a_grad = clip_sum(grad_mid * proj_out)
    proj_grad = outer_dot(att_out, grad_proj_v)
    grad_att = back_dot(grad_proj_v, proj_w).astype(jnp.bfloat16)
    grad_att_win = split_heads(to_windows(grad_att), n_heads)
    soft_probs = soft_scores(query_win, key_win, bias, key_ok, score_scale)
    grad_probs = jnp.einsum(
        "nqhd,nkhd->nhqk", grad_att_win, value_win, preferred_element_type=jnp.float32
    )
    row_delta = jnp.sum(soft_probs * grad_probs, axis=-1, keepdims=True)
    grad_scores = (soft_probs * (grad_probs - row_delta)).astype(jnp.bfloat16)
    grad_bias = jnp.sum(grad_scores.astype(jnp.float32), axis=0)
    grad_query = (
        jnp.einsum("nhqk,nkhd->nqhd", grad_scores, key_win, preferred_element_type=jnp.float32)
        * score_scale
    )
    grad_key = (
        jnp.einsum("nhqk,nqhd->nkhd", grad_scores, query_win, preferred_element_type=jnp.float32)
        * score_scale
    )
    grad_value = jnp.einsum(
        "nhqk,nqhd->nkhd",
        soft_probs.astype(jnp.bfloat16),
        grad_att_win,
        preferred_element_type=jnp.float32,
    )
    n_win = grad_query.shape[0]
    grad_query = from_windows(grad_query.reshape(n_win, grad_query.shape[1], width_d), stream.shape)
    grad_key_full, grad_value_full = return_keys(
        grad_key.reshape(n_win, grad_key.shape[1], width_d),
        grad_value.reshape(n_win, grad_value.shape[1], width_d),
    )
    grad_qkv_v = jnp.concatenate([grad_query, grad_key_full, grad_value_full], axis=-1).astype(
        jnp.bfloat16
    )
    qkv_grad = outer_dot(normed_a, grad_qkv_v)
    grad_normed = back_dot(grad_qkv_v, qkv_w)
    unused_norm, norm_pull = jax.vjp(modulate, stream, row_of(mod_rows, 0), row_of(mod_rows, 1))
    grad_stream, shift_a_grad, scale_a_grad = norm_pull(grad_normed)
    grad_stream = grad_stream + grad_mid
    mod_grad = jnp.stack(
        [
            shift_a_grad.reshape(n_clips, width_d),
            scale_a_grad.reshape(n_clips, width_d),
            gate_a_grad,
            shift_m_grad.reshape(n_clips, width_d),
            scale_m_grad.reshape(n_clips, width_d),
            gate_m_grad,
        ],
        axis=1,
    )
    return (grad_stream, mod_grad, (qkv_grad, proj_grad, up_grad, down_grad), grad_bias)


def on_device_general(
    frames_in, size_group, modulation, w_qkv, w_proj, w_up, w_down, table_sp, table_st, cotangent
):
    n_clips, local_frames, n_rows, n_cols, width_d = frames_in.shape
    n_heads = table_sp.shape[0]
    score_scale = (width_d // n_heads) ** (-0.5)
    first_frame = lax.axis_index("frame") * local_frames
    local_shape = (n_clips, local_frames, n_rows, n_cols, width_d)
    whole_shape = (n_clips, FRAMES, n_rows, n_cols, width_d)
    gathered = (
        lax.all_gather(w_qkv, "clip", axis=0, tiled=True),
        lax.all_gather(w_proj, "clip", axis=0, tiled=True),
        lax.all_gather(w_up, "clip", axis=0, tiled=True),
        lax.all_gather(w_down, "clip", axis=0, tiled=True),
    )
    column_ids = jnp.arange(n_cols, dtype=jnp.int32)
    column_limit = n_cols - 3 * (2 - size_group)
    wide_ok = column_ids[None, :] < column_limit[:, None]
    local_ok = jnp.broadcast_to(wide_ok[:, None, None, :], (n_clips, local_frames, n_rows, n_cols))
    spatial_ok = spatial_windows(local_ok[..., None])[..., 0]
    frame_ok = jnp.arange(FRAMES, dtype=jnp.int32) < FILLED
    cube_grid = wide_ok[:, None, None, :] & frame_ok[None, :, None, None]
    cube_grid = jnp.broadcast_to(cube_grid, (n_clips, FRAMES, n_rows, n_cols))
    cube_ok = cube_windows(cube_grid[..., None])[..., 0]
    span_sp = 2 * SWIN - 1

    def build_spatial(table):
        return expand_bias(table.reshape(n_heads, span_sp, span_sp), SWIN)

    def build_cube(table):
        return cube_bias(table, first_frame, local_frames)

    bias_sp, pull_sp = jax.vjp(build_spatial, table_sp)
    bias_st, pull_st = jax.vjp(build_cube, table_st)

    def spatial_keys(key_local, value_local):
        return (spatial_windows(key_local), spatial_windows(value_local))

    def cube_keys(key_local, value_local):
        key_all, value_all = (
            lax.all_gather(key_local, "frame", axis=1, tiled=True),
            lax.all_gather(value_local, "frame", axis=1, tiled=True),
        )
        return (cube_windows(key_all), cube_windows(value_all))

    def spatial_return(grad_key, grad_value):
        return (spatial_unwindow(grad_key, local_shape), spatial_unwindow(grad_value, local_shape))

    def cube_return(grad_key, grad_value):
        key_whole = cube_unwindow(grad_key, whole_shape)
        value_whole = cube_unwindow(grad_value, whole_shape)
        return (
            lax.psum_scatter(
                key_whole.astype(jnp.bfloat16), "frame", scatter_dimension=1, tiled=True
            ).astype(jnp.float32),
            lax.psum_scatter(
                value_whole.astype(jnp.bfloat16), "frame", scatter_dimension=1, tiled=True
            ).astype(jnp.float32),
        )

    weights_sp = (gathered[0][:, 0], gathered[1][:, 0], gathered[2][:, 0], gathered[3][:, 0])
    weights_st = (gathered[0][:, 1], gathered[1][:, 1], gathered[2][:, 1], gathered[3][:, 1])
    stream_mid, saved_sp = general_forward(
        frames_in.astype(jnp.float32),
        modulation[:, 0:6],
        weights_sp,
        n_heads,
        bias_sp,
        spatial_ok,
        spatial_windows,
        spatial_unwindow,
        spatial_keys,
        score_scale,
    )
    stream_end, saved_st = general_forward(
        stream_mid,
        modulation[:, 6:12],
        weights_st,
        n_heads,
        bias_st,
        cube_ok,
        cube_windows,
        cube_unwindow,
        cube_keys,
        score_scale,
    )
    mixed = stream_end.astype(jnp.bfloat16)
    again = (
        lax.all_gather(w_qkv, "clip", axis=0, tiled=True),
        lax.all_gather(w_proj, "clip", axis=0, tiled=True),
        lax.all_gather(w_up, "clip", axis=0, tiled=True),
        lax.all_gather(w_down, "clip", axis=0, tiled=True),
    )
    back_sp = (again[0][:, 0], again[1][:, 0], again[2][:, 0], again[3][:, 0])
    back_st = (again[0][:, 1], again[1][:, 1], again[2][:, 1], again[3][:, 1])
    key_again, value_again = (
        lax.all_gather(saved_st[5], "frame", axis=1, tiled=True),
        lax.all_gather(saved_st[6], "frame", axis=1, tiled=True),
    )
    key_win_st = split_heads(cube_windows(key_again), n_heads)
    value_win_st = split_heads(cube_windows(value_again), n_heads)
    grad_stream, mod_grad_st, grads_st, bias_grad_st = general_backward(
        cotangent.astype(jnp.float32),
        saved_st,
        modulation[:, 6:12],
        back_st,
        n_heads,
        bias_st,
        cube_ok,
        cube_windows,
        cube_unwindow,
        cube_return,
        key_win_st,
        value_win_st,
        score_scale,
    )
    grad_stream, mod_grad_sp, grads_sp, bias_grad_sp = general_backward(
        grad_stream,
        saved_sp,
        modulation[:, 0:6],
        back_sp,
        n_heads,
        bias_sp,
        spatial_ok,
        spatial_windows,
        spatial_unwindow,
        spatial_return,
        saved_sp[3],
        saved_sp[4],
        score_scale,
    )
    table_sp_grad = pull_sp(bias_grad_sp)[0]
    table_st_grad = pull_st(bias_grad_st)[0]
    full_qkv = jnp.stack([grads_sp[0], grads_st[0]], axis=1)
    full_proj = jnp.stack([grads_sp[1], grads_st[1]], axis=1)
    full_up = jnp.stack([grads_sp[2], grads_st[2]], axis=1)
    full_down = jnp.stack([grads_sp[3], grads_st[3]], axis=1)
    shares = (
        lax.psum_scatter(
            full_qkv.astype(jnp.bfloat16), "clip", scatter_dimension=0, tiled=True
        ).astype(jnp.float32),
        lax.psum_scatter(
            full_proj.astype(jnp.bfloat16), "clip", scatter_dimension=0, tiled=True
        ).astype(jnp.float32),
        lax.psum_scatter(
            full_up.astype(jnp.bfloat16), "clip", scatter_dimension=0, tiled=True
        ).astype(jnp.float32),
        lax.psum_scatter(
            full_down.astype(jnp.bfloat16), "clip", scatter_dimension=0, tiled=True
        ).astype(jnp.float32),
    )
    mod_grad = jnp.concatenate([mod_grad_sp, mod_grad_st], axis=1)
    summed = (
        lax.psum(shares[0].astype(jnp.bfloat16), "frame").astype(jnp.float32),
        lax.psum(shares[1].astype(jnp.bfloat16), "frame").astype(jnp.float32),
        lax.psum(shares[2].astype(jnp.bfloat16), "frame").astype(jnp.float32),
        lax.psum(shares[3].astype(jnp.bfloat16), "frame").astype(jnp.float32),
        lax.psum(mod_grad.astype(jnp.bfloat16), "frame").astype(jnp.float32),
        lax.psum(table_sp_grad.astype(jnp.bfloat16), "frame").astype(jnp.float32),
        lax.psum(table_st_grad.astype(jnp.bfloat16), "frame").astype(jnp.float32),
    )
    tables = (
        lax.psum(summed[5].astype(jnp.bfloat16), "clip").astype(jnp.float32),
        lax.psum(summed[6].astype(jnp.bfloat16), "clip").astype(jnp.float32),
    )
    return (
        mixed,
        grad_stream.astype(jnp.bfloat16),
        summed[4],
        summed[0],
        summed[1],
        summed[2],
        summed[3],
        tables[0],
        tables[1],
    )


def solution(mesh):
    placed = (
        P("clip", "frame", None, None, None),
        P("clip"),
        P("clip", None, None),
        P("clip", None, None),
        P("clip", None, None),
        P("clip", None, None),
        P("clip", None, None),
        P(),
        P(),
        P("clip", "frame", None, None, None),
    )
    whole_windows = mesh.shape["frame"] == 2 and mesh.shape["clip"] == 16
    return jax.shard_map(
        on_device if whole_windows else on_device_general,
        mesh=mesh,
        in_specs=placed,
        out_specs=(
            P("clip", "frame", None, None, None),
            P("clip", "frame", None, None, None),
            P("clip", None, None),
            P("clip", None, None),
            P("clip", None, None),
            P("clip", None, None),
            P("clip", None, None),
            P(),
            P(),
        ),
        check_vma=False,
    )
```

```python
import functools

import jax
import jax.numpy as jnp
import numpy as np
from jax import lax
from jax.experimental import pallas as pl
from jax.experimental.pallas import tpu as pltpu
from jax.sharding import PartitionSpec as P

SWIN = 16
TWIN = 8
FRAMES = 8
FILLED = 5
KEYF = 6
NEG_FILL = -1000000000.0
NORM_EPS = 1e-06
F32 = jnp.float32
BF16 = jnp.bfloat16
NT = (((1,), (1,)), ((), ()))
TN = (((0,), (0,)), ((), ()))


def dot_nn(a, b):
    return jnp.dot(a, b, preferred_element_type=F32)


def dot_nt(a, b):
    return lax.dot_general(a, b, NT, preferred_element_type=F32)


def dot_tn(a, b):
    return lax.dot_general(a, b, TN, preferred_element_type=F32)


def norm_stats(values):
    mean = jnp.mean(values, axis=-1, keepdims=True)
    centered = values - mean
    spread = jnp.mean(centered * centered, axis=-1, keepdims=True)
    inv = lax.rsqrt(spread + NORM_EPS)
    return centered * inv, inv


def pick_sp():
    span = 2 * SWIN - 1
    k, b, ci, lane = np.ogrid[0:8, 0:span, 0:SWIN, 0:128]
    hit = (k == 7 - lane // SWIN) & (b == SWIN - 1 + ci - lane % SWIN)
    return hit.reshape(8 * span, SWIN * 128).astype(np.float32)


def pick_st():
    span = 2 * TWIN - 1
    r, b, ci, lane = np.ogrid[0:span, 0:span, 0:TWIN, 0:128]
    hit = (r == span - 1 - lane // TWIN) & (b == TWIN - 1 + ci - lane % TWIN)
    return hit.reshape(span * span, TWIN * 128).astype(np.float32)


def spread_sp(table):
    n_heads = table.shape[0]
    span = 2 * SWIN - 1
    padded = jnp.pad(table, ((0, 0), (span, 0))).reshape(n_heads * 4, 8 * span)
    out = jnp.dot(padded, pick_sp(), precision=lax.Precision.HIGHEST)
    return out.reshape(n_heads, 4, SWIN, 128)


def spread_st(table):
    n_heads = table.shape[0]
    span = 2 * TWIN - 1
    fspan = 2 * FRAMES - 1
    flat = table.reshape(n_heads * fspan, span * span)
    out = jnp.dot(flat, pick_st(), precision=lax.Precision.HIGHEST)
    return out.reshape(n_heads, fspan, TWIN, 128)


def gather_sp(spread):
    n_heads = spread.shape[0]
    span = 2 * SWIN - 1
    flat = spread.reshape(n_heads * 4, SWIN * 128)
    out = lax.dot_general(flat, pick_sp(), NT, precision=lax.Precision.HIGHEST)
    return out.reshape(n_heads, 32 * span)[:, span:]


def gather_st(spread):
    n_heads = spread.shape[0]
    span = 2 * TWIN - 1
    fspan = 2 * FRAMES - 1
    flat = spread.reshape(n_heads * fspan, TWIN * 128)
    out = lax.dot_general(flat, pick_st(), NT, precision=lax.Precision.HIGHEST)
    return out.reshape(n_heads, fspan * span * span)


def fill_bias_sp(spread_ref, hh, bias_ref):
    spread = jnp.concatenate([spread_ref[hh, g] for g in (3, 2, 1, 0)], axis=1)
    width = spread.shape[1]
    win = SWIN * SWIN
    for ri in range(SWIN):
        shift = (width - (SWIN - 1 - ri) * SWIN) % width
        rolled = pltpu.roll(spread, shift, 1) if shift else spread
        bias_ref[ri * SWIN : (ri + 1) * SWIN, :] = rolled[:, :win]


def fold_bias_sp(grad_ref, out_ref, hh):
    win = SWIN * SWIN
    width = 2 * win
    total = None
    for ri in range(SWIN):
        rows = grad_ref[ri * SWIN : (ri + 1) * SWIN, :]
        rows = jnp.concatenate([rows, jnp.zeros((SWIN, width - win), F32)], axis=1)
        shift = (SWIN - 1 - ri) * SWIN
        rows = pltpu.roll(rows, shift, 1) if shift else rows
        total = rows if total is None else total + rows
    for g in range(4):
        out_ref[hh, g] = total[:, (3 - g) * 128 : (4 - g) * 128]


def fill_bias_st(spread_ref, hh, bias_ref):
    lanes = lax.broadcasted_iota(jnp.int32, (TWIN, 128), 1)
    half = TWIN * TWIN
    n_pairs = KEYF // 2
    for ri in range(TWIN):
        shift = (128 - (TWIN - 1 - ri) * TWIN) % 128
        cache = {}

        def low_of(f):
            if f not in cache:
                rows = spread_ref[hh, 2 * FRAMES - 2 - f]
                cache[f] = pltpu.roll(rows, shift, 1) if shift else rows
            return cache[f]

        pairs = {}
        for fi in range(FRAMES):
            for pair in range(n_pairs):
                f = FRAMES - 1 - fi + 2 * pair
                if f not in pairs:
                    pairs[f] = jnp.where(
                        lanes < half, low_of(f), pltpu.roll(low_of(f + 1), half, 1)
                    )
                row = fi * half + ri * TWIN
                bias_ref[row : row + TWIN, pair * 128 : (pair + 1) * 128] = pairs[f]


def fold_bias_st(grad_ref, out_ref, hh):
    lanes = lax.broadcasted_iota(jnp.int32, (TWIN, 128), 1)
    half = TWIN * TWIN
    n_pairs = KEYF // 2
    fspan = 2 * FRAMES - 1
    totals = [None] * fspan
    for ri in range(TWIN):
        sums = {}
        for fi in range(FRAMES):
            for pair in range(n_pairs):
                f = FRAMES - 1 - fi + 2 * pair
                row = fi * half + ri * TWIN
                part = grad_ref[row : row + TWIN, pair * 128 : (pair + 1) * 128]
                sums[f] = part if f not in sums else sums[f] + part
        for f in range(fspan):
            piece = None
            if f in sums:
                piece = jnp.where(lanes < half, sums[f], 0.0)
            if f - 1 in sums:
                upper = pltpu.roll(jnp.where(lanes >= half, sums[f - 1], 0.0), half, 1)
                piece = upper if piece is None else piece + upper
            if piece is None:
                continue
            shift = (TWIN - 1 - ri) * TWIN
            piece = pltpu.roll(piece, shift, 1) if shift else piece
            totals[f] = piece if totals[f] is None else totals[f] + piece
    for f in range(fspan):
        out_ref[hh, 2 * FRAMES - 2 - f] = jnp.zeros((TWIN, 128), F32) if totals[f] is None else totals[f]


def lane_mask(rows, hh):
    lanes = lax.broadcasted_iota(jnp.int32, (rows, 128), 1)
    return (lanes < 64) if hh == 0 else (lanes >= 64)


def attend_forward(spatial, n_win, n_query, n_key, chunk, q_ref, k_ref, v_ref, m_ref, ok_ref, att_ref, p_ref, bias_ref):
    for hh in range(2):
        if spatial:
            fill_bias_sp(m_ref, hh, bias_ref.at[hh])
        else:
            fill_bias_st(m_ref, hh, bias_ref.at[hh])
    own = lane_mask(chunk, 0)
    for n in range(n_win):
        key = k_ref[n * n_query : n * n_query + n_key, :]
        val = v_ref[n * n_query : n * n_query + n_key, :]
        ok = ok_ref[n] > 0.0
        for c in range(n_query // chunk):
            rows = slice(n * n_query + c * chunk, n * n_query + (c + 1) * chunk)
            query = q_ref[rows, :]
            query = query * jnp.asarray(0.125, BF16)
            outs = []
            for hh in range(2):
                mine = own if hh == 0 else jnp.logical_not(own)
                picked = jnp.where(mine, query, jnp.zeros_like(query))
                scores = dot_nt(picked, key) + bias_ref[hh, c * chunk : (c + 1) * chunk, :]
                scores = jnp.where(ok, scores, NEG_FILL)
                top = jnp.max(scores, axis=-1, keepdims=True)
                expo = jnp.exp(scores - top)
                probs = (expo * (1.0 / jnp.sum(expo, axis=-1, keepdims=True))).astype(BF16)
                p_ref[hh, n, c * chunk : (c + 1) * chunk, :] = probs
                outs.append(dot_nn(probs, val))
            att_ref[rows, :] = jnp.where(own, outs[0], outs[1]).astype(BF16)


def attend_backward(
    spatial, n_win, n_query, n_key, chunk, head, q_ref, k_ref, v_ref, do_ref, p_ref, g_ref, dm_ref, db_ref
):
    width = g_ref.shape[1] // 3
    own = lane_mask(chunk, 0)
    own_k = lane_mask(n_key, 0)

    def store(rows, which, values):
        g_ref[rows, pl.ds(pl.multiple_of(which * width + head * 128, 128), 128)] = values

    db_ref[...] = jnp.zeros_like(db_ref)
    for n in range(n_win):
        keys = slice(n * n_query, n * n_query + n_key)
        key = k_ref[keys, :]
        val = v_ref[keys, :]
        gk = [None, None]
        gv = [None, None]
        for c in range(n_query // chunk):
            rows = slice(n * n_query + c * chunk, n * n_query + (c + 1) * chunk)
            part = slice(c * chunk, (c + 1) * chunk)
            query = q_ref[rows, :]
            gout = do_ref[rows, :]
            gq = []
            for hh in range(2):
                mine = own if hh == 0 else jnp.logical_not(own)
                probs = p_ref[hh, n, part, :]
                gsel = jnp.where(mine, gout, jnp.zeros_like(gout))
                dprob = dot_nt(gsel, val)
                soft = probs.astype(F32)
                delta = jnp.sum(soft * dprob, axis=-1, keepdims=True)
                dscore = (soft * (dprob - delta)).astype(BF16)
                db_ref[hh, part, :] += dscore.astype(F32)
                gq.append(dot_nn(dscore, key))
                dk = dot_tn(dscore, query)
                dv = dot_tn(probs, gout)
                gk[hh] = dk if gk[hh] is None else gk[hh] + dk
                gv[hh] = dv if gv[hh] is None else gv[hh] + dv
            store(rows, 0, (jnp.where(own, gq[0], gq[1]) * 0.125).astype(BF16))
        store(keys, 1, (jnp.where(own_k, gk[0], gk[1]) * 0.125).astype(BF16))
        store(keys, 2, jnp.where(own_k, gv[0], gv[1]).astype(BF16))
        if n_key < n_query:
            rest = slice(n * n_query + n_key, (n + 1) * n_query)
            empty = jnp.zeros((n_query - n_key, 128), BF16)
            store(rest, 1, empty)
            store(rest, 2, empty)
    for hh in range(2):
        if spatial:
            fold_bias_sp(db_ref.at[hh], dm_ref, hh)
        else:
            fold_bias_st(db_ref.at[hh], dm_ref, hh)


def attention_shapes(spatial, tokens):
    n_query = SWIN * SWIN if spatial else FRAMES * TWIN * TWIN
    n_key = n_query if spatial else KEYF * TWIN * TWIN
    return tokens // n_query, n_query, n_key, n_query


ROWS = 64
COLS = 1024
MESH = pl.DeviceIdType.MESH


def place(n_clip):
    clip = lax.axis_index("clip")
    x = lax.axis_index("frame")
    z = clip // 4
    y = lax.rem(clip // 2, 2)
    c = lax.rem(clip, 2)
    return clip, z, y, c, x


def remote(src, dst, send, recv, clip, frame):
    return pltpu.make_async_remote_copy(
        src_ref=src,
        dst_ref=dst,
        send_sem=send,
        recv_sem=recv,
        device_id={"clip": clip, "frame": frame},
        device_id_type=MESH,
    )


def greet(targets):
    barrier = pltpu.get_barrier_semaphore()
    count = 0
    for clip, frame, valid in targets:
        if valid is None:
            pl.semaphore_signal(barrier, inc=1, device_id={"clip": clip, "frame": frame}, device_id_type=MESH)
            count = count + 1
        else:
            @pl.when(valid)
            def _():
                pl.semaphore_signal(barrier, inc=1, device_id={"clip": clip, "frame": frame}, device_id_type=MESH)
            count = count + valid.astype(jnp.int32)
    pl.semaphore_wait(barrier, count)


GATHER_TAIL = 6


def gather_tick(t, n, nz, where, wide, shard, full, local, up_s, up_r, dn_s, dn_r, y_s, y_r, x_s, x_r, c_s, c_r):
    clip, z, y, c, x = where
    last = nz - 1
    steps = nz - 1

    def phases(i, hi):
        lo = COLS - hi
        fetch = pl.ds(pl.multiple_of(x * lo, 128), hi)
        give = pl.ds(pl.multiple_of(x * hi, 128), lo)

        def own():
            return pltpu.make_async_copy(
                shard.at[i, :, fetch], full.at[i, z, y, c, :, fetch], local.at[i]
            )

        def up(s, origin):
            src = shard.at[i, :, fetch] if s == 0 else full.at[i, origin, y, c, :, fetch]
            return remote(src, full.at[i, origin, y, c, :, fetch], up_s.at[s, i], up_r.at[s, i], clip + 4, x)

        def down(s, origin):
            src = shard.at[i, :, fetch] if s == 0 else full.at[i, origin, y, c, :, fetch]
            return remote(src, full.at[i, origin, y, c, :, fetch], dn_s.at[s, i], dn_r.at[s, i], clip - 4, x)

        def over_y():
            src = full.at[i, :, y, c, :, fetch]
            return remote(src, src, y_s.at[i], y_r.at[i], clip + 2 - 4 * y, x)

        def over_x():
            src = full.at[i, :, :, c, :, give]
            return remote(src, src, x_s.at[i], x_r.at[i], clip, 1 - x)

        def over_c():
            src = full.at[i, :, :, c]
            return remote(src, src, c_s.at[i], c_r.at[i], clip + 1 - 2 * c, x)

        def z_wait(s):
            @pl.when(z - 1 - s >= 0)
            def _():
                up(s, z - 1 - s).wait_recv()

            @pl.when(z + 1 + s <= last)
            def _():
                down(s, z + 1 + s).wait_recv()

        def z_start(s):
            @pl.when(jnp.logical_and(z < last, z - s >= 0))
            def _():
                up(s, z - s).start()

            @pl.when(jnp.logical_and(z > 0, z + s <= last))
            def _():
                down(s, z + s).start()

        def z_sent(s):
            @pl.when(jnp.logical_and(z < last, z - s >= 0))
            def _():
                up(s, z - s).wait_send()

            @pl.when(jnp.logical_and(z > 0, z + s <= last))
            def _():
                down(s, z + s).wait_send()

        def first():
            own().start()
            z_start(0)

        def along(s):
            z_wait(s - 1)
            z_start(s)

        def to_y():
            z_wait(steps - 1)
            own().wait()
            over_y().start()

        def to_x():
            over_y().wait_recv()
            over_x().start()

        def to_c():
            over_x().wait_recv()
            over_c().start()

        def finish():
            over_c().wait_recv()
            for s in range(steps):
                z_sent(s)
            over_y().wait_send()
            over_x().wait_send()
            over_c().wait_send()

        mids = [functools.partial(along, s) for s in range(1, steps)]
        return [first] + mids + [to_y, to_x, to_c, finish]

    for k in range(steps + 4):
        i = t - k
        valid = jnp.logical_and(i >= 0, i < n)
        larger = lax.rem(i + 3, 3) < wide
        for hi, chosen in ((640, jnp.logical_not(larger)), (768, larger)):
            @pl.when(jnp.logical_and(valid, chosen))
            def _(i=i, hi=hi, k=k):
                phases(i, hi)[k]()


def greet_gather(nz, where):
    clip, z, y, c, x = where
    greet([
        (clip + 4, x, z < nz - 1),
        (clip - 4, x, z > 0),
        (clip + 2 - 4 * y, x, None),
        (clip, 1 - x, None),
        (clip + 1 - 2 * c, x, None),
    ])


def gather_sems(n, nz):
    dma = pltpu.SemaphoreType.DMA
    z = dma((nz - 1, n))
    one = dma((n,))
    return [one, z, z, z, z, one, one, one, one, one, one]


NBUF = 3
REDUCE_TAIL = 7
Y_FIRST = 640
NACC = 4


def reduce_tick(t, n, nz, where, sources, out, acc, cbuf, ya, xa, yb, xb, tb, zb, sb, fb, ob,
                loc, c_s, c_r, ya_s, ya_r, xa_s, xa_r, yb_s, yb_r, xb_s, xb_r, z_s, z_r, f_s, f_r, o_s,
                cred_c, cred_y, cred_x, cred_z, cred_f):
    clip, z, y, c, x = where
    half = ROWS // 2
    peer_c = clip + 1 - 2 * c
    peer_y = clip + 2 - 4 * y
    mine = pl.ds(pl.multiple_of(x * half, half), half)
    theirs = pl.ds(pl.multiple_of((1 - x) * half, half), half)
    left = pl.ds(0, Y_FIRST)
    right = pl.ds(Y_FIRST, COLS - Y_FIRST)

    def slot(i):
        return lax.rem(i, NBUF)

    def aslot(i):
        return lax.rem(i, NACC)

    def load(i, source, first):
        return pltpu.make_async_copy(source.at[i - first, :, :, c], acc.at[aslot(i)], loc.at[slot(i)])

    def over_c(i, source, first):
        src = source.at[i - first, :, :, 1 - c]
        return remote(src, cbuf.at[slot(i)], c_s.at[slot(i)], c_r.at[slot(i)], peer_c, x)

    def over_ya(i):
        return remote(acc.at[aslot(i), :, 1 - y, :, left], ya.at[slot(i)], ya_s.at[slot(i)], ya_r.at[slot(i)], peer_y, x)

    def over_xa(i):
        return remote(acc.at[aslot(i), :, :, theirs, right], xa.at[slot(i)], xa_s.at[slot(i)], xa_r.at[slot(i)], clip, 1 - x)

    def over_xb(i):
        return remote(acc.at[aslot(i), :, y, theirs, left], xb.at[slot(i)], xb_s.at[slot(i)], xb_r.at[slot(i)], clip, 1 - x)

    def over_yb(i):
        return remote(acc.at[aslot(i), :, 1 - y, mine, right], yb.at[slot(i)], yb_s.at[slot(i)], yb_r.at[slot(i)], peer_y, x)

    def over_z(i, k):
        to = lax.rem(z + k, nz)
        return remote(tb.at[slot(i), to], zb.at[slot(i), k - 1], z_s.at[slot(i), k - 1], z_r.at[slot(i), k - 1],
                      clip + 4 * (to - z), x)

    def over_f(i):
        return remote(sb.at[slot(i)], fb.at[slot(i)], f_s.at[slot(i)], f_r.at[slot(i)], clip, 1 - x)

    def write(i):
        return pltpu.make_async_copy(ob.at[slot(i)], out.at[i], o_s.at[slot(i)])

    def credit(sem, who, frame, i):
        @pl.when(i + NBUF < n)
        def _():
            pl.semaphore_signal(sem, inc=1, device_id={"clip": who, "frame": frame}, device_id_type=MESH)

    def need(sem, i):
        @pl.when(i >= NBUF)
        def _():
            pl.semaphore_wait(sem, 1)

    def item(i):
        return jnp.logical_and(i >= 0, i < n)

    i = t - 6

    @pl.when(item(i))
    def _(i=i):
        write(i).wait()

    i = t

    @pl.when(item(i))
    def _(i=i):
        need(cred_c, i)
        first = 0
        for source, skip, count in sources:

            @pl.when(jnp.logical_and(i >= first, i < first + count))
            def _(source=source, offset=first - skip):
                over_c(i, source, offset).start()
                load(i, source, offset).start()

            first += count

    i = t - 1

    @pl.when(item(i))
    def _(i=i):
        over_c(i, sources[0][0], i).wait()
        load(i, sources[0][0], i).wait()
        a, b = aslot(i), slot(i)

        def body(k, carry):
            acc[a, k] = acc[a, k] + cbuf[b, k]
            return carry

        lax.fori_loop(0, nz, body, 0)
        credit(cred_c, peer_c, x, i)
        need(cred_y, i)
        need(cred_x, i)
        over_ya(i).start()
        over_xa(i).start()

    i = t - 2

    @pl.when(item(i))
    def _(i=i):
        over_ya(i).wait()
        over_xa(i).wait()
        a, b = aslot(i), slot(i)

        def body(k, carry):
            acc[a, k, y, :, left] = acc[a, k, y, :, left] + ya[b, k]
            acc[a, k, :, mine, right] = acc[a, k, :, mine, right] + xa[b, k]
            return carry

        lax.fori_loop(0, nz, body, 0)
        over_xb(i).start()
        over_yb(i).start()

    i = t - 3

    @pl.when(item(i))
    def _(i=i):
        over_xb(i).wait()
        over_yb(i).wait()
        a, b = aslot(i), slot(i)

        def body(k, carry):
            tb[b, k, :, left] = acc[a, k, y, mine, left] + xb[b, k]
            tb[b, k, :, right] = acc[a, k, y, mine, right] + yb[b, k]
            return carry

        lax.fori_loop(0, nz, body, 0)
        credit(cred_y, peer_y, x, i)
        credit(cred_x, clip, 1 - x, i)
        for k in range(1, nz):
            need(cred_z.at[k - 1], i)
            over_z(i, k).start()

    i = t - 4

    @pl.when(item(i))
    def _(i=i):
        for k in range(1, nz):
            over_z(i, k).wait()
        b = slot(i)
        total = tb[b, z].astype(F32)
        for k in range(1, nz):
            total = total + zb[b, k - 1].astype(F32)
        sb[b] = total.astype(BF16)
        for k in range(1, nz):
            sender = lax.rem(z + nz - k, nz)
            credit(cred_z.at[k - 1], clip + 4 * (sender - z), x, i)
        need(cred_f, i)
        over_f(i).start()

    i = t - 5

    @pl.when(item(i))
    def _(i=i):
        over_f(i).wait()
        b = slot(i)
        ob[b, mine, :] = sb[b].astype(F32)
        ob[b, theirs, :] = fb[b].astype(F32)
        credit(cred_f, clip, 1 - x, i)
        write(i).start()


def greet_reduce(nz, where):
    clip, z, y, c, x = where
    others = [(clip + 4 * (lax.rem(z + k, nz) - z), x, None) for k in range(1, nz)]
    greet(others + [
        (clip + 2 - 4 * y, x, None),
        (clip, 1 - x, None),
        (clip + 1 - 2 * c, x, None),
    ])


def exchange_tick(t, nz, where, small, totals, boxes, mod_box, sems):
    clip, z, y, c, x = where
    steps = [(clip, 1 - x), (clip + 1 - 2 * c, x), (clip + 2 - 4 * y, x)]
    bit = 1
    while bit < nz:
        flip = lax.rem(z // bit, 2)
        steps.append((clip + 4 * bit * (1 - 2 * flip), x))
        bit *= 2

    def copies(k):
        to, frame = steps[k]
        found = [
            remote(boxes[j].at[k, 0], boxes[j].at[k, 1], sems.at[j, 0, k], sems.at[j, 1, k], to, frame)
            for j in range(2)
        ]
        if k == 0:
            found.append(remote(small[0], mod_box, sems.at[2, 0, 0], sems.at[2, 1, 0], to, frame))
        return found

    for k in range(len(steps)):
        @pl.when(t == k + 1)
        def _(k=k):
            for copy in copies(k):
                copy.wait()
            for j in range(2):
                totals[1 + j][...] = boxes[j][k, 0].astype(F32) + boxes[j][k, 1].astype(F32)
            if k == 0:
                totals[0][...] = small[0][...] + mod_box[...]

        @pl.when(t == k)
        def _(k=k):
            for j in range(2):
                source = small[1 + j] if k == 0 else totals[1 + j]
                boxes[j][k, 0] = source[...].astype(BF16)
            for copy in copies(k):
                copy.start()


def exchange_steps(nz):
    return 3 + (nz - 1).bit_length()


def reduce_kernel(pick, nz, grads, small0, small1, small2, out, total0, total1, total2, *rest):
    n_comm = len(reduce_scratch(nz))
    comm, (box0, box1, mod_box, sems) = rest[:n_comm], rest[n_comm:]
    skip, n = pick
    where = place(4 * nz)
    clip, z, y, c, x = where
    greet_reduce(nz, where)

    def step(t, carry):
        exchange_tick(
            t, nz, where, (small0, small1, small2), (total0, total1, total2), (box0, box1), mod_box, sems
        )
        reduce_tick(t, n, nz, where, [(grads, skip, n)], out, *comm)
        return carry

    lax.fori_loop(0, n + REDUCE_TAIL, step, 0)


def reduce_scratch(nz):
    half = ROWS // 2
    rest = COLS - Y_FIRST
    dma = pltpu.SemaphoreType.DMA
    one = dma((NBUF,))
    regular = pltpu.SemaphoreType.REGULAR
    return [
        pltpu.VMEM((NACC, nz, 2, ROWS, COLS), BF16),
        pltpu.VMEM((NBUF, nz, 2, ROWS, COLS), BF16),
        pltpu.VMEM((NBUF, nz, ROWS, Y_FIRST), BF16),
        pltpu.VMEM((NBUF, nz, 2, half, rest), BF16),
        pltpu.VMEM((NBUF, nz, half, rest), BF16),
        pltpu.VMEM((NBUF, nz, half, Y_FIRST), BF16),
        pltpu.VMEM((NBUF, nz, half, COLS), BF16),
        pltpu.VMEM((NBUF, nz - 1, half, COLS), BF16),
        pltpu.VMEM((NBUF, half, COLS), BF16),
        pltpu.VMEM((NBUF, half, COLS), BF16),
        pltpu.VMEM((NBUF, ROWS, COLS), F32),
        one, one, one, one, one, one, one, one, one, one, one,
        dma((NBUF, nz - 1)), dma((NBUF, nz - 1)),
        one, one, one,
        regular, regular, regular, regular((nz - 1,)), regular,
    ]


def reduce_last(grads, pick, small, nz, cid):
    n = pick[1]
    steps = exchange_steps(nz)
    vmem = pl.BlockSpec(memory_space=pltpu.VMEM)
    return pl.pallas_call(
        functools.partial(reduce_kernel, pick, nz),
        out_shape=[jax.ShapeDtypeStruct((n, ROWS, COLS), F32)]
        + [jax.ShapeDtypeStruct(v.shape, F32) for v in small],
        in_specs=[pl.BlockSpec(memory_space=pl.ANY), vmem, vmem, vmem],
        out_specs=[pl.BlockSpec(memory_space=pl.ANY), vmem, vmem, vmem],
        scratch_shapes=reduce_scratch(nz)
        + [pltpu.VMEM((steps, 2) + v.shape, BF16) for v in small[1:]]
        + [pltpu.VMEM(small[0].shape, F32), pltpu.SemaphoreType.DMA((3, 2, steps))],
        compiler_params=pltpu.CompilerParams(
            collective_id=cid, has_side_effects=True, vmem_limit_bytes=48 * 1024 * 1024
        ),
        name="reduce_last",
    )(grads, *small)


CHUNK = 512
STEP_ROWS = 128
MIB = 1024 * 1024
GELU_C = 0.7978845608028654
GELU_A = 0.044715


def fixed(shape, **kw):
    zeros = (0,) * len(shape)
    return pl.BlockSpec(shape, lambda i: zeros, pipeline_mode=pl.Buffered(1), **kw)


def over_rows(tokens, body):
    def step(k, carry):
        body(pl.ds(pl.multiple_of(k * STEP_ROWS, STEP_ROWS), STEP_ROWS))
        return carry

    lax.fori_loop(0, tokens // STEP_ROWS, step, 0)


def down_rows(w_ref):
    groups = w_ref.shape[1] // ROWS
    return jnp.concatenate(
        [w_ref[s, c * ROWS : (c + 1) * ROWS, :] for c in range(groups) for s in range(2)], axis=0
    )


FRONT_ROWS = 256
GATHER_US = 5.0


def forward_plan(tokens, width):
    rows = tokens // FRONT_ROWS
    sizes = (rows, 3, width // 128, 1, rows, 4, rows)
    starts = [0]
    for size in sizes:
        starts.append(starts[-1] + size)
    return starts


def plan_gather(starts, spatial, need, n_items, nz):
    takes = (1.0, 2.6, 1.9 if spatial else 3.6, 2.2, 1.3, 6.5, 0.8)
    total = n_items + nz + 2
    counts, done, clock, last = [], 0, 0.0, -GATHER_US
    for section, (lo, hi) in enumerate(zip(starts, starts[1:])):
        for step in range(lo, hi):
            before = done
            while done < total and (done < need.get(step, 0) or clock - last >= GATHER_US):
                early = 3.0 if done < 6 else GATHER_US
                clock = max(clock, last + early)
                last = clock
                done += 1
            counts.append(done - before)
            clock += takes[section]
    return counts, total


def forward_body(
    spatial, shapes, wide, n_own, own_first, counts, total, nz,
    s_ref, m_ref, b_ref, ok_ref, shard_hbm, prev_hbm,
    na_ref, qkv_ref, att_ref, p_ref, proj_ref, mid_ref, nm_ref, act_ref, dact_ref, down_ref, res_ref, full_hbm, peer_hbm,
    n_scr, q_scr, a_scr, acc_ref, mid_scr, bias_ref, w_scr, d_scr, w_sem, d_sem, send_ref, send_sem, peer_sem, *sems,
):
    n_win, n_query, n_key, chunk = shapes
    tokens, width = acc_ref.shape
    starts = forward_plan(tokens, width)
    a0, a1, a2, a3, a4, a5, a6, end = starts
    step = pl.program_id(0)
    where = place(4 * nz)

    @pl.when(step == 0)
    def _():
        greet_gather(nz, where)

    lo = jnp.zeros((), jnp.int32)
    hi = jnp.zeros((), jnp.int32)
    for s, count in enumerate(counts):
        if count:
            lo = lo + count * (step > s).astype(jnp.int32)
            hi = hi + count * (step >= s).astype(jnp.int32)

    def tick(t, carry):
        gather_tick(t, n_own, nz, where, wide, shard_hbm, full_hbm, *sems)
        return carry

    lax.fori_loop(lo, hi, tick, 0)

    def item_ref(item):
        if item >= own_first:
            return full_hbm.at[item - own_first]
        return prev_hbm.at[PREV_ITEMS + item]

    ready = []
    done = 0
    for count in counts:
        done += count
        ready.append(done)

    def start_of(item, use):
        if item < own_first:
            return max(use - 1, 0)
        for s in range(max(use - 1, 0), use + 1):
            if ready[s] >= item - own_first + nz + 3:
                return s
        raise ValueError("late item")

    jobs = []
    uses = [(a1, 0), (a1 + 1, 1), (a1 + 2, 2), (a3, 3)] + [(a5 + i, UP_ITEMS[i]) for i in range(4)]
    for k, (use, item) in enumerate(uses):
        copy = pltpu.make_async_copy(item_ref(item), w_scr.at[k % 2], w_sem.at[k % 2])
        jobs.append((start_of(item, use), use, copy))
    for i in range(4):
        items = (DOWN_ITEMS[2 * (i // 2)], DOWN_ITEMS[2 * (i // 2) + 1])
        first = max(start_of(item, a5 + i) for item in items)
        for k, item in enumerate(items):
            source = item_ref(item).at[pl.ds((nz // 2) * (i % 2), nz // 2)]
            copy = pltpu.make_async_copy(source, d_scr.at[i % 2, k], d_sem.at[i % 2, k])
            jobs.append((first, a5 + i, copy))
    for first, use, copy in jobs:
        @pl.when(step == first)
        def _(copy=copy):
            copy.start()
    for first, use, copy in jobs:
        @pl.when(step == use)
        def _(copy=copy):
            copy.wait()

    def weight(k):
        return w_scr[k].reshape(width, width)

    def rows_at(i):
        return pl.ds(pl.multiple_of(i * FRONT_ROWS, FRONT_ROWS), FRONT_ROWS)

    @pl.when(step < a1)
    def _():
        normed, _ = norm_stats(s_ref[...].astype(F32))
        value = (normed * (1.0 + m_ref[1:2, :]) + m_ref[0:1, :]).astype(BF16)
        n_scr[rows_at(step), :] = value
        na_ref[...] = value

    @pl.when(jnp.logical_and(step >= a1, step < a2))
    def _():
        i = step - a1
        value = dot_nn(n_scr[...], weight(lax.rem(i, 2))).astype(BF16)
        q_scr[:, pl.ds(pl.multiple_of(i * width, width), width)] = value
        qkv_ref[...] = value

    @pl.when(jnp.logical_and(step >= a2, step < a3))
    def _():
        def lanes(k):
            return q_scr.at[:, pl.ds(pl.multiple_of(k * width + (step - a2) * 128, 128), 128)]

        attend_forward(
            spatial, n_win, n_query, n_key, chunk, lanes(0), lanes(1), lanes(2), b_ref, ok_ref, att_ref, p_ref, bias_ref
        )
        a_scr[:, pl.ds(pl.multiple_of((step - a2) * 128, 128), 128)] = att_ref[...]

    @pl.when(step == a3)
    def _():
        acc_ref[...] = dot_nn(a_scr[...], weight(1))

    @pl.when(jnp.logical_and(step >= a4, step < a5))
    def _():
        rows = rows_at(step - a4)
        proj = acc_ref[rows, :]
        proj_ref[...] = proj.astype(BF16)
        mid = s_ref[...].astype(F32) + m_ref[2:3, :] * proj
        mid_ref[...] = mid
        mid_scr[rows, :] = mid
        normed, _ = norm_stats(mid)
        value = (normed * (1.0 + m_ref[4:5, :]) + m_ref[3:4, :]).astype(BF16)
        n_scr[rows, :] = value
        nm_ref[...] = value

    @pl.when(jnp.logical_and(step >= a5, step < a6))
    def _():
        i = step - a5
        slot = lax.rem(i, 2)
        w_up = weight(slot)
        first = d_scr[slot, 0].reshape(-1, ROWS, width)
        second = d_scr[slot, 1].reshape(-1, ROWS, width)
        w_down = jnp.concatenate(
            [part for k in range(first.shape[0]) for part in (first[k], second[k])], axis=0
        )
        pieces = 4
        each = tokens // pieces
        ups = [dot_nn(n_scr[k * each : (k + 1) * each, :], w_up) for k in range(pieces)]
        for k in range(pieces):
            rows = slice(k * each, (k + 1) * each)
            up = ups[k]
            square = up * up
            tanh = jnp.tanh(up * (GELU_C + (GELU_C * GELU_A) * square))
            half = 0.5 + 0.5 * tanh
            act = up * half
            dact_ref[rows, :] = (
                half + act * (1.0 - tanh) * (GELU_C + (3.0 * GELU_C * GELU_A) * square)
            ).astype(BF16)
            act = act.astype(BF16)
            act_ref[rows, :] = act
            acc_ref[rows, :] = jnp.where(i == 0, 0.0, acc_ref[rows, :]) + dot_nn(act, w_down)

    @pl.when(step >= a6)
    def _():
        rows = rows_at(step - a6)
        down = acc_ref[rows, :]
        down_ref[...] = down.astype(BF16)
        res_ref[...] = (mid_scr[rows, :] + m_ref[5:6, :] * down).astype(res_ref.dtype)

    clip, _, _, _, x = where

    def to_peer(k):
        return remote(send_ref.at[k], peer_hbm.at[k], send_sem.at[k], peer_sem.at[k], clip, 1 - x)

    if spatial:
        @pl.when(step >= a6)
        def _():
            half = FRONT_ROWS // 2
            theirs = pl.ds(pl.multiple_of((1 - x) * half, half), half)
            send_ref[step - a6] = res_ref[theirs, :].astype(BF16)
            to_peer(step - a6).start()

    @pl.when(step == end - 1)
    def _():
        lax.fori_loop(sum(counts), total, tick, 0)
        if spatial:
            for k in range(send_ref.shape[0]):
                to_peer(k).wait()


DOWN_ITEMS = (4, 5, 8, 9)
UP_ITEMS = (6, 7, 10, 11)
PREV_ITEMS = 12


def block_forward(stream, mods, shard, wide, n_own, prev, own_first, spread, key_ok, spatial, result_type, nz, cid):
    tokens, width = stream.shape
    shapes = attention_shapes(spatial, tokens)
    n_win, n_query, n_key, _ = shapes
    pairs = width // 128
    a0, a1, a2, a3, a4, a5, a6, end = starts = forward_plan(tokens, width)
    n_send = tokens // FRONT_ROWS
    tail = spread.shape[1:]
    zeros = (0,) * len(tail)
    need = {}
    for i in range(3):
        need[a1 + i] = i
    need[a3] = 3
    for i in range(4):
        need[a5 + i] = max(UP_ITEMS[i], DOWN_ITEMS[2 * (i // 2) + 1])
    need = {s: item - own_first + nz + 3 for s, item in need.items() if item >= own_first}
    counts, total = plan_gather(starts, spatial, need, n_own, nz)

    def at(start, stop):
        return lambda i: jnp.clip(i - start, 0, stop - start - 1)

    def row_block(place_of):
        return pl.BlockSpec((FRONT_ROWS, width), lambda i: (place_of(i), 0))

    def s_at(i):
        return jnp.where(i < a1, i, at(a4, a5)(i))

    heads = at(a2, a3)
    anywhere = pl.BlockSpec(memory_space=pl.ANY)
    hidden = pl.BlockSpec((tokens, width), lambda i: (0, at(a5, a6)(i)))
    body = functools.partial(forward_body, spatial, shapes, wide, n_own, own_first, counts, total, nz)
    extra = [] if prev is None else [prev]
    if prev is None:
        whole = body

        def body(*refs):
            return whole(*refs[:5], None, *refs[5:])

    dma = pltpu.SemaphoreType.DMA
    bf16_rows = jax.ShapeDtypeStruct((tokens, width), BF16)
    outs = pl.pallas_call(
        body,
        grid=(end,),
        in_specs=[
            row_block(s_at),
            fixed(mods.shape),
            pl.BlockSpec((2,) + tail, lambda i: (heads(i),) + zeros),
            pl.BlockSpec((n_win, 1, n_key), lambda i: (0, 0, 0)),
            anywhere,
        ] + [anywhere] * len(extra),
        out_specs=[
            row_block(at(a0, a1)),
            pl.BlockSpec((tokens, width), lambda i: (0, at(a1, a2)(i))),
            pl.BlockSpec((tokens, 128), lambda i: (0, heads(i))),
            pl.BlockSpec((2, n_win, n_query, n_key), lambda i: (heads(i), 0, 0, 0)),
            row_block(at(a4, a5)),
            row_block(at(a4, a5)),
            row_block(at(a4, a5)),
            hidden,
            hidden,
            row_block(at(a6, end)),
            row_block(at(a6, end)),
            anywhere,
            anywhere,
        ],
        out_shape=[
            bf16_rows,
            jax.ShapeDtypeStruct((tokens, 3 * width), BF16),
            bf16_rows,
            jax.ShapeDtypeStruct((2 * pairs, n_win, n_query, n_key), BF16),
            bf16_rows,
            jax.ShapeDtypeStruct((tokens, width), F32),
            bf16_rows,
            jax.ShapeDtypeStruct((tokens, 4 * width), BF16),
            jax.ShapeDtypeStruct((tokens, 4 * width), BF16),
            bf16_rows,
            jax.ShapeDtypeStruct((tokens, width), result_type),
            jax.ShapeDtypeStruct((n_own, nz, 2, 2, ROWS, COLS), BF16),
            jax.ShapeDtypeStruct((n_send, FRONT_ROWS // 2, width), BF16),
        ],
        scratch_shapes=[
            pltpu.VMEM((tokens, width), BF16),
            pltpu.VMEM((tokens, 3 * width), BF16),
            pltpu.VMEM((tokens, width), BF16),
            pltpu.VMEM((tokens, width), F32),
            pltpu.VMEM((tokens, width), F32),
            pltpu.VMEM((2, n_query, n_key), F32),
            pltpu.VMEM((2, nz, 2, 2, ROWS, COLS), BF16),
            pltpu.VMEM((2, 2, nz // 2, 2, 2, ROWS, COLS), BF16),
            dma((2,)),
            dma((2, 2)),
            pltpu.VMEM((n_send, FRONT_ROWS // 2, width), BF16),
            dma((n_send,)),
            dma((n_send,)),
        ] + gather_sems(n_own, nz),
        compiler_params=pltpu.CompilerParams(
            collective_id=cid, has_side_effects=True, vmem_limit_bytes=64 * MIB
        ),
        name="block_forward",
    )(stream, mods, spread, key_ok, shard, *extra)
    normed_a, qkv, att, probs, proj, mid, normed_m, act, dact, down, result, full, peer = outs
    saved = (stream, normed_a, qkv, probs, att, proj, mid, normed_m, act, dact, down)
    return result, saved, full, peer


def norm_back_rows(values, scale_row, grad):
    normed, inv = norm_stats(values)
    u = grad * (1.0 + scale_row)
    out = (
        u
        - jnp.mean(u, axis=-1, keepdims=True)
        - normed * jnp.mean(u * normed, axis=-1, keepdims=True)
    ) * inv
    return out, jnp.sum(grad, axis=0, keepdims=True), jnp.sum(grad * normed, axis=0, keepdims=True)


BLOCK_ROWS = 128
TICK_US = (5.5, 6.5)


def backward_plan(tokens, width):
    rows = tokens // BLOCK_ROWS
    chunks = 4 * width // CHUNK
    halves = width // CHUNK
    pairs = width // 128
    sizes = (rows, chunks, rows, halves, pairs, 3 * halves, rows, 3 * halves)
    starts = [0]
    for size in sizes:
        starts.append(starts[-1] + size)
    return starts


def backward_body(
    spatial, shapes, n_prev, n_own, tick_steps, nz,
    g_ref, down_ref, mid_ref, proj_ref, s_ref, m_ref, act_ref, dact_ref, w_ref, up_ref, dn_ref,
    q_ref, k_ref, v_ref, p_ref, nm_hbm, att_hbm, na_hbm, mixed_hbm, prev_hbm,
    out_ref, dm_ref, rows_ref, grads_hbm, share_hbm, peer_hbm, swap_hbm,
    res_ref, gv_ref, e_ref, gm_ref, ga_ref, gq_ref, db_ref, gdb_ref, gub_ref,
    res_sem, gd_sem, gu_sem, send_ref, send_sem, peer_sem, mix_sem, swap_sem, *comm,
):
    n_win, n_query, n_key, chunk = shapes
    tokens, width = e_ref.shape
    starts = backward_plan(tokens, width)
    a0, a1, a2, a3, a4, a5, a6, a7, end = starts
    halves = width // CHUNK
    step = pl.program_id(0)
    where = place(4 * nz)
    n_items = n_prev + n_own
    sources = [(prev_hbm, 9, n_prev)] if n_prev else []
    sources.append((grads_hbm, 0, n_own))

    @pl.when(step == 0)
    def _():
        greet_reduce(nz, where)

    def tick(t):
        reduce_tick(t, n_items, nz, where, sources, share_hbm, *comm)

    due = jnp.zeros((), jnp.bool_)
    passed = jnp.zeros((), jnp.int32)
    for s in tick_steps:
        due = jnp.logical_or(due, step == s)
        passed = passed + (step > s).astype(jnp.int32)

    def resident(source):
        return pltpu.make_async_copy(source, res_ref, res_sem)

    def put_down(i):
        slot = lax.rem(i, 2)
        target = grads_hbm.at[pl.ds(4 * (i // 4) + 2, 2), pl.ds(lax.rem(i, 4), 1)]
        return pltpu.make_async_copy(gdb_ref.at[slot], target, gd_sem.at[slot])

    def put_cols(i, item, half):
        slot = lax.rem(i, 2)
        cols = pl.ds(pl.multiple_of(half * CHUNK, CHUNK), CHUNK)
        target = grads_hbm.at[item, :, :, :, :, cols]
        return pltpu.make_async_copy(gub_ref.at[slot], target, gu_sem.at[slot])

    def keep_cols(i, values):
        gub_ref[lax.rem(i, 2)] = values.reshape(gub_ref.shape[1:])

    def rows_at(i):
        return pl.ds(pl.multiple_of(i * BLOCK_ROWS, BLOCK_ROWS), BLOCK_ROWS)

    def add_e(first, left, right):
        part = tokens // 2
        for k in range(2):
            rows = slice(k * part, (k + 1) * part)
            value = dot_nt(left[rows], right)

            @pl.when(first)
            def _(rows=rows, value=value):
                e_ref[rows, :] = value

            @pl.when(jnp.logical_not(first))
            def _(rows=rows, value=value):
                e_ref[rows, :] += value

    @pl.when(step == 0)
    def _():
        resident(nm_hbm).start()
        rows_ref[...] = jnp.zeros_like(rows_ref)

    @pl.when(step < a1)
    def _():
        grad = g_ref[...].astype(F32)
        gv_ref[rows_at(step), :] = (m_ref[5:6, :] * grad).astype(BF16)
        rows_ref[5:6, :] += jnp.sum(grad * down_ref[...].astype(F32), axis=0, keepdims=True)

    @pl.when(step == a1)
    def _():
        resident(nm_hbm).wait()

    @pl.when(jnp.logical_and(step >= a1, step < a2))
    def _():
        i = step - a1

        @pl.when(i >= 2)
        def _():
            put_down(i).wait()
            put_cols(i, 4, 0).wait()

        gdv = gv_ref[...]
        grad_act = dot_nt(gdv, down_rows(dn_ref))
        gup = (grad_act * dact_ref[...].astype(F32)).astype(BF16)
        slot = lax.rem(i, 2)
        grad_down = dot_tn(act_ref[...], gdv).astype(BF16)
        for k in range(CHUNK // ROWS):
            gdb_ref[slot, k % 2, 0, k // 4, (k // 2) % 2] = grad_down[k * ROWS : (k + 1) * ROWS, :]
        put_down(i).start()
        keep_cols(i, dot_tn(res_ref[...], gup).astype(BF16))
        put_cols(i, 4 * (i // 4) + lax.rem(i // 2, 2), lax.rem(i, halves)).start()
        add_e(i == 0, gup, up_ref[0])

    @pl.when(step == a2)
    def _():
        resident(att_hbm).start()
        for k in range(2):
            put_down(k).wait()
            put_cols(k, 4, 0).wait()

    @pl.when(jnp.logical_and(step >= a2, step < a3))
    def _():
        rows = rows_at(step - a2)
        out, shift, scale = norm_back_rows(mid_ref[...], m_ref[4:5, :], e_ref[rows, :])
        grad_mid = out + g_ref[...].astype(F32)
        gm_ref[rows, :] = grad_mid
        gv_ref[rows, :] = (m_ref[2:3, :] * grad_mid).astype(BF16)
        rows_ref[3:4, :] += shift
        rows_ref[4:5, :] += scale
        rows_ref[2:3, :] += jnp.sum(grad_mid * proj_ref[...].astype(F32), axis=0, keepdims=True)

    @pl.when(step == a3)
    def _():
        resident(att_hbm).wait()

    @pl.when(jnp.logical_and(step >= a3, step < a4))
    def _():
        i = step - a3
        part = gv_ref[:, pl.ds(pl.multiple_of(i * CHUNK, CHUNK), CHUNK)]
        keep_cols(i, dot_tn(res_ref[...], part).astype(BF16))
        put_cols(i, 8, i).start()
        add_e(i == 0, part, w_ref[0])

    @pl.when(step == a4)
    def _():
        resident(na_hbm).start()
        ga_ref[...] = e_ref[...].astype(BF16)
        for k in range(2):
            put_cols(k, 8, 0).wait()

    @pl.when(jnp.logical_and(step >= a4, step < a5))
    def _():
        head = step - a4
        lanes = pl.ds(pl.multiple_of(head * 128, 128), 128)
        attend_backward(
            spatial, n_win, n_query, n_key, chunk, head,
            q_ref, k_ref, v_ref, ga_ref.at[:, lanes], p_ref, gq_ref, dm_ref, db_ref,
        )

    @pl.when(jnp.logical_and(step >= a5, step < a6))
    def _():
        i = step - a5
        add_e(i == 0, gq_ref[:, pl.ds(pl.multiple_of(i * CHUNK, CHUNK), CHUNK)], w_ref[0])

    clip, _, _, _, x = where

    def to_peer(k):
        return remote(send_ref.at[k], peer_hbm.at[k], send_sem.at[k], peer_sem.at[k], clip, 1 - x)

    def mixed_to_peer(k):
        block = 4 * (k // 2) + 2 * (1 - x) + k % 2
        rows = pl.ds(pl.multiple_of(block * BLOCK_ROWS, BLOCK_ROWS), BLOCK_ROWS)
        return remote(mixed_hbm.at[rows], swap_hbm.at[k], mix_sem.at[k], swap_sem.at[k], clip, 1 - x)

    if not spatial:
        @pl.when(step == 0)
        def _():
            for k in range(send_ref.shape[0]):
                mixed_to_peer(k).start()

    @pl.when(jnp.logical_and(step >= a6, step < a7))
    def _():
        rows = rows_at(step - a6)
        out, shift, scale = norm_back_rows(s_ref[...].astype(F32), m_ref[1:2, :], e_ref[rows, :])
        out_ref[...] = (out + gm_ref[rows, :]).astype(out_ref.dtype)
        rows_ref[0:1, :] += shift
        rows_ref[1:2, :] += scale

    if not spatial:
        block = step - a6
        half = lax.rem(block, 4) // 2

        @pl.when(jnp.logical_and(jnp.logical_and(step >= a6, step < a7), half == 1 - x))
        def _():
            k = 2 * (block // 4) + lax.rem(block, 2)
            send_ref[k] = out_ref[...].astype(BF16)
            to_peer(k).start()

    @pl.when(step == a7)
    def _():
        resident(na_hbm).wait()

    @pl.when(step >= a7)
    def _():
        i = step - a7

        @pl.when(i >= 2)
        def _():
            put_cols(i, 8, 0).wait()

        part = gq_ref[:, pl.ds(pl.multiple_of(i * CHUNK, CHUNK), CHUNK)]
        keep_cols(i, dot_tn(res_ref[...], part).astype(BF16))
        put_cols(i, 9 + i // halves, lax.rem(i, halves)).start()

    @pl.when(due)
    def _():
        tick(passed)

    @pl.when(step == end - 1)
    def _():
        for k in range(2):
            put_cols(k, 8, 0).wait()

        def rest(t, carry):
            tick(t)
            return carry

        lax.fori_loop(len(tick_steps), n_items + REDUCE_TAIL, rest, 0)
        if not spatial:
            for k in range(send_ref.shape[0]):
                to_peer(k).wait()
                mixed_to_peer(k).wait()


def plan_ticks(starts, spatial, ready, spacing):
    takes = (0.6, 5.0, 0.9, 2.5, 3.6 if spatial else 4.6, 1.7, 0.9, 1.7)
    steps, clock, last = [], 0.0, -spacing
    for section, (lo, hi) in enumerate(zip(starts, starts[1:])):
        for step in range(lo, hi):
            clock += takes[section]
            k = len(steps)
            busy = section == 7 and not spatial
            if not busy and (k >= len(ready) or step >= ready[k]) and clock - last >= spacing:
                steps.append(step)
                last = clock
    return tuple(steps)


def block_backward(grad, saved, mods, w_first, first_base, w_second, second_base, spread_shape, spatial, out_type, mixed, prev, nz, cid):
    stream, normed_a, qkv, probs, att, proj, mid, normed_m, act, dact, down = saved
    tokens, width = mid.shape
    shapes = attention_shapes(spatial, tokens)
    n_win, n_query, n_key, _ = shapes
    pairs = width // 128
    halves = width // CHUNK
    a0, a1, a2, a3, a4, a5, a6, a7, end = backward_plan(tokens, width)
    tail = spread_shape[1:]
    zeros = (0,) * len(tail)

    def at(start, stop):
        return lambda i: jnp.clip(i - start, 0, max(stop - start - 1, 0))

    def row_block(place_of):
        return pl.BlockSpec((BLOCK_ROWS, width), lambda i: (place_of(i), 0))

    def g_at(i):
        return jnp.where(i < a1, i, at(a2, a3)(i))

    def first_at(i):
        third = at(a5, a6)(i)
        item = jnp.where(i < a5, 3, third // halves)
        half = jnp.where(i < a5, at(a3, a4)(i), third % halves)
        return (first_base + item, 0, half)

    def up_at(i):
        k = at(a1, a2)(i)
        return (second_base + 2 + 4 * (k // 4) + (k // 2) % 2, 0, k % 2)

    def down_at(i):
        k = at(a1, a2)(i)
        return (second_base // 2 + 2 * (k // 4), k % 4, 0)

    heads = at(a4, a5)
    hidden = pl.BlockSpec((tokens, CHUNK), lambda i: (0, at(a1, a2)(i)))
    anywhere = pl.BlockSpec(memory_space=pl.ANY)
    n_own = 9
    n_prev = 0 if prev is None else 3
    n_items = n_prev + n_own
    extra = [] if prev is None else [prev]
    n_send = tokens // (2 * BLOCK_ROWS)
    ready = [0] * n_prev + [a1 + 3, a1 + 5, a1 + 5, a1 + 5, a1 + 7, a2, a2, a2, a4]
    tick_steps = plan_ticks((a0, a1, a2, a3, a4, a5, a6, a7, end), spatial, ready, TICK_US[spatial])
    body = functools.partial(backward_body, spatial, shapes, n_prev, n_own, tick_steps, nz)
    if prev is None:
        whole = body

        def body(*refs):
            return whole(*refs[:19], None, *refs[19:])

    dma = pltpu.SemaphoreType.DMA
    return pl.pallas_call(
        body,
        grid=(end,),
        in_specs=[
            row_block(g_at),
            row_block(at(a0, a1)),
            row_block(at(a2, a3)),
            row_block(at(a2, a3)),
            row_block(at(a6, a7)),
            fixed(mods.shape),
            hidden,
            hidden,
            pl.BlockSpec((1, width, CHUNK), first_at),
            pl.BlockSpec((1, width, CHUNK), up_at),
            pl.BlockSpec((2, CHUNK // 2, width), down_at),
            pl.BlockSpec((tokens, 128), lambda i: (0, heads(i))),
            pl.BlockSpec((tokens, 128), lambda i: (0, pairs + heads(i))),
            pl.BlockSpec((tokens, 128), lambda i: (0, 2 * pairs + heads(i))),
            pl.BlockSpec((2, n_win, n_query, n_key), lambda i: (heads(i), 0, 0, 0)),
            anywhere, anywhere, anywhere, anywhere,
        ] + [anywhere] * len(extra),
        out_specs=[
            row_block(at(a6, a7)),
            pl.BlockSpec((2,) + tail, lambda i: (heads(i),) + zeros),
            pl.BlockSpec((8, width), lambda i: (0, 0)),
            anywhere,
            anywhere,
            anywhere,
            anywhere,
        ],
        out_shape=[
            jax.ShapeDtypeStruct((tokens, width), out_type),
            jax.ShapeDtypeStruct(spread_shape, F32),
            jax.ShapeDtypeStruct((8, width), F32),
            jax.ShapeDtypeStruct((12, nz, 2, 2, ROWS, COLS), BF16),
            jax.ShapeDtypeStruct((n_items, ROWS, COLS), F32),
            jax.ShapeDtypeStruct((n_send, BLOCK_ROWS, width), BF16),
            jax.ShapeDtypeStruct((n_send, BLOCK_ROWS, width), BF16),
        ],
        scratch_shapes=[
            pltpu.VMEM((tokens, width), BF16),
            pltpu.VMEM((tokens, width), BF16),
            pltpu.VMEM((tokens, width), F32),
            pltpu.VMEM((tokens, width), F32),
            pltpu.VMEM((tokens, width), BF16),
            pltpu.VMEM((tokens, 3 * width), BF16),
            pltpu.VMEM((2, n_query, n_key), F32),
            pltpu.VMEM((2, 2, 1, 2, 2, ROWS, COLS), BF16),
            pltpu.VMEM((2, nz, 2, 2, ROWS, CHUNK), BF16),
            dma,
            dma((2,)),
            dma((2,)),
            pltpu.VMEM((n_send, BLOCK_ROWS, width), BF16),
            dma((n_send,)),
            dma((n_send,)),
            dma((n_send,)),
            dma((n_send,)),
        ] + reduce_scratch(nz),
        compiler_params=pltpu.CompilerParams(
            collective_id=cid, has_side_effects=True, vmem_limit_bytes=64 * MIB
        ),
        name="block_backward",
    )(grad, down, mid, proj, stream, mods, act, dact, w_first, w_second, w_second, qkv, qkv, qkv, probs,
      normed_m, att, normed_a, mixed, *extra)


def swap_rows(values, me, swap, recv=None):
    keep = lax.dynamic_index_in_dim(values, me, 1, keepdims=False)
    if recv is None:
        send = lax.dynamic_index_in_dim(values, 1 - me, 1, keepdims=False)
        recv = lax.ppermute(send.astype(BF16), "frame", swap)
    recv = recv.reshape(keep.shape).astype(values.dtype)
    first = jnp.where(me == 0, keep, recv)
    second = jnp.where(me == 0, recv, keep)
    full = jnp.concatenate([first, second], axis=0)
    return full.transpose(2, 0, 1, 3, 4).reshape(-1, values.shape[-1])


def unswap_rows(values, me, swap, n_cw, f_l, recv=None):
    depth = values.shape[-1]
    full = values.reshape(n_cw, 2, f_l, TWIN, TWIN, depth)
    keep = lax.dynamic_index_in_dim(full, me, 1, keepdims=False)
    if recv is None:
        send = lax.dynamic_index_in_dim(full, 1 - me, 1, keepdims=False)
        recv = lax.ppermute(send.astype(BF16), "frame", swap)
    recv = recv.reshape(keep.shape).astype(values.dtype)
    first = jnp.where(me == 0, keep, recv)
    second = jnp.where(me == 0, recv, keep)
    both = jnp.stack([first, second], axis=0)
    return both.transpose(2, 0, 3, 1, 4, 5).reshape(-1, depth)


def pack_shards(shards, b):
    w_qkv, w_proj, w_up, w_down = [w[:, b] for w in shards]
    first = w_qkv.reshape(ROWS, 3, COLS).transpose(1, 0, 2)
    ups = w_up.reshape(ROWS, 2, 8, 2, 128).transpose(3, 1, 0, 2, 4).reshape(4, ROWS, COLS)
    downs = w_down.reshape(-1, ROWS, COLS)
    return [first, w_proj[None]], [downs[0:2], ups[0:2], downs[2:4], ups[2:4]]


def on_device(
    frames_in, size_group, modulation, w_qkv, w_proj, w_up, w_down, table_sp, table_st, cotangent
):
    n_clips, f_l, n_rows, n_cols, width = frames_in.shape
    me = lax.axis_index("frame")
    swap = [(0, 1), (1, 0)]
    n_cw = n_cols // TWIN
    nz = lax.axis_size("clip") // 4
    natural = (f_l, 2, TWIN, n_cw, TWIN, width)
    shards = (w_qkv, w_proj, w_up, w_down)
    packed = [pack_shards(shards, b) for b in range(2)]
    early = jnp.concatenate(packed[0][0] + packed[0][1] + packed[1][0], axis=0)
    late = jnp.concatenate(packed[1][1], axis=0)
    limit = n_cols - 3 * (2 - size_group[0])
    wide = (jnp.arange(n_cols, dtype=jnp.int32) < limit).astype(F32)
    ok_sp = jnp.broadcast_to(wide[None, None, None, :], (f_l, 1, n_rows, n_cols))
    ok_sp = ok_sp.reshape(f_l, 1, n_rows * n_cols)
    frame_ok = (jnp.arange(KEYF) < FILLED).astype(F32)
    ok_st = wide.reshape(n_cw, 1, 1, TWIN) * frame_ok[None, :, None, None]
    ok_st = jnp.broadcast_to(ok_st, (n_cw, KEYF, TWIN, TWIN)).reshape(n_cw, 1, -1)
    spread0 = spread_sp(table_sp)
    spread1 = spread_st(table_st)
    mods = modulation[0].reshape(2, 6, width)
    mods = jnp.pad(mods, ((0, 0), (0, 2), (0, 0)))
    cot = swap_rows(cotangent.reshape(natural), me, swap)
    stream0 = frames_in.reshape(-1, width)
    mid_stream, saved0, full0, peer0 = block_forward(
        stream0, mods[0], early, 2, 16, None, 0, spread0, ok_sp, True, F32, nz, 1
    )
    stream1 = swap_rows(mid_stream.reshape(natural), me, swap, peer0)
    end_stream, saved1, full1, _ = block_forward(
        stream1, mods[1], late, 1, 8, full0, 4, spread1, ok_st, False, BF16, nz, 5
    )
    full0 = full0.reshape(-1, width, width)
    full1 = full1.reshape(-1, width, width)
    grad1, gspread1, rows1, gw1, shares1, peer1, mixed1 = block_backward(
        cot, saved1, mods[1], full0, 12, full1, 0, spread1.shape, False, F32, end_stream, None, nz, 2
    )
    mixed = unswap_rows(end_stream, me, swap, n_cw, f_l, mixed1).reshape(frames_in.shape)
    grad_mid = unswap_rows(grad1, me, swap, n_cw, f_l, peer1)
    grad0, gspread0, rows0, gw0, shares0, _, _ = block_backward(
        grad_mid, saved0, mods[0], full0, 0, full0, 4, spread0.shape, True, BF16, end_stream, gw1, nz, 3
    )

    def wide_pad(table):
        return jnp.pad(table, ((0, 0), (0, -table.shape[1] % 128)))

    small = (
        jnp.pad(jnp.concatenate([rows0[:6], rows1[:6]], axis=0), ((0, 4), (0, 0))),
        wide_pad(gather_sp(gspread0)),
        wide_pad(gather_st(gspread1)),
    )
    last, mods_sum, sp_sum, st_sum = reduce_last(gw0, (9, 3), small, nz, 4)

    def pair(first, second):
        return jnp.stack([first, second], axis=1)

    def qkv_of(items):
        return jnp.concatenate([items[0], items[1], items[2]], axis=-1)

    def up_of(items):
        parts = jnp.stack([items[0], items[1], items[4], items[5]]).reshape(2, 2, ROWS, 8, 128)
        return parts.transpose(2, 1, 3, 0, 4).reshape(ROWS, 4 * COLS)

    def down_of(items):
        return jnp.concatenate([items[2], items[3], items[6], items[7]], axis=0)

    own0 = shares0[3:]
    outs = (
        pair(qkv_of(last), qkv_of(shares0[0:3])),
        pair(own0[8], shares1[8]),
        pair(up_of(own0), up_of(shares1)),
        pair(down_of(own0), down_of(shares1)),
    )
    mod_grad = mods_sum[:12][None]
    g_sp = sp_sum[:, : table_sp.shape[1]]
    g_st = st_sum[:, : table_st.shape[1]]
    grad_in = grad0.reshape(frames_in.shape)
    return (mixed, grad_in, mod_grad, outs[0], outs[1], outs[2], outs[3], g_sp, g_st)


HIGHEST = lax.Precision.HIGHEST


def layer_norm(values):
    centered = values - jnp.mean(values, axis=-1, keepdims=True)
    spread = jnp.mean(centered * centered, axis=-1, keepdims=True)
    return centered * lax.rsqrt(spread + NORM_EPS)


def modulate(values, shift_row, scale_row):
    return layer_norm(values) * (1.0 + scale_row) + shift_row


def gelu_tanh(values):
    return jax.nn.gelu(values, approximate=True)


def row_of(mod_rows, which):
    return mod_rows[:, which][:, None, None, None, :]


def clip_sum(values):
    return jnp.sum(values, axis=(1, 2, 3))


def flat_dot(values, weight):
    flat_in = values.reshape(-1, values.shape[-1])
    flat_out = jnp.dot(flat_in, weight, preferred_element_type=jnp.float32)
    return flat_out.reshape(values.shape[:-1] + (weight.shape[1],))


def back_dot(grad_values, weight):
    flat_in = grad_values.reshape(-1, grad_values.shape[-1])
    flat_out = jnp.einsum("nb,ab->na", flat_in, weight, preferred_element_type=jnp.float32)
    return flat_out.reshape(grad_values.shape[:-1] + (weight.shape[0],))


def outer_dot(left_values, right_values):
    left_flat = left_values.reshape(-1, left_values.shape[-1])
    right_flat = right_values.reshape(-1, right_values.shape[-1])
    return jnp.einsum("na,nb->ab", left_flat, right_flat, preferred_element_type=jnp.float32)


def split_heads(values, n_heads):
    return values.reshape(values.shape[0], values.shape[1], n_heads, -1)


def offset_pick(side_len):
    position = jnp.arange(side_len, dtype=jnp.int32)
    offsets = position[:, None] - position[None, :] + side_len - 1
    targets = jnp.arange(2 * side_len - 1, dtype=jnp.int32)
    return (offsets[:, :, None] == targets[None, None, :]).astype(jnp.float32)


def expand_bias(table, side_len):
    one_hot = offset_pick(side_len)
    rows_done = jnp.einsum("hab,xya->hxyb", table, one_hot, precision=HIGHEST)
    full_bias = jnp.einsum("hxyb,uvb->hxuyv", rows_done, one_hot, precision=HIGHEST)
    return full_bias.reshape(table.shape[0], side_len * side_len, side_len * side_len)


def cube_bias(table_st, first_frame, local_frames):
    n_heads = table_st.shape[0]
    span_frames = 2 * FRAMES - 1
    side_span = 2 * TWIN - 1
    table_cube = table_st.reshape(n_heads, span_frames, side_span * side_span)
    query_frames = first_frame + jnp.arange(local_frames, dtype=jnp.int32)
    key_frames = jnp.arange(FRAMES, dtype=jnp.int32)
    offsets = query_frames[:, None] - key_frames[None, :] + FRAMES - 1
    choose = (
        offsets[:, :, None] == jnp.arange(span_frames, dtype=jnp.int32)[None, None, :]
    ).astype(jnp.float32)
    picked = jnp.einsum("hoz,jfo->hjfz", table_cube, choose, precision=HIGHEST)
    squares = expand_bias(picked.reshape(-1, side_span, side_span), TWIN)
    squares = squares.reshape(n_heads, local_frames, FRAMES, TWIN * TWIN, TWIN * TWIN)
    squares = squares.transpose(0, 1, 3, 2, 4)
    return squares.reshape(n_heads, local_frames * TWIN * TWIN, FRAMES * TWIN * TWIN)


def spatial_windows(values):
    n_clips, n_frames, n_rows, n_cols, n_depth = values.shape
    blocked = values.reshape(n_clips, n_frames, n_rows // SWIN, SWIN, n_cols // SWIN, SWIN, n_depth)
    return blocked.transpose(0, 1, 2, 4, 3, 5, 6).reshape(-1, SWIN * SWIN, n_depth)


def spatial_unwindow(values, full_shape):
    n_clips, n_frames, n_rows, n_cols, n_depth = full_shape
    blocked = values.reshape(n_clips, n_frames, n_rows // SWIN, n_cols // SWIN, SWIN, SWIN, n_depth)
    return blocked.transpose(0, 1, 2, 4, 3, 5, 6).reshape(full_shape)


def cube_windows(values):
    n_clips, n_frames, n_rows, n_cols, n_depth = values.shape
    blocked = values.reshape(n_clips, n_frames, n_rows // TWIN, TWIN, n_cols // TWIN, TWIN, n_depth)
    blocked = blocked.transpose(0, 2, 4, 1, 3, 5, 6)
    return blocked.reshape(
        n_clips * (n_rows // TWIN) * (n_cols // TWIN), n_frames * TWIN * TWIN, n_depth
    )


def cube_unwindow(values, full_shape):
    n_clips, n_frames, n_rows, n_cols, n_depth = full_shape
    blocked = values.reshape(n_clips, n_rows // TWIN, n_cols // TWIN, n_frames, TWIN, TWIN, n_depth)
    return blocked.transpose(0, 3, 1, 4, 2, 5, 6).reshape(full_shape)


def soft_scores(query_win, key_win, bias, key_ok, score_scale):
    scores = jnp.einsum("nqhd,nkhd->nhqk", query_win, key_win, preferred_element_type=jnp.float32)
    scores = scores * score_scale + bias[None]
    scores = jnp.where(key_ok[:, None, None, :], scores, NEG_FILL)
    row_top = jnp.max(scores, axis=-1, keepdims=True)
    expo_values = jnp.exp(scores - row_top)
    return expo_values / jnp.sum(expo_values, axis=-1, keepdims=True)


def general_forward(
    stream,
    mod_rows,
    weights,
    n_heads,
    bias,
    key_ok,
    to_windows,
    from_windows,
    fetch_keys,
    score_scale,
):
    qkv_w, proj_w, up_w, down_w = weights
    width_d = stream.shape[-1]
    normed_a = modulate(stream, row_of(mod_rows, 0), row_of(mod_rows, 1)).astype(jnp.bfloat16)
    qkv_values = flat_dot(normed_a, qkv_w).astype(jnp.bfloat16)
    key_local = qkv_values[..., width_d : 2 * width_d]
    value_local = qkv_values[..., 2 * width_d :]
    query_win = split_heads(to_windows(qkv_values[..., :width_d]), n_heads)
    key_flat, value_flat = fetch_keys(key_local, value_local)
    key_win = split_heads(key_flat, n_heads)
    value_win = split_heads(value_flat, n_heads)
    soft_probs = soft_scores(query_win, key_win, bias, key_ok, score_scale)
    att_win = jnp.einsum(
        "nhqk,nkhd->nqhd",
        soft_probs.astype(jnp.bfloat16),
        value_win,
        preferred_element_type=jnp.float32,
    ).astype(jnp.bfloat16)
    att_out = from_windows(
        att_win.reshape(att_win.shape[0], att_win.shape[1], width_d), stream.shape
    )
    proj_out = flat_dot(att_out, proj_w)
    mid_stream = stream + row_of(mod_rows, 2) * proj_out
    normed_m = modulate(mid_stream, row_of(mod_rows, 3), row_of(mod_rows, 4)).astype(jnp.bfloat16)
    up_value = flat_dot(normed_m, up_w)
    active = gelu_tanh(up_value).astype(jnp.bfloat16)
    down_out = flat_dot(active, down_w)
    result = mid_stream + row_of(mod_rows, 5) * down_out
    saved = (
        stream,
        normed_a,
        query_win,
        key_win,
        value_win,
        key_local,
        value_local,
        att_out,
        proj_out,
        mid_stream,
        normed_m,
        up_value,
        active,
        down_out,
    )
    return (result, saved)


def general_backward(
    grad_out,
    saved,
    mod_rows,
    weights,
    n_heads,
    bias,
    key_ok,
    to_windows,
    from_windows,
    return_keys,
    key_win,
    value_win,
    score_scale,
):
    (
        stream,
        normed_a,
        query_win,
        unused_key,
        unused_value,
        key_local,
        value_local,
        att_out,
        proj_out,
        mid_stream,
        normed_m,
        up_value,
        active,
        down_out,
    ) = saved
    qkv_w, proj_w, up_w, down_w = weights
    n_clips = stream.shape[0]
    width_d = stream.shape[-1]
    grad_down_v = (row_of(mod_rows, 5) * grad_out).astype(jnp.bfloat16)
    gate_m_grad = clip_sum(grad_out * down_out)
    down_grad = outer_dot(active, grad_down_v)
    grad_act = back_dot(grad_down_v, down_w)
    unused_gelu, gelu_pull = jax.vjp(gelu_tanh, up_value)
    grad_up_v = gelu_pull(grad_act)[0].astype(jnp.bfloat16)
    up_grad = outer_dot(normed_m, grad_up_v)
    grad_normed = back_dot(grad_up_v, up_w)
    unused_norm, norm_pull = jax.vjp(modulate, mid_stream, row_of(mod_rows, 3), row_of(mod_rows, 4))
    grad_mid, shift_m_grad, scale_m_grad = norm_pull(grad_normed)
    grad_mid = grad_mid + grad_out
    grad_proj_v = (row_of(mod_rows, 2) * grad_mid).astype(jnp.bfloat16)
    gate_a_grad = clip_sum(grad_mid * proj_out)
    proj_grad = outer_dot(att_out, grad_proj_v)
    grad_att = back_dot(grad_proj_v, proj_w).astype(jnp.bfloat16)
    grad_att_win = split_heads(to_windows(grad_att), n_heads)
    soft_probs = soft_scores(query_win, key_win, bias, key_ok, score_scale)
    grad_probs = jnp.einsum(
        "nqhd,nkhd->nhqk", grad_att_win, value_win, preferred_element_type=jnp.float32
    )
    row_delta = jnp.sum(soft_probs * grad_probs, axis=-1, keepdims=True)
    grad_scores = (soft_probs * (grad_probs - row_delta)).astype(jnp.bfloat16)
    grad_bias = jnp.sum(grad_scores.astype(jnp.float32), axis=0)
    grad_query = (
        jnp.einsum("nhqk,nkhd->nqhd", grad_scores, key_win, preferred_element_type=jnp.float32)
        * score_scale
    )
    grad_key = (
        jnp.einsum("nhqk,nqhd->nkhd", grad_scores, query_win, preferred_element_type=jnp.float32)
        * score_scale
    )
    grad_value = jnp.einsum(
        "nhqk,nqhd->nkhd",
        soft_probs.astype(jnp.bfloat16),
        grad_att_win,
        preferred_element_type=jnp.float32,
    )
    n_win = grad_query.shape[0]
    grad_query = from_windows(grad_query.reshape(n_win, grad_query.shape[1], width_d), stream.shape)
    grad_key_full, grad_value_full = return_keys(
        grad_key.reshape(n_win, grad_key.shape[1], width_d),
        grad_value.reshape(n_win, grad_value.shape[1], width_d),
    )
    grad_qkv_v = jnp.concatenate([grad_query, grad_key_full, grad_value_full], axis=-1).astype(
        jnp.bfloat16
    )
    qkv_grad = outer_dot(normed_a, grad_qkv_v)
    grad_normed = back_dot(grad_qkv_v, qkv_w)
    unused_norm, norm_pull = jax.vjp(modulate, stream, row_of(mod_rows, 0), row_of(mod_rows, 1))
    grad_stream, shift_a_grad, scale_a_grad = norm_pull(grad_normed)
    grad_stream = grad_stream + grad_mid
    mod_grad = jnp.stack(
        [
            shift_a_grad.reshape(n_clips, width_d),
            scale_a_grad.reshape(n_clips, width_d),
            gate_a_grad,
            shift_m_grad.reshape(n_clips, width_d),
            scale_m_grad.reshape(n_clips, width_d),
            gate_m_grad,
        ],
        axis=1,
    )
    return (grad_stream, mod_grad, (qkv_grad, proj_grad, up_grad, down_grad), grad_bias)


def on_device_general(
    frames_in, size_group, modulation, w_qkv, w_proj, w_up, w_down, table_sp, table_st, cotangent
):
    n_clips, local_frames, n_rows, n_cols, width_d = frames_in.shape
    n_heads = table_sp.shape[0]
    score_scale = (width_d // n_heads) ** (-0.5)
    first_frame = lax.axis_index("frame") * local_frames
    local_shape = (n_clips, local_frames, n_rows, n_cols, width_d)
    whole_shape = (n_clips, FRAMES, n_rows, n_cols, width_d)
    gathered = (
        lax.all_gather(w_qkv, "clip", axis=0, tiled=True),
        lax.all_gather(w_proj, "clip", axis=0, tiled=True),
        lax.all_gather(w_up, "clip", axis=0, tiled=True),
        lax.all_gather(w_down, "clip", axis=0, tiled=True),
    )
    column_ids = jnp.arange(n_cols, dtype=jnp.int32)
    column_limit = n_cols - 3 * (2 - size_group)
    wide_ok = column_ids[None, :] < column_limit[:, None]
    local_ok = jnp.broadcast_to(wide_ok[:, None, None, :], (n_clips, local_frames, n_rows, n_cols))
    spatial_ok = spatial_windows(local_ok[..., None])[..., 0]
    frame_ok = jnp.arange(FRAMES, dtype=jnp.int32) < FILLED
    cube_grid = wide_ok[:, None, None, :] & frame_ok[None, :, None, None]
    cube_grid = jnp.broadcast_to(cube_grid, (n_clips, FRAMES, n_rows, n_cols))
    cube_ok = cube_windows(cube_grid[..., None])[..., 0]
    span_sp = 2 * SWIN - 1

    def build_spatial(table):
        return expand_bias(table.reshape(n_heads, span_sp, span_sp), SWIN)

    def build_cube(table):
        return cube_bias(table, first_frame, local_frames)

    bias_sp, pull_sp = jax.vjp(build_spatial, table_sp)
    bias_st, pull_st = jax.vjp(build_cube, table_st)

    def spatial_keys(key_local, value_local):
        return (spatial_windows(key_local), spatial_windows(value_local))

    def cube_keys(key_local, value_local):
        key_all, value_all = (
            lax.all_gather(key_local, "frame", axis=1, tiled=True),
            lax.all_gather(value_local, "frame", axis=1, tiled=True),
        )
        return (cube_windows(key_all), cube_windows(value_all))

    def spatial_return(grad_key, grad_value):
        return (spatial_unwindow(grad_key, local_shape), spatial_unwindow(grad_value, local_shape))

    def cube_return(grad_key, grad_value):
        key_whole = cube_unwindow(grad_key, whole_shape)
        value_whole = cube_unwindow(grad_value, whole_shape)
        return (
            lax.psum_scatter(
                key_whole.astype(jnp.bfloat16), "frame", scatter_dimension=1, tiled=True
            ).astype(jnp.float32),
            lax.psum_scatter(
                value_whole.astype(jnp.bfloat16), "frame", scatter_dimension=1, tiled=True
            ).astype(jnp.float32),
        )

    weights_sp = (gathered[0][:, 0], gathered[1][:, 0], gathered[2][:, 0], gathered[3][:, 0])
    weights_st = (gathered[0][:, 1], gathered[1][:, 1], gathered[2][:, 1], gathered[3][:, 1])
    stream_mid, saved_sp = general_forward(
        frames_in.astype(jnp.float32),
        modulation[:, 0:6],
        weights_sp,
        n_heads,
        bias_sp,
        spatial_ok,
        spatial_windows,
        spatial_unwindow,
        spatial_keys,
        score_scale,
    )
    stream_end, saved_st = general_forward(
        stream_mid,
        modulation[:, 6:12],
        weights_st,
        n_heads,
        bias_st,
        cube_ok,
        cube_windows,
        cube_unwindow,
        cube_keys,
        score_scale,
    )
    mixed = stream_end.astype(jnp.bfloat16)
    again = (
        lax.all_gather(w_qkv, "clip", axis=0, tiled=True),
        lax.all_gather(w_proj, "clip", axis=0, tiled=True),
        lax.all_gather(w_up, "clip", axis=0, tiled=True),
        lax.all_gather(w_down, "clip", axis=0, tiled=True),
    )
    back_sp = (again[0][:, 0], again[1][:, 0], again[2][:, 0], again[3][:, 0])
    back_st = (again[0][:, 1], again[1][:, 1], again[2][:, 1], again[3][:, 1])
    key_again, value_again = (
        lax.all_gather(saved_st[5], "frame", axis=1, tiled=True),
        lax.all_gather(saved_st[6], "frame", axis=1, tiled=True),
    )
    key_win_st = split_heads(cube_windows(key_again), n_heads)
    value_win_st = split_heads(cube_windows(value_again), n_heads)
    grad_stream, mod_grad_st, grads_st, bias_grad_st = general_backward(
        cotangent.astype(jnp.float32),
        saved_st,
        modulation[:, 6:12],
        back_st,
        n_heads,
        bias_st,
        cube_ok,
        cube_windows,
        cube_unwindow,
        cube_return,
        key_win_st,
        value_win_st,
        score_scale,
    )
    grad_stream, mod_grad_sp, grads_sp, bias_grad_sp = general_backward(
        grad_stream,
        saved_sp,
        modulation[:, 0:6],
        back_sp,
        n_heads,
        bias_sp,
        spatial_ok,
        spatial_windows,
        spatial_unwindow,
        spatial_return,
        saved_sp[3],
        saved_sp[4],
        score_scale,
    )
    table_sp_grad = pull_sp(bias_grad_sp)[0]
    table_st_grad = pull_st(bias_grad_st)[0]
    full_qkv = jnp.stack([grads_sp[0], grads_st[0]], axis=1)
    full_proj = jnp.stack([grads_sp[1], grads_st[1]], axis=1)
    full_up = jnp.stack([grads_sp[2], grads_st[2]], axis=1)
    full_down = jnp.stack([grads_sp[3], grads_st[3]], axis=1)
    shares = (
        lax.psum_scatter(
            full_qkv.astype(jnp.bfloat16), "clip", scatter_dimension=0, tiled=True
        ).astype(jnp.float32),
        lax.psum_scatter(
            full_proj.astype(jnp.bfloat16), "clip", scatter_dimension=0, tiled=True
        ).astype(jnp.float32),
        lax.psum_scatter(
            full_up.astype(jnp.bfloat16), "clip", scatter_dimension=0, tiled=True
        ).astype(jnp.float32),
        lax.psum_scatter(
            full_down.astype(jnp.bfloat16), "clip", scatter_dimension=0, tiled=True
        ).astype(jnp.float32),
    )
    mod_grad = jnp.concatenate([mod_grad_sp, mod_grad_st], axis=1)
    summed = (
        lax.psum(shares[0].astype(jnp.bfloat16), "frame").astype(jnp.float32),
        lax.psum(shares[1].astype(jnp.bfloat16), "frame").astype(jnp.float32),
        lax.psum(shares[2].astype(jnp.bfloat16), "frame").astype(jnp.float32),
        lax.psum(shares[3].astype(jnp.bfloat16), "frame").astype(jnp.float32),
        lax.psum(mod_grad.astype(jnp.bfloat16), "frame").astype(jnp.float32),
        lax.psum(table_sp_grad.astype(jnp.bfloat16), "frame").astype(jnp.float32),
        lax.psum(table_st_grad.astype(jnp.bfloat16), "frame").astype(jnp.float32),
    )
    tables = (
        lax.psum(summed[5].astype(jnp.bfloat16), "clip").astype(jnp.float32),
        lax.psum(summed[6].astype(jnp.bfloat16), "clip").astype(jnp.float32),
    )
    return (
        mixed,
        grad_stream.astype(jnp.bfloat16),
        summed[4],
        summed[0],
        summed[1],
        summed[2],
        summed[3],
        tables[0],
        tables[1],
    )


def solution(mesh):
    placed = (
        P("clip", "frame", None, None, None),
        P("clip"),
        P("clip", None, None),
        P("clip", None, None),
        P("clip", None, None),
        P("clip", None, None),
        P("clip", None, None),
        P(),
        P(),
        P("clip", "frame", None, None, None),
    )
    whole_windows = mesh.shape["frame"] == 2 and mesh.shape["clip"] == 16
    return jax.shard_map(
        on_device if whole_windows else on_device_general,
        mesh=mesh,
        in_specs=placed,
        out_specs=(
            P("clip", "frame", None, None, None),
            P("clip", "frame", None, None, None),
            P("clip", None, None),
            P("clip", None, None),
            P("clip", None, None),
            P("clip", None, None),
            P("clip", None, None),
            P(),
            P(),
        ),
        check_vma=False,
    )
```
